128 devices in a mesh: tm: 32 (over x, z, y_hi), ffn: 4 (over y_lo, core).
Axes of the slice: x: 4, y: 4 (y_hi: 2, y_lo: 2; y = y_hi * 2 + y_lo), z: 4, core: 2. Of those that a mesh axis runs over, the one named last changes fastest.
Arguments:
- frames: bfloat16 [65536, 512], P('tm'), may hold values from -60 to 60
- upstream: bfloat16 [65536, 512], P('tm'), may hold values from -6 to 6
- recording: int32 [65536], replicated, may hold values from 0 to 7, never falling along the last dimension, each value on 1 to 16384 neighbouring positions
- first_gain: float32 [512], replicated, may hold values from 0.1 to 1.9
- query_weight: bfloat16 [512, 512], P(None, 'ffn'), may hold values from -0.5 to 0.5
- key_weight: bfloat16 [512, 512], P(None, 'ffn'), may hold values from -0.5 to 0.5
- value_weight: bfloat16 [512, 512], P(None, 'ffn'), may hold values from -0.25 to 0.25
- out_weight: bfloat16 [512, 512], P('ffn'), may hold values from -0.25 to 0.25
- second_gain: float32 [512], replicated, may hold values from 0.1 to 1.9
- inner_weight: bfloat16 [512, 2048], P(None, 'ffn'), may hold values from -0.25 to 0.25
- outer_weight: bfloat16 [2048, 512], P('ffn'), may hold values from -0.125 to 0.125
Outputs:
- grad_frames: float32 [65536, 512], P(('tm', 'ffn'))
- grad_query_weight: float32 [512, 512], P(None, 'ffn')
- grad_key_weight: float32 [512, 512], P(None, 'ffn')
- grad_value_weight: float32 [512, 512], P(None, 'ffn')
- grad_out_weight: float32 [512, 512], P('ffn')
- grad_inner_weight: float32 [512, 2048], P(None, 'ffn')
- grad_outer_weight: float32 [2048, 512], P('ffn')
The draws below stay inside these ranges and needn't reach their ends.
Inputs may be any that keep to these rules, and one draw needn't show every extreme that they name: Ids never fall along time; each recording spans 1 to 16384 frames and one spans exactly that many.
All inputs are finite; a program needn't handle non-finite values.
Results may differ from the reference program's by a relative error of at most 0.025.
Values may be sent and summed in bfloat16 or wider, within the bound.
No kernel may reach another device: no remote copies, remote signals or barrier semaphores. Data moves between devices by JAX's collectives and lax.ppermute only.
A program may use at most 128 MiB of HBM per device.

```python
import math
import jax
import jax.numpy as jnp
import numpy as np
from jax import lax

D = 512
HEADS = 8
FF = 2048
HEAD_DIM = 64
HALF = 256
FRAMES_DEV = 2048
TOKENS = 65536
RECORDINGS = 8
HEAD_GROUPS = 4


def projection_draw(key, salt):
    base = jax.random.truncated_normal(jax.random.fold_in(key, salt), -6.0, 6.0, (D, D), jnp.float32) / math.sqrt(D)
    return jnp.clip(base, -0.5, 0.5).astype(jnp.bfloat16)


def draw_query_weight(key, part):
    return projection_draw(key, 11)


def draw_key_weight(key, part):
    return projection_draw(key, 12)


def draw_frames(key, part):
    drawn = jax.random.truncated_normal(jax.random.fold_in(key, 13), -6.0, 6.0, (TOKENS, D), jnp.float32)
    return drawn.astype(jnp.bfloat16)


def shard_levels(key, shape, shards, low, largest):
    loudness, own = 1.0, jax.random.fold_in(key, 6)
    for dim, shards_of in shards:
        draws = jnp.exp(jax.random.uniform(jax.random.fold_in(own, dim), (shards_of,), jnp.float32, low / len(shards), largest / len(shards)))
        loudness = loudness * jnp.repeat(draws, shape[dim] // shards_of).reshape([-1 if axis == dim else 1 for axis in range(len(shape))])
    return loudness


def profile(count, total, reach, slope):
    portions = [(1 << 20) // math.isqrt(standing ** slope) + 1 for standing in range(2, count + 1)]
    spare, holding = total - reach - (count - 1), [1] * (count - 1)
    while spare > 0:
        candidates = [i for i in range(count - 1) if holding[i] < reach]
        mass, remaining = sum([portions[i] for i in candidates]), spare
        for i in candidates:
            more = min(reach - holding[i], max(1, remaining * portions[i] // mass), spare)
            holding[i] = holding[i] + more
            spare = spare - more
    return np.array([reach] + holding)


def ragged(key, amount, total, reach, skew):
    if amount == 2:
        one = jax.random.randint(key, (), max(1, total - reach), min(reach, total - 1) + 1)
        return jnp.stack([one, total - one])
    lengths = jnp.asarray(profile(amount, total, reach, skew), jnp.int32)
    couples = (amount - 1) // 2
    source_of, taker = lengths[1:1 + 2 * couples:2], lengths[2:2 + 2 * couples:2]
    margin = jnp.minimum(source_of - 1, reach - taker)
    passed = jax.random.randint(jax.random.fold_in(key, 1), (couples,), 0, 1 << 20) % (margin + 1)
    lengths = lengths.at[1:1 + 2 * couples:2].set(source_of - passed).at[2:2 + 2 * couples:2].set(taker + passed)
    return lengths[jax.random.permutation(jax.random.fold_in(key, 2), amount)]


def gaussian(own_key, shape, deviation, most, cuts=(), held_as=jnp.bfloat16):
    factor_of = shard_levels(own_key, shape, cuts, -0.22, 0.18) if cuts else 1.0
    entries = jax.random.normal(own_key, shape, jnp.float32) * deviation * factor_of
    return jnp.minimum(jnp.maximum(entries, -most), most).astype(held_as)


def setup_inputs(seed: int = 0) -> dict:
    keys = jax.random.split(jax.random.key(seed), 12)
    return {
        "frames": draw_frames(jax.random.fold_in(keys[11], 71), 0),
        "upstream": gaussian(keys[1], (TOKENS, D), 1.0, 6.0, ((0, 32),)),
        "recording": jnp.searchsorted(jnp.cumsum(ragged(keys[2], RECORDINGS, TOKENS, 8 * FRAMES_DEV, 0)), jnp.arange(TOKENS), side="right").astype(jnp.int32),
        "first_gain": jnp.clip(1.0 + 0.18 * jax.random.normal(keys[3], (D,), jnp.float32), 0.1, 1.9),
        "query_weight": draw_query_weight(jax.random.fold_in(keys[11], 71), 0),
        "key_weight": draw_key_weight(jax.random.fold_in(keys[11], 71), 0),
        "value_weight": gaussian(keys[6], (D, D), D ** -0.5, 0.25, ((1, 4),)),
        "out_weight": gaussian(keys[7], (D, D), D ** -0.5, 0.25, ((0, 4),)),
        "second_gain": jnp.clip(1.0 + 0.18 * jax.random.normal(keys[8], (D,), jnp.float32), 0.1, 1.9),
        "inner_weight": gaussian(keys[9], (D, FF), D ** -0.5, 0.25, ((1, 4),)),
        "outer_weight": gaussian(keys[10], (FF, D), FF ** -0.5, 0.125, ((0, 4),)),
    }


epsilon = 1e-05
masked_score = -1e+30

def layer_norm(inputs):
    center = lax.optimization_barrier(jnp.mean(inputs, axis=-1, keepdims=True))
    shifted = inputs - center
    inverse = lax.rsqrt(lax.optimization_barrier(jnp.mean(shifted * shifted, axis=-1, keepdims=True)) + epsilon)
    return (shifted * inverse, inverse)

def norm_back(grad_normed, scaled, inverse, gain):
    weighted = grad_normed * gain
    first_mean = lax.optimization_barrier(jnp.mean(weighted, axis=-1, keepdims=True))
    second_mean = lax.optimization_barrier(jnp.mean(weighted * scaled, axis=-1, keepdims=True))
    return inverse * (weighted - first_mean - scaled * second_mean)

def round_trip(array):
    return lax.optimization_barrier(array.astype(jnp.bfloat16)).astype(jnp.float32)

def grouped_sum(pairs):
    total = None
    for left, right in pairs:
        left_groups = left.astype(jnp.float32).reshape(left.shape[0], HEAD_GROUPS, left.shape[1] // HEAD_GROUPS)
        right_groups = right.astype(jnp.float32).reshape(HEAD_GROUPS, right.shape[0] // HEAD_GROUPS, right.shape[1])
        term = jnp.einsum('rgc,gco->gro', left_groups, right_groups)
        total = term if total is None else total + term
    rounded = round_trip(total)
    return lax.optimization_barrier(jnp.sum(rounded, axis=0))

def split_heads(block):
    return block.astype(jnp.float32).reshape(block.shape[0], HEADS, HEAD_DIM)

def block_allowed(record_query, record_key):
    block_rows = record_query.shape[0]
    offsets = lax.broadcasted_iota(jnp.int32, (block_rows, 2 * block_rows), 1) - lax.broadcasted_iota(jnp.int32, (block_rows, 2 * block_rows), 0)
    band = (offsets >= 0) & (offsets < block_rows)
    return band & (record_query[:, None] == record_key[None, :])

def softmax_block(query_block, key_block, allowed):
    scores = jnp.einsum('qhd,khd->hqk', query_block, key_block) * HEAD_DIM ** (-0.5)
    scores = jnp.where(allowed[None], scores, masked_score)
    peak = lax.optimization_barrier(jnp.max(scores, axis=-1, keepdims=True))
    weights = jnp.exp(scores - peak)
    return weights / lax.optimization_barrier(jnp.sum(weights, axis=-1, keepdims=True))

def block_pieces(block_index, queries, key_pad, value_pad, recording, record_pad):
    block_rows = 2 * HALF
    start = (block_index * block_rows).astype(jnp.int32)
    query_block = split_heads(lax.dynamic_slice_in_dim(queries, start, block_rows, 0))
    key_block = split_heads(lax.dynamic_slice_in_dim(key_pad, start, 2 * block_rows, 0))
    value_block = split_heads(lax.dynamic_slice_in_dim(value_pad, start, 2 * block_rows, 0))
    record_query = lax.dynamic_slice_in_dim(recording, start, block_rows, 0)
    record_key = lax.dynamic_slice_in_dim(record_pad, start, 2 * block_rows, 0)
    return (start, query_block, key_block, value_block, block_allowed(record_query, record_key))

def padded_inputs(key_rows, value_rows, recording):
    key_pad = jnp.pad(key_rows, ((HALF, HALF), (0, 0)))
    value_pad = jnp.pad(value_rows, ((HALF, HALF), (0, 0)))
    record_pad = jnp.pad(recording, (HALF, HALF), constant_values=-1)
    return (key_pad, value_pad, record_pad)

def attention_context(queries, key_rows, value_rows, recording):
    key_pad, value_pad, record_pad = padded_inputs(key_rows, value_rows, recording)
    block_rows = 2 * HALF

    def one_block(block_index):
        start, query_block, key_block, value_block, allowed = block_pieces(block_index, queries, key_pad, value_pad, recording, record_pad)
        probability_low = round_trip(softmax_block(query_block, key_block, allowed))
        context = jnp.einsum('hqk,khd->qhd', probability_low, value_block)
        return context.reshape(block_rows, D).astype(jnp.bfloat16)
    blocks = TOKENS // block_rows
    return lax.map(one_block, jnp.arange(blocks, dtype=jnp.int32)).reshape(TOKENS, D)

def intersection_add(pieces):
    block_rows = 2 * HALF
    lower = pieces[:, :block_rows]
    upper = pieces[:, block_rows:]
    padded = jnp.pad(lower, ((0, 1), (0, 0), (0, 0))) + jnp.pad(upper, ((1, 0), (0, 0), (0, 0)))
    return padded.reshape(-1, D)[HALF:HALF + TOKENS]

def attention_grads(queries, key_rows, value_rows, recording, grad_context):
    key_pad, value_pad, record_pad = padded_inputs(key_rows, value_rows, recording)
    block_rows = 2 * HALF

    def one_block(block_index):
        start, query_block, key_block, value_block, allowed = block_pieces(block_index, queries, key_pad, value_pad, recording, record_pad)
        grad_block = split_heads(lax.dynamic_slice_in_dim(grad_context, start, block_rows, 0))
        probability = softmax_block(query_block, key_block, allowed)
        probability_low = round_trip(probability)
        grad_prob = jnp.einsum('qhd,khd->hqk', grad_block, value_block)
        inner_sum = lax.optimization_barrier(jnp.sum(grad_prob * probability, axis=-1, keepdims=True))
        grad_scores = round_trip(probability * (grad_prob - inner_sum) * HEAD_DIM ** (-0.5))
        grad_query = jnp.einsum('hqk,khd->qhd', grad_scores, key_block).reshape(block_rows, D)
        grad_key = jnp.einsum('hqk,qhd->khd', grad_scores, query_block).reshape(2 * block_rows, D)
        grad_value = jnp.einsum('hqk,qhd->khd', probability_low, grad_block).reshape(2 * block_rows, D)
        return (grad_query, grad_key, grad_value)
    blocks = TOKENS // block_rows
    query_parts, key_parts, value_parts = lax.map(one_block, jnp.arange(blocks, dtype=jnp.int32))
    return (query_parts.reshape(TOKENS, D), intersection_add(key_parts), intersection_add(value_parts))

def reference(frames, upstream, recording, first_gain, query_weight, key_weight, value_weight, out_weight, second_gain, inner_weight, outer_weight):
    frames_wide = frames.astype(jnp.float32)
    upstream_wide = upstream.astype(jnp.float32)
    scaled_first, inverse_first = layer_norm(frames_wide)
    normed_first = (scaled_first * first_gain).astype(jnp.bfloat16)
    queries = jnp.dot(normed_first, query_weight, preferred_element_type=jnp.float32).astype(jnp.bfloat16)
    key_rows = jnp.dot(normed_first, key_weight, preferred_element_type=jnp.float32).astype(jnp.bfloat16)
    value_rows = jnp.dot(normed_first, value_weight, preferred_element_type=jnp.float32).astype(jnp.bfloat16)
    context = attention_context(queries, key_rows, value_rows, recording)
    middle = frames_wide + grouped_sum([(context, out_weight)])
    scaled_second, inverse_second = layer_norm(middle)
    normed_second = (scaled_second * second_gain).astype(jnp.bfloat16)
    inner_pre = jnp.dot(normed_second, inner_weight, preferred_element_type=jnp.float32)
    activation = jax.nn.silu(inner_pre).astype(jnp.bfloat16)
    sigmoid_inner = jax.nn.sigmoid(inner_pre)
    grad_act = jnp.dot(upstream, outer_weight.T, preferred_element_type=jnp.float32) * 0.5
    grad_inner = (grad_act * sigmoid_inner * (1.0 + inner_pre * (1.0 - sigmoid_inner))).astype(jnp.bfloat16)
    grad_second = grouped_sum([(grad_inner, inner_weight.T)])
    grad_middle = upstream_wide + norm_back(grad_second, scaled_second, inverse_second, second_gain)
    grad_middle_low = grad_middle.astype(jnp.bfloat16)
    grad_context = jnp.dot(grad_middle_low, out_weight.T, preferred_element_type=jnp.float32).astype(jnp.bfloat16)
    grad_query, grad_key, grad_value = attention_grads(queries, key_rows, value_rows, recording, grad_context)
    grad_query = grad_query.astype(jnp.bfloat16)
    grad_key = grad_key.astype(jnp.bfloat16)
    grad_value = grad_value.astype(jnp.bfloat16)
    grad_first = grouped_sum([(grad_query, query_weight.T), (grad_key, key_weight.T), (grad_value, value_weight.T)])
    grad_frames = grad_middle + norm_back(grad_first, scaled_first, inverse_first, first_gain)
    weight_scale = 1.0 / math.sqrt(TOKENS)
    grad_query_weight = jnp.dot(normed_first.T, grad_query, preferred_element_type=jnp.float32) * weight_scale
    grad_key_weight = jnp.dot(normed_first.T, grad_key, preferred_element_type=jnp.float32) * weight_scale
    grad_value_weight = jnp.dot(normed_first.T, grad_value, preferred_element_type=jnp.float32) * weight_scale
    grad_out_weight = jnp.dot(context.T, grad_middle_low, preferred_element_type=jnp.float32) * weight_scale
    grad_inner_weight = jnp.dot(normed_second.T, grad_inner, preferred_element_type=jnp.float32) * weight_scale
    grad_outer_weight = jnp.dot(activation.T, upstream, preferred_element_type=jnp.float32) * 0.5 * weight_scale
    return (grad_frames, grad_query_weight, grad_key_weight, grad_value_weight, grad_out_weight, grad_inner_weight, grad_outer_weight)
```

```python
import math

import jax
import jax.numpy as jnp
from jax import lax
from jax.experimental import pallas as pl
from jax.experimental.pallas import tpu as pltpu
from jax.sharding import PartitionSpec as P

HEAD_DIM = 64
HALF = 256
ROWS = 512
EXT = ROWS + 2 * HALF
QB = 128
WIN = QB + 2 * HALF
BLOCKS = ROWS // QB
GC = 128
D = 512
epsilon = 1e-05
masked_score = -1e30
BF = jnp.bfloat16
F32 = jnp.float32
AXES = ("tm", "ffn")
VMEM = pltpu.VMEM
WHOLE = pl.BlockSpec(memory_space=pltpu.VMEM)


def dot(a, b):
    return jnp.dot(a, b, preferred_element_type=F32)


def dot_nt(a, b):
    return lax.dot_general(a, b, (((1,), (1,)), ((), ())), preferred_element_type=F32)


def params():
    return pltpu.CompilerParams(vmem_limit_bytes=40 * 1024 * 1024)


def cost(flops, nbytes, trans=0):
    return pl.CostEstimate(flops=int(flops), bytes_accessed=int(nbytes), transcendentals=int(trans))


def norm_rows(x):
    center = jnp.mean(x, axis=-1, keepdims=True)
    shifted = x - center
    inverse = lax.rsqrt(jnp.mean(shifted * shifted, axis=-1, keepdims=True) + epsilon)
    return shifted * inverse, inverse


def norm_back(grad_normed, scaled, inverse, gain):
    weighted = grad_normed * gain
    first = jnp.mean(weighted, axis=-1, keepdims=True)
    second = jnp.mean(weighted * scaled, axis=-1, keepdims=True)
    return inverse * (weighted - first - scaled * second)


def norm_kernel(i_ref, frames_ref, halo_ref, gain_ref, col_ref, row_ref, n_ref, nt_ref, bias_ref):
    step = pl.program_id(0)
    at = 2 * i_ref[0] - 1 + step
    outside = (at < 0) | (at > 7)
    x = jnp.where(outside, halo_ref[...].astype(F32), frames_ref[...].astype(F32))
    scaled, _ = norm_rows(x)
    normed = scaled * gain_ref[...]
    n_ref[...] = normed.astype(BF)
    nt_ref[...] = normed.T.astype(BF)
    keys = col_ref[pl.ds(pl.multiple_of(step * QB, QB), WIN), :]
    offset = lax.broadcasted_iota(jnp.int32, (WIN, QB), 0) - lax.broadcasted_iota(
        jnp.int32, (WIN, QB), 1
    )
    band = (offset >= 0) & (offset < 2 * HALF)
    bias_ref[0] = jnp.where(band & (keys == row_ref[0]), 0.0, masked_score)


def run_norm(frames, halo, gain, rec_ext, index):
    rec_col = rec_ext.reshape(EXT, 1)
    rec_row = rec_ext[HALF : HALF + ROWS].reshape(BLOCKS, 1, QB)
    spec = pltpu.PrefetchScalarGridSpec(
        num_scalar_prefetch=1,
        grid=(4,),
        in_specs=[
            pl.BlockSpec((HALF, D), lambda j, i: (jnp.clip(2 * i[0] - 1 + j, 0, 7), 0)),
            pl.BlockSpec((HALF, D), lambda j, i: (0, 0)),
            pl.BlockSpec((1, D), lambda j, i: (0, 0)),
            pl.BlockSpec((EXT, 1), lambda j, i: (0, 0)),
            pl.BlockSpec((1, 1, QB), lambda j, i: (j, 0, 0)),
        ],
        out_specs=[
            pl.BlockSpec((HALF, D), lambda j, i: (j, 0)),
            pl.BlockSpec((D, HALF), lambda j, i: (0, j)),
            pl.BlockSpec((1, WIN, QB), lambda j, i: (j, 0, 0)),
        ],
    )
    return pl.pallas_call(
        norm_kernel,
        grid_spec=spec,
        out_shape=[
            jax.ShapeDtypeStruct((EXT, D), BF),
            jax.ShapeDtypeStruct((D, EXT), BF),
            jax.ShapeDtypeStruct((BLOCKS, WIN, QB), F32),
        ],
        compiler_params=params(),
        cost_estimate=cost(EXT * D * 12, 5e6),
        name="norm_first",
    )(index.reshape(1), frames, halo, gain.reshape(1, D), rec_col, rec_row)


def stack_heads(block):
    lane = lax.broadcasted_iota(jnp.int32, block.shape, 1)
    zero = jnp.zeros_like(block)
    low = jnp.where(lane < HEAD_DIM, block, zero)
    high = jnp.where(lane < HEAD_DIM, zero, block)
    return jnp.concatenate([low, high], axis=0)


def pick_heads(both):
    return jnp.concatenate([both[:HEAD_DIM, :QB], both[HEAD_DIM:, QB:]], axis=0).T


def context_kernel(n_ref, wq_ref, wk_ref, wv_ref, bias_ref, q_ref, k_ref, v_ref, ctx_ref, lse_ref, vt_ref):
    n = n_ref[...]
    q_ref[...] = dot(n_ref[HALF : HALF + ROWS], wq_ref[...]).astype(BF) * 0.125
    k_ref[...] = dot(n, wk_ref[...]).astype(BF)
    v = dot(n, wv_ref[...])
    v_ref[...] = v.astype(BF)
    vt_ref[...] = v.T.astype(BF)
    for b in range(BLOCKS):
        win = slice(b * QB, b * QB + WIN)
        rows = slice(b * QB, b * QB + QB)
        queries = stack_heads(q_ref[rows])
        bias = bias_ref[b]
        scores = dot_nt(k_ref[win], queries) + jnp.concatenate([bias, bias], axis=1)
        peak = jnp.max(scores, axis=0, keepdims=True)
        weights = jnp.exp(scores - peak)
        total = jnp.sum(weights, axis=0, keepdims=True)
        both = dot(vt_ref[:, win], weights.astype(BF)) / total
        ctx_ref[rows] = pick_heads(both).astype(BF)
        lse_ref[b] = peak + jnp.log(total)


def run_context(normed, wq, wk, wv, bias):
    return pl.pallas_call(
        context_kernel,
        in_specs=[WHOLE] * 5,
        out_specs=[WHOLE] * 5,
        out_shape=[
            jax.ShapeDtypeStruct((ROWS, GC), BF),
            jax.ShapeDtypeStruct((EXT, GC), BF),
            jax.ShapeDtypeStruct((EXT, GC), BF),
            jax.ShapeDtypeStruct((ROWS, GC), BF),
            jax.ShapeDtypeStruct((BLOCKS, 1, 2 * QB), F32),
        ],
        scratch_shapes=[VMEM((GC, EXT), BF)],
        compiler_params=params(),
        cost_estimate=cost(2e9, 4e6, BLOCKS * WIN * 2 * QB),
        name="context",
    )(normed, wq, wk, wv, bias)


def attention_back_kernel(
    gml_ref, wo_ref, q_ref, k_ref, v_ref, lse_ref, bias_ref, nt_ref,
    dq_ref, dk_ref, dv_ref, dw_ref, g_ref, kt_ref, dka_ref, dva_ref,
):
    g_ref[...] = dot_nt(gml_ref[...], wo_ref[...]).astype(BF)
    kt_ref[...] = k_ref[...].T
    dka_ref[...] = jnp.zeros_like(dka_ref)
    dva_ref[...] = jnp.zeros_like(dva_ref)
    for b in range(BLOCKS):
        win = slice(b * QB, b * QB + WIN)
        rows = slice(b * QB, b * QB + QB)
        queries = stack_heads(q_ref[rows])
        grads = stack_heads(g_ref[rows])
        bias = bias_ref[b]
        scores = dot_nt(k_ref[win], queries) + jnp.concatenate([bias, bias], axis=1)
        prob = jnp.exp(scores - lse_ref[b])
        grad_prob = dot_nt(v_ref[win], grads)
        inner = jnp.sum(prob * grad_prob, axis=0, keepdims=True)
        grad_scores = (prob * (grad_prob - inner)).astype(BF)
        dva_ref[win] += dot(prob.astype(BF), grads)
        dka_ref[win] += dot(grad_scores, queries)
        both = dot(kt_ref[:, win], grad_scores)
        dq_ref[rows] = (pick_heads(both) * 0.125).astype(BF)
    dk_ref[...] = dka_ref[...].astype(BF)
    dv_ref[...] = dva_ref[...].astype(BF)
    dw_ref[:D] = dot(nt_ref[:, HALF : HALF + ROWS], dq_ref[...]).astype(BF)
    dw_ref[D : 2 * D] = dot(nt_ref[...], dk_ref[...]).astype(BF)
    dw_ref[2 * D :] = dot(nt_ref[...], dv_ref[...]).astype(BF)


def run_attention_back(gml, wo, q, k, v, lse, bias, nt):
    return pl.pallas_call(
        attention_back_kernel,
        in_specs=[WHOLE] * 8,
        out_specs=[WHOLE] * 4,
        out_shape=[
            jax.ShapeDtypeStruct((ROWS, GC), BF),
            jax.ShapeDtypeStruct((EXT, GC), BF),
            jax.ShapeDtypeStruct((EXT, GC), BF),
            jax.ShapeDtypeStruct((3 * D, GC), BF),
        ],
        scratch_shapes=[
            VMEM((ROWS, GC), BF),
            VMEM((GC, EXT), BF),
            VMEM((EXT, GC), F32),
            VMEM((EXT, GC), F32),
        ],
        compiler_params=params(),
        cost_estimate=cost(4e9, 6e6, BLOCKS * WIN * 2 * QB),
        name="attention_back",
    )(gml, wo, q, k, v, lse, bias, nt)


def feed_kernel(*refs):
    own_ref, up_ref, gain_ref = refs[:3]
    ctx = refs[3:7]
    wo = refs[7:11]
    wi = refs[11:15]
    wu = refs[15:19]
    gm_ref, gml_ref = refs[19:21]
    dwi = refs[21:25]
    dwu = refs[25:29]
    dwo = refs[29:33]
    sc_ref, n2_ref, n2t_ref, upt_ref, gs_ref = refs[33:]
    up = up_ref[...]
    middle = own_ref[...].astype(F32)
    for k in range(4):
        middle = middle + dot(ctx[k][...], wo[k][...])
    scaled, inverse = norm_rows(middle)
    sc_ref[...] = scaled
    normed = scaled * gain_ref[...]
    n2_ref[...] = normed.astype(BF)
    n2t_ref[...] = normed.T.astype(BF)
    upt_ref[...] = up.T
    for k in range(4):
        pre = dot(n2_ref[...], wi[k][...])
        grad_act = dot_nt(up_ref[...], wu[k][...]) * 0.5
        gate = jax.nn.sigmoid(pre)
        act = (pre * gate).astype(BF)
        grad_inner = (grad_act * gate * (1.0 + pre * (1.0 - gate))).astype(BF)
        dwi[k][...] = dot(n2t_ref[...], grad_inner).astype(BF)
        dwu[k][...] = (dot(upt_ref[...], act) * 0.5).astype(BF)
        back = dot_nt(grad_inner, wi[k][...])
        if k == 0:
            gs_ref[...] = back
        else:
            gs_ref[...] += back
    grad_middle = up.astype(F32) + norm_back(gs_ref[...], sc_ref[...], inverse, gain_ref[...])
    gm_ref[...] = grad_middle
    gml_ref[...] = grad_middle.astype(BF)
    for k in range(4):
        dwo[k][...] = dot(ctx[k][...].T, gml_ref[...]).astype(BF)


def run_feed(own, up, gain, ctx, wo, wi, wu):
    sq = jax.ShapeDtypeStruct((D, D), BF)
    return pl.pallas_call(
        feed_kernel,
        in_specs=[WHOLE] * 19,
        out_specs=[WHOLE] * 14,
        out_shape=[jax.ShapeDtypeStruct((ROWS, D), F32), jax.ShapeDtypeStruct((ROWS, D), BF)]
        + [sq] * 8
        + [jax.ShapeDtypeStruct((GC, D), BF)] * 4,
        scratch_shapes=[
            VMEM((ROWS, D), F32),
            VMEM((ROWS, D), BF),
            VMEM((D, ROWS), BF),
            VMEM((D, ROWS), BF),
            VMEM((ROWS, D), F32),
        ],
        compiler_params=params(),
        cost_estimate=cost(7e9, 14e6, ROWS * 2048),
        name="feed",
    )(own, up, gain.reshape(1, D), *ctx, *wo, *wi, *wu)


def first_kernel(*refs):
    dq, dk, dv = refs[0:4], refs[4:8], refs[8:12]
    wq, wk, wv = refs[12:16], refs[16:20], refs[20:24]
    own_ref, before_ref, after_ref = refs[24:]
    acc = None
    for k in range(4):
        term = dot_nt(dk[k][...], wk[k][...]) + dot_nt(dv[k][...], wv[k][...])
        acc = term if acc is None else acc + term
    before_ref[...] = acc[:HALF].astype(BF)
    after_ref[...] = acc[HALF + ROWS :].astype(BF)
    own = acc[HALF : HALF + ROWS]
    for k in range(4):
        own = own + dot_nt(dq[k][...], wq[k][...])
    own_ref[...] = own


def run_first(dq, dk, dv, wq, wk, wv):
    return pl.pallas_call(
        first_kernel,
        in_specs=[WHOLE] * 24,
        out_specs=[WHOLE] * 3,
        out_shape=[
            jax.ShapeDtypeStruct((ROWS, D), F32),
            jax.ShapeDtypeStruct((HALF, D), BF),
            jax.ShapeDtypeStruct((HALF, D), BF),
        ],
        compiler_params=params(),
        cost_estimate=cost(3e9, 6e6),
        name="first_grad",
    )(*dq, *dk, *dv, *wq, *wk, *wv)


def last_kernel(gf_ref, low_ref, high_ref, own_ref, gain_ref, gm_ref, out_ref):
    scaled, inverse = norm_rows(own_ref[...].astype(F32))
    grad = gf_ref[...] + jnp.concatenate(
        [low_ref[...].astype(F32), high_ref[...].astype(F32)], axis=0
    )
    out_ref[...] = gm_ref[...] + norm_back(grad, scaled, inverse, gain_ref[...])


def run_last(gf, low, high, own, gain, gm):
    return pl.pallas_call(
        last_kernel,
        in_specs=[WHOLE] * 6,
        out_specs=WHOLE,
        out_shape=jax.ShapeDtypeStruct((ROWS, D), F32),
        compiler_params=params(),
        cost_estimate=cost(ROWS * D * 20, 5e6),
        name="frames_grad",
    )(gf, low, high, own, gain.reshape(1, D), gm)


def swap(array, bits):
    return lax.ppermute(array, AXES, [(n, n ^ bits) for n in range(128)])


def add_low(*arrays):
    return sum(a.astype(F32) for a in arrays).astype(BF)


def local(
    frames,
    upstream,
    recording,
    first_gain,
    query_weight,
    key_weight,
    value_weight,
    out_weight,
    second_gain,
    inner_weight,
    outer_weight,
):
    t = lax.axis_index("tm")
    i = lax.axis_index("ffn")
    slab = frames.shape[0]
    devices = lax.axis_size("tm") * 4

    edge = jnp.where(i == 3, frames[slab - HALF :], frames[:HALF])
    pairs = [(4 * n + 3, 4 * n + 4) for n in range(31)] + [(4 * n + 4, 4 * n + 3) for n in range(31)]
    halo = lax.ppermute(edge, AXES, pairs)

    own_proj = jnp.concatenate(
        [query_weight, key_weight, value_weight, out_weight.reshape(D, GC)], axis=0
    )
    proj = [own_proj, swap(own_proj, 1), swap(own_proj, 2), swap(own_proj, 7)]
    wq = [w[:D] for w in proj]
    wk = [w[D : 2 * D] for w in proj]
    wv = [w[2 * D : 3 * D] for w in proj]
    wo = [w[3 * D :].reshape(GC, D) for w in proj]

    inner_own, outer_own, _, _ = lax.optimization_barrier(
        (inner_weight, outer_weight, proj[2], proj[3])
    )
    inner_far = swap(inner_own, 2)
    outer_far = swap(outer_own, 6)
    wi = [inner_weight, swap(inner_own, 1), inner_far, swap(inner_far, 1)]
    wu = [outer_weight, swap(outer_own, 1), outer_far, swap(outer_far, 1)]

    record_pad = jnp.pad(recording, (HALF, HALF), constant_values=-1)
    rec_ext = lax.dynamic_slice_in_dim(record_pad, t * slab + i * ROWS, EXT)
    own = lax.dynamic_slice_in_dim(frames, i * ROWS, ROWS, 0)
    up = lax.dynamic_slice_in_dim(upstream, i * ROWS, ROWS, 0)

    normed, normed_t, bias = run_norm(frames, halo, first_gain, rec_ext, i)
    qs, ks, vs, ctx, lse = [], [], [], [], []
    for k in range(4):
        q, key, v, c, s = run_context(normed, wq[k], wk[k], wv[k], bias)
        qs.append(q)
        ks.append(key)
        vs.append(v)
        ctx.append(c)
        lse.append(s)

    outs = run_feed(own, up, second_gain, ctx, wo, wi, wu)
    grad_middle, gml = outs[:2]
    feeds = [
        jnp.concatenate([outs[2 + k], outs[6 + k]], axis=0).reshape(2 * D, D) for k in range(4)
    ]
    douts = [outs[10 + k] for k in range(4)]

    got1, got3 = swap(feeds[1], 1), swap(feeds[3], 1)
    near = add_low(feeds[0], got1)
    far = add_low(feeds[2], got3)
    got = jnp.concatenate([swap(far[:D], 2), swap(far[D:], 6)], axis=0)
    feed_sum = add_low(near, got)

    def total(part):
        parts = lax.all_to_all(part, "tm", 0, 0, tiled=True)
        summed = jnp.sum(parts.astype(F32), axis=0, keepdims=True).astype(BF)
        return lax.all_to_all(jnp.broadcast_to(summed, part.shape), "tm", 0, 0, tiled=True)

    feed_total = total(feed_sum.reshape(32, 32, D)).reshape(2 * D, D)

    dq, dk, dv, dw = [None] * 4, [None] * 4, [None] * 4, [None] * 4
    for k in (3, 2, 1, 0):
        dq[k], dk[k], dv[k], dw[k] = run_attention_back(
            gml, wo[k], qs[k], ks[k], vs[k], lse[k], bias, normed_t
        )
    sends = [
        jnp.concatenate([dw[k], douts[k].reshape(GC, 4, GC).transpose(1, 0, 2).reshape(D, GC)], axis=0)
        for k in range(4)
    ]
    proj_sum = add_low(sends[0], swap(sends[1], 1), swap(sends[2], 2), swap(sends[3], 7))
    proj_total = total(proj_sum.reshape(32, 64, GC)).reshape(4 * D, GC)

    gf, before, after = run_first(dq, dk, dv, wq, wk, wv)
    low = lax.ppermute(after, AXES, [(n, n + 1) for n in range(devices - 1)])
    high = lax.ppermute(before, AXES, [(n + 1, n) for n in range(devices - 1)])
    grad_frames = run_last(gf, low, high, own, first_gain, grad_middle)

    scale = 1.0 / math.sqrt(recording.shape[0])
    feed_total = feed_total.astype(F32) * scale
    proj_total = proj_total.astype(F32) * scale
    grad_out = proj_total[3 * D :].reshape(4, GC, GC).transpose(1, 0, 2).reshape(GC, D)
    return (
        grad_frames,
        proj_total[:D],
        proj_total[D : 2 * D],
        proj_total[2 * D : 3 * D],
        grad_out,
        feed_total[:D],
        feed_total[D:].T,
    )


def solution(mesh):
    in_specs = (
        P("tm", None),
        P("tm", None),
        P(),
        P(),
        P(None, "ffn"),
        P(None, "ffn"),
        P(None, "ffn"),
        P("ffn", None),
        P(),
        P(None, "ffn"),
        P("ffn", None),
    )
    out_specs = (
        P(("tm", "ffn"), None),
        P(None, "ffn"),
        P(None, "ffn"),
        P(None, "ffn"),
        P("ffn", None),
        P(None, "ffn"),
        P("ffn", None),
    )
    return jax.shard_map(local, mesh=mesh, in_specs=in_specs, out_specs=out_specs, check_vma=False)
```

```python
import functools
import math

import jax
import jax.numpy as jnp
from jax import lax
from jax.experimental import pallas as pl
from jax.experimental.pallas import tpu as pltpu
from jax.sharding import PartitionSpec as P

HEAD_DIM = 64
HALF = 256
ROWS = 512
EXT = ROWS + 2 * HALF
QB = 128
WIN = QB + 2 * HALF
BLOCKS = ROWS // QB
GC = 128
D = 512
epsilon = 1e-05
masked_score = -1e30
BF = jnp.bfloat16
F32 = jnp.float32
AXES = ("tm", "ffn")
VMEM = pltpu.VMEM
WHOLE = pl.BlockSpec(memory_space=pltpu.VMEM)


def dot(a, b):
    return jnp.dot(a, b, preferred_element_type=F32)


def dot_nt(a, b):
    return lax.dot_general(a, b, (((1,), (1,)), ((), ())), preferred_element_type=F32)


def params(mib=16):
    return pltpu.CompilerParams(vmem_limit_bytes=mib * 1024 * 1024)


def cost(flops, nbytes, trans=0):
    return pl.CostEstimate(flops=int(flops), bytes_accessed=int(nbytes), transcendentals=int(trans))


def norm_rows(x):
    center = jnp.mean(x, axis=-1, keepdims=True)
    shifted = x - center
    inverse = lax.rsqrt(jnp.mean(shifted * shifted, axis=-1, keepdims=True) + epsilon)
    return shifted * inverse, inverse


def norm_back(grad_normed, scaled, inverse, gain):
    weighted = grad_normed * gain
    first = jnp.mean(weighted, axis=-1, keepdims=True)
    second = jnp.mean(weighted * scaled, axis=-1, keepdims=True)
    return inverse * (weighted - first - scaled * second)


def norm_kernel(i_ref, frames_ref, halo_ref, gain_ref, col_ref, row_ref, n_ref, nt_ref, bias_ref):
    step = pl.program_id(0)
    at = 2 * i_ref[0] - 1 + step
    outside = (at < 0) | (at > 7)
    x = jnp.where(outside, halo_ref[...].astype(F32), frames_ref[...].astype(F32))
    scaled, _ = norm_rows(x)
    normed = scaled * gain_ref[...]
    n_ref[...] = normed.astype(BF)
    nt_ref[...] = normed.T.astype(BF)
    keys = col_ref[pl.ds(pl.multiple_of(step * QB, QB), WIN), :]
    offset = lax.broadcasted_iota(jnp.int32, (WIN, QB), 0) - lax.broadcasted_iota(
        jnp.int32, (WIN, QB), 1
    )
    band = (offset >= 0) & (offset < 2 * HALF)
    bias_ref[0] = jnp.where(band & (keys == row_ref[0]), 0.0, masked_score)


def run_norm(frames, halo, gain, rec_ext, index):
    rec_col = rec_ext.reshape(EXT, 1)
    rec_row = rec_ext[HALF : HALF + ROWS].reshape(BLOCKS, 1, QB)
    spec = pltpu.PrefetchScalarGridSpec(
        num_scalar_prefetch=1,
        grid=(4,),
        in_specs=[
            pl.BlockSpec((HALF, D), lambda j, i: (jnp.clip(2 * i[0] - 1 + j, 0, 7), 0)),
            pl.BlockSpec((HALF, D), lambda j, i: (0, 0)),
            pl.BlockSpec((1, D), lambda j, i: (0, 0)),
            pl.BlockSpec((EXT, 1), lambda j, i: (0, 0)),
            pl.BlockSpec((1, 1, QB), lambda j, i: (j, 0, 0)),
        ],
        out_specs=[
            pl.BlockSpec((HALF, D), lambda j, i: (j, 0)),
            pl.BlockSpec((D, HALF), lambda j, i: (0, j)),
            pl.BlockSpec((1, WIN, QB), lambda j, i: (j, 0, 0)),
        ],
    )
    return pl.pallas_call(
        norm_kernel,
        grid_spec=spec,
        out_shape=[
            jax.ShapeDtypeStruct((EXT, D), BF),
            jax.ShapeDtypeStruct((D, EXT), BF),
            jax.ShapeDtypeStruct((BLOCKS, WIN, QB), F32),
        ],
        compiler_params=params(),
        cost_estimate=cost(EXT * D * 12, 5e6),
        name="norm_first",
    )(index.reshape(1), frames, halo, gain.reshape(1, D), rec_col, rec_row)


def wide(vo_ref):
    return jnp.concatenate([vo_ref[D + j * GC : D + (j + 1) * GC] for j in range(4)], axis=1)


def stack_heads(block):
    lane = lax.broadcasted_iota(jnp.int32, block.shape, 1)
    zero = jnp.zeros_like(block)
    low = jnp.where(lane < HEAD_DIM, block, zero)
    high = jnp.where(lane < HEAD_DIM, zero, block)
    return jnp.concatenate([low, high], axis=0)


def pick_heads(both):
    return jnp.concatenate([both[:HEAD_DIM, :QB], both[HEAD_DIM:, QB:]], axis=0).T


def context_kernel(n_ref, qk_ref, vo_ref, bias_ref, q_ref, k_ref, v_ref, ctx_ref, lse_ref, vt_ref):
    n = n_ref[...]
    q_ref[...] = dot(n_ref[HALF : HALF + ROWS], qk_ref[:D]).astype(BF) * 0.125
    k_ref[...] = dot(n, qk_ref[D:]).astype(BF)
    v = dot(n, vo_ref[:D])
    v_ref[...] = v.astype(BF)
    vt_ref[...] = v.T.astype(BF)
    for b in range(BLOCKS):
        win = slice(b * QB, b * QB + WIN)
        rows = slice(b * QB, b * QB + QB)
        queries = stack_heads(q_ref[rows])
        bias = bias_ref[b]
        scores = dot_nt(k_ref[win], queries) + jnp.concatenate([bias, bias], axis=1)
        peak = jnp.max(scores, axis=0, keepdims=True)
        weights = jnp.exp(scores - peak)
        total = jnp.sum(weights, axis=0, keepdims=True)
        both = dot(vt_ref[:, win], weights.astype(BF)) / total
        ctx_ref[rows] = pick_heads(both).astype(BF)
        lse_ref[b] = peak + jnp.log(total)


def run_context(normed, qk, vo, bias):
    return pl.pallas_call(
        context_kernel,
        in_specs=[WHOLE] * 4,
        out_specs=[WHOLE] * 5,
        out_shape=[
            jax.ShapeDtypeStruct((ROWS, GC), BF),
            jax.ShapeDtypeStruct((EXT, GC), BF),
            jax.ShapeDtypeStruct((EXT, GC), BF),
            jax.ShapeDtypeStruct((ROWS, GC), BF),
            jax.ShapeDtypeStruct((BLOCKS, 1, 2 * QB), F32),
        ],
        scratch_shapes=[VMEM((GC, EXT), BF)],
        compiler_params=params(),
        cost_estimate=cost(2e9, 4e6, BLOCKS * WIN * 2 * QB),
        name="context",
    )(normed, qk, vo, bias)


def attention_back_kernel(
    gml_ref, vo_ref, ctx_ref, q_ref, k_ref, v_ref, lse_ref, bias_ref, nt_ref,
    dq_ref, dk_ref, dv_ref, dw_ref, g_ref, kt_ref, dka_ref, dva_ref,
):
    g_ref[...] = dot_nt(gml_ref[...], wide(vo_ref)).astype(BF)
    grad_out = dot(ctx_ref[...].T, gml_ref[...]).astype(BF)
    for j in range(4):
        dw_ref[3 * D + j * GC : 3 * D + (j + 1) * GC] = grad_out[:, j * GC : (j + 1) * GC]
    kt_ref[...] = k_ref[...].T
    dka_ref[...] = jnp.zeros_like(dka_ref)
    dva_ref[...] = jnp.zeros_like(dva_ref)
    for b in range(BLOCKS):
        win = slice(b * QB, b * QB + WIN)
        rows = slice(b * QB, b * QB + QB)
        queries = stack_heads(q_ref[rows])
        grads = stack_heads(g_ref[rows])
        bias = bias_ref[b]
        scores = dot_nt(k_ref[win], queries) + jnp.concatenate([bias, bias], axis=1)
        prob = jnp.exp(scores - lse_ref[b])
        grad_prob = dot_nt(v_ref[win], grads)
        inner = jnp.sum(prob * grad_prob, axis=0, keepdims=True)
        grad_scores = (prob * (grad_prob - inner)).astype(BF)
        dva_ref[win] += dot(prob.astype(BF), grads)
        dka_ref[win] += dot(grad_scores, queries)
        both = dot(kt_ref[:, win], grad_scores)
        dq_ref[rows] = (pick_heads(both) * 0.125).astype(BF)
    dk_ref[...] = dka_ref[...].astype(BF)
    dv_ref[...] = dva_ref[...].astype(BF)
    dw_ref[:D] = dot(nt_ref[:, HALF : HALF + ROWS], dq_ref[...]).astype(BF)
    dw_ref[D : 2 * D] = dot(nt_ref[...], dk_ref[...]).astype(BF)
    dw_ref[2 * D : 3 * D] = dot(nt_ref[...], dv_ref[...]).astype(BF)


def run_attention_back(gml, vo, ctx, q, k, v, lse, bias, nt):
    return pl.pallas_call(
        attention_back_kernel,
        in_specs=[WHOLE] * 9,
        out_specs=[WHOLE] * 4,
        out_shape=[
            jax.ShapeDtypeStruct((ROWS, GC), BF),
            jax.ShapeDtypeStruct((EXT, GC), BF),
            jax.ShapeDtypeStruct((EXT, GC), BF),
            jax.ShapeDtypeStruct((4 * D, GC), BF),
        ],
        scratch_shapes=[
            VMEM((ROWS, GC), BF),
            VMEM((GC, EXT), BF),
            VMEM((EXT, GC), F32),
            VMEM((EXT, GC), F32),
        ],
        compiler_params=params(),
        cost_estimate=cost(4e9, 6e6, BLOCKS * WIN * 2 * QB),
        name="attention_back",
    )(gml, vo, ctx, q, k, v, lse, bias, nt)


def feed_kernel(*refs):
    own_ref, up_ref, gain_ref = refs[:3]
    ctx = refs[3:7]
    vo = refs[7:11]
    wi = refs[11:15]
    wu = refs[15:19]
    gm_ref, gml_ref, keep_ref, give_ref = refs[19:23]
    sc_ref, n2_ref, n2t_ref, upt_ref, gs_ref = refs[23:]
    up = up_ref[...]
    middle = own_ref[...].astype(F32)
    for k in range(4):
        middle = middle + dot(ctx[k][...], wide(vo[k]))
    scaled, inverse = norm_rows(middle)
    sc_ref[...] = scaled
    normed = scaled * gain_ref[...]
    n2_ref[...] = normed.astype(BF)
    n2t_ref[...] = normed.T.astype(BF)
    upt_ref[...] = up.T
    for k in range(4):
        pre = dot(n2_ref[...], wi[k][...])
        grad_act = dot_nt(up_ref[...], wu[k][...]) * 0.5
        gate = jax.nn.sigmoid(pre)
        act = (pre * gate).astype(BF)
        grad_inner = (grad_act * gate * (1.0 + pre * (1.0 - gate))).astype(BF)
        to = give_ref if k % 2 else keep_ref
        to[k // 2, :D] = dot(n2t_ref[...], grad_inner).astype(BF)
        to[k // 2, D:] = (dot(upt_ref[...], act) * 0.5).astype(BF)
        back = dot_nt(grad_inner, wi[k][...])
        if k == 0:
            gs_ref[...] = back
        else:
            gs_ref[...] += back
    grad_middle = up.astype(F32) + norm_back(gs_ref[...], sc_ref[...], inverse, gain_ref[...])
    gm_ref[...] = grad_middle
    gml_ref[...] = grad_middle.astype(BF)


def run_feed(own, up, gain, ctx, vo, wi, wu):
    return pl.pallas_call(
        feed_kernel,
        in_specs=[WHOLE] * 19,
        out_specs=[WHOLE] * 4,
        out_shape=[
            jax.ShapeDtypeStruct((ROWS, D), F32),
            jax.ShapeDtypeStruct((ROWS, D), BF),
            jax.ShapeDtypeStruct((2, 2 * D, D), BF),
            jax.ShapeDtypeStruct((2, 2 * D, D), BF),
        ],
        scratch_shapes=[
            VMEM((ROWS, D), F32),
            VMEM((ROWS, D), BF),
            VMEM((D, ROWS), BF),
            VMEM((D, ROWS), BF),
            VMEM((ROWS, D), F32),
        ],
        compiler_params=params(),
        cost_estimate=cost(7e9, 14e6, ROWS * 2048),
        name="feed",
    )(own, up, gain.reshape(1, D), *ctx, *vo, *wi, *wu)


def first_kernel(*refs):
    dq, dk, dv = refs[0:4], refs[4:8], refs[8:12]
    qk, vo = refs[12:16], refs[16:20]
    own_ref, before_ref, after_ref = refs[20:]
    acc = None
    for k in range(4):
        term = dot_nt(dk[k][...], qk[k][D:]) + dot_nt(dv[k][...], vo[k][:D])
        acc = term if acc is None else acc + term
    before_ref[...] = acc[:HALF].astype(BF)
    after_ref[...] = acc[HALF + ROWS :].astype(BF)
    own = acc[HALF : HALF + ROWS]
    for k in range(4):
        own = own + dot_nt(dq[k][...], qk[k][:D])
    own_ref[...] = own


def run_first(dq, dk, dv, qk, vo):
    return pl.pallas_call(
        first_kernel,
        in_specs=[WHOLE] * 20,
        out_specs=[WHOLE] * 3,
        out_shape=[
            jax.ShapeDtypeStruct((ROWS, D), F32),
            jax.ShapeDtypeStruct((HALF, D), BF),
            jax.ShapeDtypeStruct((HALF, D), BF),
        ],
        compiler_params=params(),
        cost_estimate=cost(3e9, 6e6),
        name="first_grad",
    )(*dq, *dk, *dv, *qk, *vo)


def last_kernel(gf_ref, low_ref, high_ref, own_ref, gain_ref, gm_ref, out_ref):
    scaled, inverse = norm_rows(own_ref[...].astype(F32))
    grad = gf_ref[...] + jnp.concatenate(
        [low_ref[...].astype(F32), high_ref[...].astype(F32)], axis=0
    )
    out_ref[...] = gm_ref[...] + norm_back(grad, scaled, inverse, gain_ref[...])


def run_last(gf, low, high, own, gain, gm):
    return pl.pallas_call(
        last_kernel,
        in_specs=[WHOLE] * 6,
        out_shape=jax.ShapeDtypeStruct((ROWS, D), F32),
        compiler_params=params(),
        cost_estimate=cost(ROWS * D * 20, 5e6),
        name="frames_grad",
    )(gf, low, high, own, gain.reshape(1, D), gm)


def pack_kernel(i_ref, frames_ref, q_ref, k_ref, v_ref, o_ref, edge_ref, all_ref, qk_ref, vo_ref):
    edge_ref[...] = frames_ref[...]
    q, k, v, o = q_ref[...], k_ref[...], v_ref[...], o_ref[...]
    out = jnp.concatenate([o[:, j * GC : (j + 1) * GC] for j in range(4)], axis=0)
    qk_ref[:D] = q
    qk_ref[D:] = k
    vo_ref[:D] = v
    vo_ref[D:] = out
    all_ref[0, :D] = q
    all_ref[0, D:] = k
    all_ref[1, :D] = v
    all_ref[1, D:] = out


def run_pack(frames, wq, wk, wv, wo, index):
    def whole(shape):
        return pl.BlockSpec(shape, lambda j, i: (0,) * len(shape))

    half = (2 * D, GC)
    return pl.pallas_call(
        pack_kernel,
        grid_spec=pltpu.PrefetchScalarGridSpec(
            num_scalar_prefetch=1,
            grid=(1,),
            in_specs=[
                pl.BlockSpec((HALF, D), lambda j, i: (jnp.where(i[0] == 3, 7, 0), 0)),
                whole((D, GC)),
                whole((D, GC)),
                whole((D, GC)),
                whole((GC, D)),
            ],
            out_specs=[whole((HALF, D)), whole((2,) + half), whole(half), whole(half)],
        ),
        out_shape=[
            jax.ShapeDtypeStruct((HALF, D), BF),
            jax.ShapeDtypeStruct((2,) + half, BF),
            jax.ShapeDtypeStruct(half, BF),
            jax.ShapeDtypeStruct(half, BF),
        ],
        compiler_params=params(),
        cost_estimate=cost(1e5, 3e6),
        name="pack",
    )(index.reshape(1), frames, wq, wk, wv, wo)


def f32(ref):
    return ref[...].astype(F32)


def feed_split_kernel(keep_ref, got_ref, near_ref, a_ref, b_ref):
    near_ref[...] = (keep_ref[0].astype(F32) + got_ref[0].astype(F32)).astype(BF)
    a_ref[...] = (keep_ref[1, :D].astype(F32) + got_ref[1, :D].astype(F32)).astype(BF)
    b_ref[...] = (keep_ref[1, D:].astype(F32) + got_ref[1, D:].astype(F32)).astype(BF)


def proj_split_kernel(keep_ref, got_ref, a_ref, b_ref):
    h = 2 * D
    a_ref[...] = (keep_ref[:h].astype(F32) + got_ref[:h].astype(F32)).astype(BF)
    b_ref[...] = (keep_ref[h:].astype(F32) + got_ref[h:].astype(F32)).astype(BF)


def feed_join_kernel(near_ref, a_ref, b_ref, out_ref):
    out_ref[:8] = (near_ref[:8].astype(F32) + a_ref[...].astype(F32)).astype(BF)
    out_ref[8:] = (near_ref[8:].astype(F32) + b_ref[...].astype(F32)).astype(BF)


def proj_join_kernel(keep_ref, got_ref, a_ref, b_ref, out_ref):
    near = keep_ref[...].astype(F32) + got_ref[...].astype(F32)
    out_ref[:8] = (near[:8] + a_ref[...].astype(F32)).astype(BF)
    out_ref[8:] = (near[8:] + b_ref[...].astype(F32)).astype(BF)


def sum_kernel(parts_ref, out_ref):
    total = parts_ref[0].astype(F32)
    for n in range(1, 16):
        total = total + parts_ref[n].astype(F32)
    out_ref[...] = total.astype(BF)


def spread_kernel(mine_ref, got_ref, out_ref):
    total = (f32(mine_ref) + f32(got_ref)).astype(BF)
    for n in range(16):
        out_ref[n] = total


def feed_end_kernel(scale, total_ref, inner_ref, outer_ref):
    for j in range(8):
        inner_ref[j * 64 : (j + 1) * 64] = total_ref[j].astype(F32) * scale
    outer = jnp.concatenate([total_ref[8 + j] for j in range(8)], axis=0)
    outer_ref[...] = outer.astype(F32).T * scale


def proj_end_kernel(scale, total_ref, q_ref, k_ref, v_ref, o_ref):
    for j in range(4):
        rows = slice(j * GC, (j + 1) * GC)
        q_ref[rows] = total_ref[j].astype(F32) * scale
        k_ref[rows] = total_ref[4 + j].astype(F32) * scale
        v_ref[rows] = total_ref[8 + j].astype(F32) * scale
        o_ref[:, rows] = total_ref[12 + j].astype(F32) * scale


def small(kernel, name, shapes, *arrays, final=False):
    outs = [jax.ShapeDtypeStruct(shape, F32 if final else BF) for shape in shapes]
    extra = {} if final else {"out_specs": [WHOLE] * len(outs)}
    return pl.pallas_call(
        kernel,
        in_specs=[WHOLE] * len(arrays),
        out_shape=outs,
        compiler_params=params(),
        cost_estimate=cost(1e6, 2e6),
        name=name,
        **extra,
    )(*arrays)


def swap(array, bits):
    return lax.ppermute(array, AXES, [(n, n ^ bits) for n in range(128)])


def after(first, *later):
    return lax.optimization_barrier((first,) + later)[0]


PEERS = [[2 * n + half for n in range(16)] for half in range(2)]


def exchange(parts):
    return lax.all_to_all(parts, "tm", 0, 0, axis_index_groups=PEERS, tiled=True)


def total_of(parts, name):
    got = exchange(parts)
    (mine,) = small(sum_kernel, name + "_sum", [parts.shape[1:]], got)
    other = swap(mine, 4)
    (spread,) = small(spread_kernel, name + "_spread", [parts.shape], mine, other)
    return exchange(spread)


def local(
    frames,
    upstream,
    recording,
    first_gain,
    query_weight,
    key_weight,
    value_weight,
    out_weight,
    second_gain,
    inner_weight,
    outer_weight,
):
    t = lax.axis_index("tm")
    i = lax.axis_index("ffn")
    slab = frames.shape[0]
    devices = lax.axis_size("tm") * 4
    scale = 1.0 / math.sqrt(recording.shape[0])

    edge, own_proj, qk_own, vo_own = run_pack(
        frames, query_weight, key_weight, value_weight, out_weight, i
    )
    pairs = [(4 * n + 3, 4 * n + 4) for n in range(31)] + [(4 * n + 4, 4 * n + 3) for n in range(31)]
    halo = lax.ppermute(edge, AXES, pairs)
    qk_far, vo_far = swap(qk_own, 2), swap(vo_own, 6)
    near_proj = swap(own_proj, 1)
    qk = [qk_own, near_proj[0], qk_far, swap(qk_far, 1)]
    vo = [vo_own, near_proj[1], vo_far, swap(vo_far, 1)]

    inner_own = after(inner_weight, qk_far, vo_far)
    outer_own = after(outer_weight, qk_far, vo_far)
    inner_far, outer_far = swap(inner_own, 2), swap(outer_own, 6)
    wi = [inner_weight, swap(inner_own, 1), inner_far, swap(inner_far, 1)]
    wu = [outer_weight, swap(outer_own, 1), outer_far, swap(outer_far, 1)]

    record_pad = jnp.pad(recording, (HALF, HALF), constant_values=-1)
    rec_ext = lax.dynamic_slice_in_dim(record_pad, t * slab + i * ROWS, EXT)
    own = lax.dynamic_slice_in_dim(frames, i * ROWS, ROWS, 0)
    up = lax.dynamic_slice_in_dim(upstream, i * ROWS, ROWS, 0)

    normed, normed_t, bias = run_norm(frames, halo, first_gain, rec_ext, i)
    qs, ks, vs, ctx, lse = [], [], [], [], []
    for k in range(4):
        q, key, v, c, s = run_context(normed, qk[k], vo[k], bias)
        qs.append(q)
        ks.append(key)
        vs.append(v)
        ctx.append(c)
        lse.append(s)

    grad_middle, gml, keep, give = run_feed(own, up, second_gain, ctx, vo, wi, wu)
    got = swap(give, 1)
    near, far_a, far_b = small(
        feed_split_kernel, "feed_split", [(2 * D, D), (D, D), (D, D)], keep, got
    )

    dq, dk, dv, dw = [None] * 4, [None] * 4, [None] * 4, [None] * 4

    def back(k, grads):
        dq[k], dk[k], dv[k], dw[k] = run_attention_back(
            grads, vo[k], ctx[k], qs[k], ks[k], vs[k], lse[k], bias, normed_t
        )

    back(3, gml)
    got3 = swap(dw[3], 1)
    back(2, after(gml, near, dq[3]))
    proj_a, proj_b = small(proj_split_kernel, "proj_split", [(2 * D, GC)] * 2, dw[2], got3)
    back(1, after(gml, proj_a))
    got1 = swap(dw[1], 1)
    back(0, after(gml, dq[1]))
    gf, before, behind = run_first(dq, dk, dv, qk, vo)
    low = lax.ppermute(behind, AXES, [(n, n + 1) for n in range(devices - 1)])
    high = lax.ppermute(before, AXES, [(n + 1, n) for n in range(devices - 1)])

    feed_got_a, feed_got_b = swap(far_a, 2), swap(far_b, 6)
    (feed_sum,) = small(
        feed_join_kernel, "feed_join", [(16, 64, D)],
        near.reshape(16, 64, D), feed_got_a.reshape(8, 64, D), feed_got_b.reshape(8, 64, D),
    )
    proj_got_a, proj_got_b = swap(proj_a, 2), swap(proj_b, 6)
    (proj_sum,) = small(
        proj_join_kernel, "proj_join", [(16, GC, GC)],
        dw[0].reshape(16, GC, GC), got1.reshape(16, GC, GC),
        proj_got_a.reshape(8, GC, GC), proj_got_b.reshape(8, GC, GC),
    )
    feed_total = total_of(feed_sum, "feed")
    proj_total = total_of(after(proj_sum, gf), "proj")
    grad_frames = run_last(gf, low, high, own, first_gain, grad_middle)

    grad_inner, grad_outer = small(
        functools.partial(feed_end_kernel, scale), "feed_end", [(D, D), (D, D)], feed_total,
        final=True,
    )
    grad_q, grad_k, grad_v, grad_o = small(
        functools.partial(proj_end_kernel, scale), "proj_end", [(D, GC)] * 3 + [(GC, D)], proj_total,
        final=True,
    )
    return (grad_frames, grad_q, grad_k, grad_v, grad_o, grad_inner, grad_outer)


def solution(mesh):
    in_specs = (
        P("tm", None),
        P("tm", None),
        P(),
        P(),
        P(None, "ffn"),
        P(None, "ffn"),
        P(None, "ffn"),
        P("ffn", None),
        P(),
        P(None, "ffn"),
        P("ffn", None),
    )
    out_specs = (
        P(("tm", "ffn"), None),
        P(None, "ffn"),
        P(None, "ffn"),
        P(None, "ffn"),
        P("ffn", None),
        P(None, "ffn"),
        P("ffn", None),
    )
    return jax.shard_map(local, mesh=mesh, in_specs=in_specs, out_specs=out_specs, check_vma=False)
```

```python
import functools
import math

import jax
import jax.numpy as jnp
from jax import lax
from jax.experimental import pallas as pl
from jax.experimental.pallas import tpu as pltpu
from jax.sharding import PartitionSpec as P

HEAD_DIM = 64
HALF = 256
ROWS = 512
EXT = ROWS + 2 * HALF
QB = 128
WIN = QB + 2 * HALF
BLOCKS = ROWS // QB
GC = 128
D = 512
epsilon = 1e-05
masked_score = -1e30
BF = jnp.bfloat16
F32 = jnp.float32
AXES = ("tm", "ffn")
VMEM = pltpu.VMEM
WHOLE = pl.BlockSpec(memory_space=pltpu.VMEM)


def dot(a, b):
    return jnp.dot(a, b, preferred_element_type=F32)


def dot_nt(a, b):
    return lax.dot_general(a, b, (((1,), (1,)), ((), ())), preferred_element_type=F32)


def params(mib=16):
    return pltpu.CompilerParams(vmem_limit_bytes=mib * 1024 * 1024)


def cost(flops, nbytes, trans=0):
    return pl.CostEstimate(
        flops=int(flops / 8), bytes_accessed=int(nbytes / 8), transcendentals=int(trans / 8)
    )


def norm_rows(x):
    center = jnp.mean(x, axis=-1, keepdims=True)
    shifted = x - center
    inverse = lax.rsqrt(jnp.mean(shifted * shifted, axis=-1, keepdims=True) + epsilon)
    return shifted * inverse, inverse


def norm_back(grad_normed, scaled, inverse, gain):
    weighted = grad_normed * gain
    first = jnp.mean(weighted, axis=-1, keepdims=True)
    second = jnp.mean(weighted * scaled, axis=-1, keepdims=True)
    return inverse * (weighted - first - scaled * second)


def norm_kernel(i_ref, ext_ref, halo_ref, gain_ref, col_ref, row_ref, n_ref, nt_ref, bias_ref):
    step = pl.program_id(0)
    outside = ((i_ref[0] == 0) & (step == 0)) | ((i_ref[0] == 3) & (step == 3))
    x = jnp.where(outside, halo_ref[...].astype(F32), ext_ref[...].astype(F32))
    scaled, _ = norm_rows(x)
    normed = scaled * gain_ref[...]
    n_ref[...] = normed.astype(BF)
    nt_ref[...] = normed.T.astype(BF)
    keys = col_ref[pl.ds(pl.multiple_of(step * QB, QB), WIN), :]
    offset = lax.broadcasted_iota(jnp.int32, (WIN, QB), 0) - lax.broadcasted_iota(
        jnp.int32, (WIN, QB), 1
    )
    band = (offset >= 0) & (offset < 2 * HALF)
    bias_ref[0] = jnp.where(band & (keys == row_ref[0]), 0.0, masked_score)


def run_norm(ext, halo, gain, rec_col, rec_row, index):
    spec = pltpu.PrefetchScalarGridSpec(
        num_scalar_prefetch=1,
        grid=(4,),
        in_specs=[
            pl.BlockSpec((HALF, D), lambda j, i: (j, 0)),
            pl.BlockSpec((HALF, D), lambda j, i: (0, 0)),
            pl.BlockSpec((1, D), lambda j, i: (0, 0)),
            pl.BlockSpec((EXT, 1), lambda j, i: (0, 0)),
            pl.BlockSpec((1, 1, QB), lambda j, i: (j, 0, 0)),
        ],
        out_specs=[
            pl.BlockSpec((HALF, D), lambda j, i: (j, 0)),
            pl.BlockSpec((D, HALF), lambda j, i: (0, j)),
            pl.BlockSpec((1, WIN, QB), lambda j, i: (j, 0, 0)),
        ],
    )
    return pl.pallas_call(
        norm_kernel,
        grid_spec=spec,
        out_shape=[
            jax.ShapeDtypeStruct((EXT, D), BF),
            jax.ShapeDtypeStruct((D, EXT), BF),
            jax.ShapeDtypeStruct((BLOCKS, WIN, QB), F32),
        ],
        compiler_params=params(),
        cost_estimate=cost(EXT * D * 12, 5e6),
        name="norm_first",
    )(index.reshape(1), ext, halo, gain.reshape(1, D), rec_col, rec_row)


def wide(vo_ref):
    return jnp.concatenate([vo_ref[D + j * GC : D + (j + 1) * GC] for j in range(4)], axis=1)


def square(packed_ref):
    return jnp.concatenate([packed_ref[(2 + j) * D : (3 + j) * D] for j in range(4)], axis=1)


def stack_heads(block):
    lane = lax.broadcasted_iota(jnp.int32, block.shape, 1)
    zero = jnp.zeros_like(block)
    low = jnp.where(lane < HEAD_DIM, block, zero)
    high = jnp.where(lane < HEAD_DIM, zero, block)
    return jnp.concatenate([low, high], axis=0)


def pick_heads(both):
    return jnp.concatenate([both[:HEAD_DIM, :QB], both[HEAD_DIM:, QB:]], axis=0).T


def context_kernel(n_ref, qk_ref, vo_ref, bias_ref, q_ref, k_ref, v_ref, ctx_ref, lse_ref, vt_ref):
    n = n_ref[...]
    q_ref[...] = dot(n_ref[HALF : HALF + ROWS], qk_ref[:D]).astype(BF) * 0.125
    k_ref[...] = dot(n, qk_ref[D : 2 * D]).astype(BF)
    v = dot(n, vo_ref[:D])
    v_ref[...] = v.astype(BF)
    vt_ref[...] = v.T.astype(BF)
    for b in range(BLOCKS):
        win = slice(b * QB, b * QB + WIN)
        rows = slice(b * QB, b * QB + QB)
        queries = stack_heads(q_ref[rows])
        bias = bias_ref[b]
        scores = dot_nt(k_ref[win], queries) + jnp.concatenate([bias, bias], axis=1)
        peak = jnp.max(scores, axis=0, keepdims=True)
        weights = jnp.exp(scores - peak)
        total = jnp.sum(weights, axis=0, keepdims=True)
        both = dot(vt_ref[:, win], weights.astype(BF)) / total
        ctx_ref[rows] = pick_heads(both).astype(BF)
        lse_ref[b] = peak + jnp.log(total)


def run_context(normed, qk, vo, bias):
    return pl.pallas_call(
        context_kernel,
        in_specs=[WHOLE] * 4,
        out_specs=[WHOLE] * 5,
        out_shape=[
            jax.ShapeDtypeStruct((ROWS, GC), BF),
            jax.ShapeDtypeStruct((EXT, GC), BF),
            jax.ShapeDtypeStruct((EXT, GC), BF),
            jax.ShapeDtypeStruct((ROWS, GC), BF),
            jax.ShapeDtypeStruct((BLOCKS, 1, 2 * QB), F32),
        ],
        scratch_shapes=[VMEM((GC, EXT), BF)],
        compiler_params=params(),
        cost_estimate=cost(2e9, 4e6, BLOCKS * WIN * 2 * QB),
        name="context",
    )(normed, qk, vo, bias)


def attention_back_kernel(place, *refs):
    gml_ref, qk_ref, vo_ref, ctx_ref, q_ref, k_ref, v_ref, lse_ref, bias_ref, nt_ref = refs[:10]
    refs = refs[10:]
    if place > 0:
        gf_in_ref, refs = refs[0], refs[1:]
    dw_ref, gf_ref, refs = refs[0], refs[1], refs[2:]
    if place == 2:
        before_ref, behind_ref, refs = refs[0], refs[1], refs[2:]
    g_ref, kt_ref, dq_ref, dka_ref, dva_ref, dk_ref, dv_ref = refs
    g_ref[...] = dot_nt(gml_ref[...], wide(vo_ref)).astype(BF)
    grad_out = dot(ctx_ref[...].T, gml_ref[...]).astype(BF)
    for j in range(4):
        dw_ref[3 * D + j * GC : 3 * D + (j + 1) * GC] = grad_out[:, j * GC : (j + 1) * GC]
    kt_ref[...] = k_ref[...].T
    dka_ref[...] = jnp.zeros_like(dka_ref)
    dva_ref[...] = jnp.zeros_like(dva_ref)
    for b in range(BLOCKS):
        win = slice(b * QB, b * QB + WIN)
        rows = slice(b * QB, b * QB + QB)
        queries = stack_heads(q_ref[rows])
        grads = stack_heads(g_ref[rows])
        bias = bias_ref[b]
        scores = dot_nt(k_ref[win], queries) + jnp.concatenate([bias, bias], axis=1)
        prob = jnp.exp(scores - lse_ref[b])
        grad_prob = dot_nt(v_ref[win], grads)
        inner = jnp.sum(prob * grad_prob, axis=0, keepdims=True)
        grad_scores = (prob * (grad_prob - inner)).astype(BF)
        dva_ref[win] += dot(prob.astype(BF), grads)
        dka_ref[win] += dot(grad_scores, queries)
        both = dot(kt_ref[:, win], grad_scores)
        dq_ref[rows] = (pick_heads(both) * 0.125).astype(BF)
    dk_ref[...] = dka_ref[...].astype(BF)
    dv_ref[...] = dva_ref[...].astype(BF)
    dw_ref[:D] = dot(nt_ref[:, HALF : HALF + ROWS], dq_ref[...]).astype(BF)
    dw_ref[D : 2 * D] = dot(nt_ref[...], dk_ref[...]).astype(BF)
    dw_ref[2 * D : 3 * D] = dot(nt_ref[...], dv_ref[...]).astype(BF)
    for part in range(4):
        rows = slice(part * HALF, (part + 1) * HALF)
        term = dot_nt(dk_ref[rows], qk_ref[D : 2 * D]) + dot_nt(dv_ref[rows], vo_ref[:D])
        if part in (1, 2):
            own = slice((part - 1) * HALF, part * HALF)
            term = term + dot_nt(dq_ref[own], qk_ref[:D])
        if place > 0:
            term = term + gf_in_ref[rows]
        if place < 2:
            gf_ref[rows] = term
        elif part == 0:
            before_ref[...] = term.astype(BF)
        elif part == 3:
            behind_ref[...] = term.astype(BF)
        else:
            gf_ref[own] = term


def run_attention_back(place, gf, *arrays):
    gf_shape = jax.ShapeDtypeStruct((ROWS if place == 2 else EXT, D), F32)
    edges = [jax.ShapeDtypeStruct((HALF, D), BF)] * 2 if place == 2 else []
    if place > 0:
        arrays = arrays + (gf,)
    return pl.pallas_call(
        functools.partial(attention_back_kernel, place),
        in_specs=[WHOLE] * len(arrays),
        out_specs=[WHOLE] * (2 + len(edges)),
        out_shape=[jax.ShapeDtypeStruct((4 * D, GC), BF), gf_shape] + edges,
        scratch_shapes=[
            VMEM((ROWS, GC), BF),
            VMEM((GC, EXT), BF),
            VMEM((ROWS, GC), BF),
            VMEM((EXT, GC), F32),
            VMEM((EXT, GC), F32),
            VMEM((EXT, GC), BF),
            VMEM((EXT, GC), BF),
        ],
        compiler_params=params(),
        cost_estimate=cost(4e9, 6e6, BLOCKS * WIN * 2 * QB),
        name="attention_back",
    )(*arrays)


def feed_group(n2_ref, n2t_ref, up_ref, upt_ref, low_ref, high_ref, to_ref):
    inner = square(low_ref)
    pre = dot(n2_ref[...], inner)
    grad_act = dot_nt(up_ref[...], square(high_ref)) * 0.5
    gate = jax.nn.sigmoid(pre)
    act = (pre * gate).astype(BF)
    grad_inner = (grad_act * gate * (1.0 + pre * (1.0 - gate))).astype(BF)
    to_ref[:D] = dot(n2t_ref[...], grad_inner).astype(BF)
    to_ref[D:] = (dot(upt_ref[...], act) * 0.5).astype(BF)
    return dot_nt(grad_inner, inner)


def feed_near_kernel(*refs):
    ext_ref, up_ref, gain_ref = refs[:3]
    ctx, high, low = refs[3:7], refs[7:11], refs[11:13]
    give_ref, keep_ref, sc_ref, inv_ref, n2_ref, n2t_ref, upt_ref, gs_ref = refs[13:]
    middle = ext_ref[HALF : HALF + ROWS].astype(F32)
    for k in range(4):
        middle = middle + dot(ctx[k][...], wide(high[k]))
    scaled, inverse = norm_rows(middle)
    sc_ref[...] = scaled
    inv_ref[...] = inverse
    normed = scaled * gain_ref[...]
    n2_ref[...] = normed.astype(BF)
    n2t_ref[...] = normed.T.astype(BF)
    upt_ref[...] = up_ref[...].T
    shared = (n2_ref, n2t_ref, up_ref, upt_ref)
    gs_ref[...] = feed_group(*shared, low[1], high[1], give_ref)
    gs_ref[...] += feed_group(*shared, low[0], high[0], keep_ref)


def run_feed_near(ext, up, gain, ctx, high, low):
    return pl.pallas_call(
        feed_near_kernel,
        in_specs=[WHOLE] * 13,
        out_specs=[WHOLE] * 8,
        out_shape=[
            jax.ShapeDtypeStruct((2 * D, D), BF),
            jax.ShapeDtypeStruct((2 * D, D), BF),
            jax.ShapeDtypeStruct((ROWS, D), F32),
            jax.ShapeDtypeStruct((ROWS, 1), F32),
            jax.ShapeDtypeStruct((ROWS, D), BF),
            jax.ShapeDtypeStruct((D, ROWS), BF),
            jax.ShapeDtypeStruct((D, ROWS), BF),
            jax.ShapeDtypeStruct((ROWS, D), F32),
        ],
        compiler_params=params(),
        cost_estimate=cost(4e9, 14e6, ROWS * 1024),
        name="feed_near",
    )(ext, up, gain.reshape(1, D), *ctx, *high, *low)


def feed_far_kernel(*refs):
    up_ref, gain_ref, sc_ref, inv_ref, n2_ref, n2t_ref, upt_ref, gs_in_ref = refs[:8]
    low, high = refs[8:10], refs[10:12]
    gm_ref, gml_ref, give_ref, keep_ref, gs_ref = refs[12:]
    shared = (n2_ref, n2t_ref, up_ref, upt_ref)
    gs_ref[...] = gs_in_ref[...] + feed_group(*shared, low[1], high[1], give_ref)
    gs_ref[...] += feed_group(*shared, low[0], high[0], keep_ref)
    grad_middle = up_ref[...].astype(F32) + norm_back(
        gs_ref[...], sc_ref[...], inv_ref[...], gain_ref[...]
    )
    gm_ref[...] = grad_middle
    gml_ref[...] = grad_middle.astype(BF)


def run_feed_far(up, gain, held, low, high):
    return pl.pallas_call(
        feed_far_kernel,
        in_specs=[WHOLE] * 12,
        out_specs=[WHOLE] * 4,
        out_shape=[
            jax.ShapeDtypeStruct((ROWS, D), F32),
            jax.ShapeDtypeStruct((ROWS, D), BF),
            jax.ShapeDtypeStruct((2 * D, D), BF),
            jax.ShapeDtypeStruct((2 * D, D), BF),
        ],
        scratch_shapes=[VMEM((ROWS, D), F32)],
        compiler_params=params(),
        cost_estimate=cost(4e9, 14e6, ROWS * 1024),
        name="feed_far",
    )(up, gain.reshape(1, D), *held, *low, *high)


def last_kernel(gf_ref, low_ref, high_ref, own_ref, gain_ref, gm_ref, out_ref):
    scaled, inverse = norm_rows(own_ref[HALF : HALF + ROWS].astype(F32))
    grad = gf_ref[...] + jnp.concatenate(
        [low_ref[...].astype(F32), high_ref[...].astype(F32)], axis=0
    )
    out_ref[...] = gm_ref[...] + norm_back(grad, scaled, inverse, gain_ref[...])


def run_last(gf, low, high, own, gain, gm):
    return pl.pallas_call(
        last_kernel,
        in_specs=[WHOLE] * 6,
        out_shape=jax.ShapeDtypeStruct((ROWS, D), F32),
        compiler_params=params(),
        cost_estimate=cost(ROWS * D * 20, 5e6),
        name="frames_grad",
    )(gf, low, high, own, gain.reshape(1, D), gm)


def edge_kernel(i_ref, frames_ref, edge_ref, sem):
    start = pl.multiple_of(jnp.where(i_ref[0] == 3, 3 * ROWS + HALF, 0), HALF)
    copy = pltpu.make_async_copy(frames_ref.at[pl.ds(start, HALF)], edge_ref, sem)
    copy.start()
    copy.wait()


def run_edge(frames, index):
    return pl.pallas_call(
        edge_kernel,
        in_specs=[
            pl.BlockSpec(memory_space=pltpu.SMEM),
            pl.BlockSpec(memory_space=pltpu.HBM),
        ],
        out_specs=WHOLE,
        out_shape=jax.ShapeDtypeStruct((HALF, D), BF),
        scratch_shapes=[pltpu.SemaphoreType.DMA],
        compiler_params=params(58),
        cost_estimate=cost(1e5, 1e6),
        name="edge",
    )(index.reshape(1), frames)


def pack_kernel(i_ref, frames_ref, up_in_ref, q_ref, k_ref, v_ref, o_ref, inner_ref, outer_ref,
                low_ref, high_ref, ext_ref, up_ref, sems):
    i = i_ref[0]

    def at(start, size):
        return pl.ds(pl.multiple_of(start, HALF), size)

    moves = [
        (q_ref, low_ref.at[pl.ds(0, D)]),
        (k_ref, low_ref.at[pl.ds(D, D)]),
        (v_ref, high_ref.at[pl.ds(0, D)]),
        (frames_ref.at[at(jnp.maximum(i * ROWS - HALF, 0), HALF)], ext_ref.at[pl.ds(0, HALF)]),
        (frames_ref.at[at(i * ROWS, ROWS)], ext_ref.at[pl.ds(HALF, ROWS)]),
        (
            frames_ref.at[at(jnp.minimum(i * ROWS + ROWS, 3 * ROWS + HALF), HALF)],
            ext_ref.at[pl.ds(HALF + ROWS, HALF)],
        ),
        (up_in_ref.at[at(i * ROWS, ROWS)], up_ref),
    ]
    for j in range(4):
        cols = pl.ds(j * GC, GC)
        moves.append((o_ref.at[:, cols], high_ref.at[pl.ds(D + j * GC, GC)]))
        moves.append((inner_ref.at[:, cols], low_ref.at[pl.ds((2 + j) * D, D)]))
        moves.append((outer_ref.at[:, cols], high_ref.at[pl.ds((2 + j) * D, D)]))
    copies = [
        pltpu.make_async_copy(source, target, sems.at[n])
        for n, (source, target) in enumerate(moves)
    ]
    for copy in copies:
        copy.start()
    for copy in copies:
        copy.wait()


def run_pack(frames, upstream, wq, wk, wv, wo, wi, wu, index):
    anywhere = pl.BlockSpec(memory_space=pltpu.HBM)
    shapes = [(6 * D, GC), (6 * D, GC), (EXT, D), (ROWS, D)]
    return pl.pallas_call(
        pack_kernel,
        in_specs=[pl.BlockSpec(memory_space=pltpu.SMEM)] + [anywhere] * 8,
        out_specs=[WHOLE] * 4,
        out_shape=[jax.ShapeDtypeStruct(shape, BF) for shape in shapes],
        scratch_shapes=[pltpu.SemaphoreType.DMA((19,))],
        compiler_params=params(58),
        cost_estimate=cost(1e5, 3e6),
        name="pack",
    )(index.reshape(1), frames, upstream, wq, wk, wv, wo, wi, wu)


def add(*terms):
    total = terms[0].astype(F32)
    for term in terms[1:]:
        total = total + term.astype(F32)
    return total.astype(BF)


def feed_split_kernel(near_ref, got_near_ref, far_ref, got_far_ref, out_ref, a_ref, b_ref):
    out_ref[...] = add(near_ref[...], got_near_ref[...])
    a_ref[...] = add(far_ref[:D], got_far_ref[:D])
    b_ref[...] = add(far_ref[D:], got_far_ref[D:])


def proj_split_kernel(keep_ref, got_ref, a_ref, b_ref):
    h = 2 * D
    a_ref[...] = add(keep_ref[:h], got_ref[:h])
    b_ref[...] = add(keep_ref[h:], got_ref[h:])


def join_kernel(near_ref, a_ref, b_ref, keep_ref, got_ref, pa_ref, pb_ref, out_ref):
    for n in range(16):
        feed, proj = (a_ref, pa_ref) if n < 8 else (b_ref, pb_ref)
        rows, part = slice(n * 64, (n + 1) * 64), slice(n % 8 * 64, (n % 8 + 1) * 64)
        out_ref[n, :64] = add(near_ref[rows], feed[part])
        for j in range(4):
            rows = slice(n * GC + j * 32, n * GC + (j + 1) * 32)
            part = slice(n % 8 * GC + j * 32, n % 8 * GC + (j + 1) * 32)
            out_ref[n, 64:, j * GC : (j + 1) * GC] = add(keep_ref[rows], got_ref[rows], proj[part])


def sum_kernel(parts_ref, out_ref):
    out_ref[...] = add(*[parts_ref[n] for n in range(16)])


def spread_kernel(mine_ref, got_ref, out_ref):
    total = add(mine_ref[...], got_ref[...])
    for n in range(16):
        out_ref[n] = total


def end_kernel(scale, total_ref, q_ref, k_ref, v_ref, o_ref, inner_ref, outer_ref):
    for n in range(8):
        inner_ref[n * 64 : (n + 1) * 64] = total_ref[n, :64].astype(F32) * scale
    outer = jnp.concatenate([total_ref[8 + n, :64] for n in range(8)], axis=0)
    outer_ref[...] = outer.astype(F32).T * scale
    for n in range(16):
        for j in range(4):
            block = total_ref[n, 64:, j * GC : (j + 1) * GC].astype(F32) * scale
            if n < 12:
                start = n % 4 * GC + j * 32
                (q_ref, k_ref, v_ref)[n // 4][start : start + 32] = block
            else:
                o_ref[j * 32 : (j + 1) * 32, (n - 12) * GC : (n - 11) * GC] = block


def small(kernel, name, shapes, *arrays, final=False):
    outs = [jax.ShapeDtypeStruct(shape, F32 if final else BF) for shape in shapes]
    extra = {} if final else {"out_specs": [WHOLE] * len(outs)}
    return pl.pallas_call(
        kernel,
        in_specs=[WHOLE] * len(arrays),
        out_shape=outs,
        compiler_params=params(),
        cost_estimate=cost(1e6, 2e6),
        name=name,
        **extra,
    )(*arrays)


def swap(array, bits):
    return lax.ppermute(array, AXES, [(n, n ^ bits) for n in range(128)])


def after(first, *later):
    return lax.optimization_barrier((first,) + later)[0]


PEERS = [[2 * n + half for n in range(16)] for half in range(2)]


def exchange(parts):
    return lax.all_to_all(parts, "tm", 0, 0, axis_index_groups=PEERS, tiled=True)


def local(
    frames,
    upstream,
    recording,
    first_gain,
    query_weight,
    key_weight,
    value_weight,
    out_weight,
    second_gain,
    inner_weight,
    outer_weight,
):
    t = lax.axis_index("tm")
    i = lax.axis_index("ffn")
    slab = frames.shape[0]
    devices = lax.axis_size("tm") * 4
    scale = 1.0 / math.sqrt(recording.shape[0])

    record_pad = jnp.pad(recording, (HALF, HALF), constant_values=-1)
    rec_ext = lax.dynamic_slice_in_dim(record_pad, t * slab + i * ROWS, EXT)
    rec_col = rec_ext.reshape(EXT, 1)
    rec_row = rec_ext[HALF : HALF + ROWS].reshape(BLOCKS, 1, QB)
    rec_col, rec_row, index = lax.optimization_barrier((rec_col, rec_row, i))
    edge = run_edge(frames, index)
    low_own, high_own, ext, up = run_pack(
        frames, upstream, query_weight, key_weight, value_weight, out_weight,
        inner_weight, outer_weight, after(index, edge),
    )
    pairs = [(4 * n + 3, 4 * n + 4) for n in range(31)] + [(4 * n + 4, 4 * n + 3) for n in range(31)]
    halo = lax.ppermute(edge, AXES, pairs)
    low_far, high_far = swap(after(low_own, halo), 2), swap(after(high_own, halo), 6)
    low_near, high_near = swap(low_own, 1), swap(high_own, 1)

    normed, normed_t, bias = run_norm(ext, halo, first_gain, rec_col, rec_row, i)
    qs, ks, vs, ctx, lse = [], [], [], [], []

    def forward(qk, vo):
        q, key, v, c, s = run_context(normed, qk, vo, bias)
        qs.append(q)
        ks.append(key)
        vs.append(v)
        ctx.append(c)
        lse.append(s)

    forward(low_own, high_own)
    forward(low_near, high_near)
    low_far, high_far = after(low_far, ctx[1]), after(high_far, ctx[1])
    low = [low_own, low_near, low_far, swap(low_far, 1)]
    high = [high_own, high_near, high_far, swap(high_far, 1)]
    forward(low[2], high[2])
    forward(low[3], high[3])

    give1, keep0, *held = run_feed_near(ext, up, second_gain, ctx, high, low[:2])
    got_near = swap(give1, 1)
    grad_middle, gml, give3, keep2 = run_feed_far(up, second_gain, held, low[2:], high[2:])
    got_far = swap(give3, 1)
    near, far_a, far_b = small(
        feed_split_kernel, "feed_split", [(2 * D, D), (D, D), (D, D)],
        keep0, got_near, keep2, got_far,
    )

    dw = [None] * 4

    def back(place, gf, k, grads):
        dw[k], *rest = run_attention_back(
            place, gf, grads, low[k], high[k], ctx[k], qs[k], ks[k], vs[k], lse[k], bias, normed_t
        )
        return rest

    (gf,) = back(0, None, 3, gml)
    got3 = swap(dw[3], 1)
    (gf,) = back(1, gf, 2, after(gml, near, gf))
    proj_a, proj_b = small(proj_split_kernel, "proj_split", [(2 * D, GC)] * 2, dw[2], got3)
    proj_got_a, proj_got_b = swap(proj_a, 2), swap(proj_b, 6)
    (gf,) = back(1, gf, 1, after(gml, proj_a))
    got1 = swap(dw[1], 1)
    feed_got_a, feed_got_b = swap(far_a, 2), swap(far_b, 6)
    gf, before, behind = back(2, gf, 0, after(gml, feed_got_a, feed_got_b))
    from_low = lax.ppermute(behind, AXES, [(n, n + 1) for n in range(devices - 1)])
    from_high = lax.ppermute(before, AXES, [(n + 1, n) for n in range(devices - 1)])

    (parts,) = small(
        join_kernel, "join", [(16, 96, D)],
        near, feed_got_a, feed_got_b, dw[0], got1, proj_got_a, proj_got_b,
    )
    got = exchange(after(parts, from_low, from_high))
    grad_frames = run_last(gf, from_low, from_high, ext, first_gain, grad_middle)
    (summed,) = small(sum_kernel, "sum", [(96, D)], after(got, grad_frames))
    (spread,) = small(spread_kernel, "spread", [(16, 96, D)], summed, swap(summed, 4))
    total = exchange(spread)
    grads = small(
        functools.partial(end_kernel, scale), "end", [(D, GC)] * 3 + [(GC, D), (D, D), (D, D)],
        total, final=True,
    )
    return (grad_frames, *grads)


def solution(mesh):
    in_specs = (
        P("tm", None),
        P("tm", None),
        P(),
        P(),
        P(None, "ffn"),
        P(None, "ffn"),
        P(None, "ffn"),
        P("ffn", None),
        P(),
        P(None, "ffn"),
        P("ffn", None),
    )
    out_specs = (
        P(("tm", "ffn"), None),
        P(None, "ffn"),
        P(None, "ffn"),
        P(None, "ffn"),
        P("ffn", None),
        P(None, "ffn"),
        P("ffn", None),
    )
    return jax.shard_map(local, mesh=mesh, in_specs=in_specs, out_specs=out_specs, check_vma=False)
```

```python
import functools
import math

import jax
import jax.numpy as jnp
from jax import lax
from jax.experimental import pallas as pl
from jax.experimental.pallas import tpu as pltpu
from jax.sharding import PartitionSpec as P

HEAD_DIM = 64
HALF = 256
ROWS = 512
EXT = ROWS + 2 * HALF
QB = 128
WIN = QB + 2 * HALF
BLOCKS = ROWS // QB
GC = 128
D = 512
epsilon = 1e-05
masked_score = -1e30
BF = jnp.bfloat16
F32 = jnp.float32
AXES = ("tm", "ffn")
VMEM = pltpu.VMEM
WHOLE = pl.BlockSpec(memory_space=pltpu.VMEM)


def dot(a, b):
    return jnp.dot(a, b, preferred_element_type=F32)


def dot_nt(a, b):
    return lax.dot_general(a, b, (((1,), (1,)), ((), ())), preferred_element_type=F32)


def params(mib=16):
    return pltpu.CompilerParams(vmem_limit_bytes=mib * 1024 * 1024)


def cost(flops, nbytes, trans=0):
    return pl.CostEstimate(
        flops=int(flops / 8), bytes_accessed=int(nbytes / 8), transcendentals=int(trans / 8)
    )


def norm_rows(x):
    center = jnp.mean(x, axis=-1, keepdims=True)
    shifted = x - center
    inverse = lax.rsqrt(jnp.mean(shifted * shifted, axis=-1, keepdims=True) + epsilon)
    return shifted * inverse, inverse


def norm_back(grad_normed, scaled, inverse, gain):
    weighted = grad_normed * gain
    first = jnp.mean(weighted, axis=-1, keepdims=True)
    second = jnp.mean(weighted * scaled, axis=-1, keepdims=True)
    return inverse * (weighted - first - scaled * second)


def norm_kernel(i_ref, ext_ref, halo_ref, gain_ref, col_ref, row_ref, n_ref, nt_ref, bias_ref):
    step = pl.program_id(0)
    outside = ((i_ref[0] == 0) & (step == 0)) | ((i_ref[0] == 3) & (step == 3))
    x = jnp.where(outside, halo_ref[...].astype(F32), ext_ref[...].astype(F32))
    scaled, _ = norm_rows(x)
    normed = scaled * gain_ref[...]
    n_ref[...] = normed.astype(BF)
    nt_ref[...] = normed.T.astype(BF)
    keys = col_ref[pl.ds(pl.multiple_of(step * QB, QB), WIN), :]
    offset = lax.broadcasted_iota(jnp.int32, (WIN, QB), 0) - lax.broadcasted_iota(
        jnp.int32, (WIN, QB), 1
    )
    band = (offset >= 0) & (offset < 2 * HALF)
    bias_ref[0] = jnp.where(band & (keys == row_ref[0]), 0.0, masked_score)


def run_norm(ext, halo, gain, rec_col, rec_row, index):
    spec = pltpu.PrefetchScalarGridSpec(
        num_scalar_prefetch=1,
        grid=(4,),
        in_specs=[
            pl.BlockSpec((HALF, D), lambda j, i: (j, 0)),
            pl.BlockSpec((HALF, D), lambda j, i: (0, 0)),
            pl.BlockSpec((1, D), lambda j, i: (0, 0)),
            pl.BlockSpec((EXT, 1), lambda j, i: (0, 0)),
            pl.BlockSpec((1, 1, QB), lambda j, i: (j, 0, 0)),
        ],
        out_specs=[
            pl.BlockSpec((HALF, D), lambda j, i: (j, 0)),
            pl.BlockSpec((D, HALF), lambda j, i: (0, j)),
            pl.BlockSpec((1, WIN, QB), lambda j, i: (j, 0, 0)),
        ],
    )
    return pl.pallas_call(
        norm_kernel,
        grid_spec=spec,
        out_shape=[
            jax.ShapeDtypeStruct((EXT, D), BF),
            jax.ShapeDtypeStruct((D, EXT), BF),
            jax.ShapeDtypeStruct((BLOCKS, WIN, QB), F32),
        ],
        compiler_params=params(),
        cost_estimate=cost(EXT * D * 12, 5e6),
        name="norm_first",
    )(index.reshape(1), ext, halo, gain.reshape(1, D), rec_col, rec_row)


def wide(vo_ref):
    return jnp.concatenate([vo_ref[D + j * GC : D + (j + 1) * GC] for j in range(4)], axis=1)


def square(one_ref, two_ref):
    tiles = [one_ref[2 * D : 3 * D], one_ref[3 * D :], two_ref[:D], two_ref[D:]]
    return jnp.concatenate(tiles, axis=1)


def stack_heads(block):
    lane = lax.broadcasted_iota(jnp.int32, block.shape, 1)
    zero = jnp.zeros_like(block)
    low = jnp.where(lane < HEAD_DIM, block, zero)
    high = jnp.where(lane < HEAD_DIM, zero, block)
    return jnp.concatenate([low, high], axis=0)


def pick_heads(both):
    return jnp.concatenate([both[:HEAD_DIM, :QB], both[HEAD_DIM:, QB:]], axis=0).T


def context_kernel(n_ref, qk_ref, vo_ref, bias_ref, q_ref, k_ref, v_ref, ctx_ref, lse_ref, vt_ref):
    n = n_ref[...]
    q_ref[...] = dot(n_ref[HALF : HALF + ROWS], qk_ref[:D]).astype(BF) * 0.125
    k_ref[...] = dot(n, qk_ref[D : 2 * D]).astype(BF)
    v = dot(n, vo_ref[:D])
    v_ref[...] = v.astype(BF)
    vt_ref[...] = v.T.astype(BF)
    for b in range(BLOCKS):
        win = slice(b * QB, b * QB + WIN)
        rows = slice(b * QB, b * QB + QB)
        queries = stack_heads(q_ref[rows])
        bias = bias_ref[b]
        scores = dot_nt(k_ref[win], queries) + jnp.concatenate([bias, bias], axis=1)
        peak = jnp.max(scores, axis=0, keepdims=True)
        weights = jnp.exp(scores - peak)
        total = jnp.sum(weights, axis=0, keepdims=True)
        both = dot(vt_ref[:, win], weights.astype(BF)) / total
        ctx_ref[rows] = pick_heads(both).astype(BF)
        lse_ref[b] = peak + jnp.log(total)


def run_context(normed, qk, vo, bias):
    return pl.pallas_call(
        context_kernel,
        in_specs=[WHOLE] * 4,
        out_specs=[WHOLE] * 5,
        out_shape=[
            jax.ShapeDtypeStruct((ROWS, GC), BF),
            jax.ShapeDtypeStruct((EXT, GC), BF),
            jax.ShapeDtypeStruct((EXT, GC), BF),
            jax.ShapeDtypeStruct((ROWS, GC), BF),
            jax.ShapeDtypeStruct((BLOCKS, 1, 2 * QB), F32),
        ],
        scratch_shapes=[VMEM((GC, EXT), BF)],
        compiler_params=params(),
        cost_estimate=cost(2e9, 4e6, BLOCKS * WIN * 2 * QB),
        name="context",
    )(normed, qk, vo, bias)


def attention_back_kernel(place, *refs):
    gml_ref, qk_ref, vo_ref, ctx_ref, q_ref, k_ref, v_ref, lse_ref, bias_ref, nt_ref = refs[:10]
    refs = refs[10:]
    if place > 0:
        gf_in_ref, refs = refs[0], refs[1:]
    dw_ref, gf_ref, refs = refs[0], refs[1], refs[2:]
    if place == 2:
        before_ref, behind_ref, refs = refs[0], refs[1], refs[2:]
    g_ref, kt_ref, dq_ref, dka_ref, dva_ref, dk_ref, dv_ref = refs
    g_ref[...] = dot_nt(gml_ref[...], wide(vo_ref)).astype(BF)
    grad_out = dot(ctx_ref[...].T, gml_ref[...]).astype(BF)
    for j in range(4):
        dw_ref[3 * D + j * GC : 3 * D + (j + 1) * GC] = grad_out[:, j * GC : (j + 1) * GC]
    kt_ref[...] = k_ref[...].T
    dka_ref[...] = jnp.zeros_like(dka_ref)
    dva_ref[...] = jnp.zeros_like(dva_ref)
    for b in range(BLOCKS):
        win = slice(b * QB, b * QB + WIN)
        rows = slice(b * QB, b * QB + QB)
        queries = stack_heads(q_ref[rows])
        grads = stack_heads(g_ref[rows])
        bias = bias_ref[b]
        scores = dot_nt(k_ref[win], queries) + jnp.concatenate([bias, bias], axis=1)
        prob = jnp.exp(scores - lse_ref[b])
        grad_prob = dot_nt(v_ref[win], grads)
        inner = jnp.sum(prob * grad_prob, axis=0, keepdims=True)
        grad_scores = (prob * (grad_prob - inner)).astype(BF)
        dva_ref[win] += dot(prob.astype(BF), grads)
        dka_ref[win] += dot(grad_scores, queries)
        both = dot(kt_ref[:, win], grad_scores)
        dq_ref[rows] = (pick_heads(both) * 0.125).astype(BF)
    dk_ref[...] = dka_ref[...].astype(BF)
    dv_ref[...] = dva_ref[...].astype(BF)
    dw_ref[:D] = dot(nt_ref[:, HALF : HALF + ROWS], dq_ref[...]).astype(BF)
    dw_ref[D : 2 * D] = dot(nt_ref[...], dk_ref[...]).astype(BF)
    dw_ref[2 * D : 3 * D] = dot(nt_ref[...], dv_ref[...]).astype(BF)
    for part in range(4):
        rows = slice(part * HALF, (part + 1) * HALF)
        term = dot_nt(dk_ref[rows], qk_ref[D : 2 * D]) + dot_nt(dv_ref[rows], vo_ref[:D])
        if part in (1, 2):
            own = slice((part - 1) * HALF, part * HALF)
            term = term + dot_nt(dq_ref[own], qk_ref[:D])
        if place > 0:
            term = term + gf_in_ref[rows]
        if place < 2:
            gf_ref[rows] = term
        elif part == 0:
            before_ref[...] = term.astype(BF)
        elif part == 3:
            behind_ref[...] = term.astype(BF)
        else:
            gf_ref[own] = term


def run_attention_back(place, gf, *arrays):
    gf_shape = jax.ShapeDtypeStruct((ROWS if place == 2 else EXT, D), F32)
    edges = [jax.ShapeDtypeStruct((HALF, D), BF)] * 2 if place == 2 else []
    if place > 0:
        arrays = arrays + (gf,)
    return pl.pallas_call(
        functools.partial(attention_back_kernel, place),
        in_specs=[WHOLE] * len(arrays),
        out_specs=[WHOLE] * (2 + len(edges)),
        out_shape=[jax.ShapeDtypeStruct((4 * D, GC), BF), gf_shape] + edges,
        scratch_shapes=[
            VMEM((ROWS, GC), BF),
            VMEM((GC, EXT), BF),
            VMEM((ROWS, GC), BF),
            VMEM((EXT, GC), F32),
            VMEM((EXT, GC), F32),
            VMEM((EXT, GC), BF),
            VMEM((EXT, GC), BF),
        ],
        compiler_params=params(),
        cost_estimate=cost(4e9, 6e6, BLOCKS * WIN * 2 * QB),
        name="attention_back",
    )(*arrays)


def feed_group(n2_ref, n2t_ref, up_ref, upt_ref, low, high, to_ref):
    inner = square(*low)
    pre = dot(n2_ref[...], inner)
    grad_act = dot_nt(up_ref[...], square(*high)) * 0.5
    gate = jax.nn.sigmoid(pre)
    act = (pre * gate).astype(BF)
    grad_inner = (grad_act * gate * (1.0 + pre * (1.0 - gate))).astype(BF)
    to_ref[:D] = dot(n2t_ref[...], grad_inner).astype(BF)
    to_ref[D:] = (dot(upt_ref[...], act) * 0.5).astype(BF)
    return dot_nt(grad_inner, inner)


def feed_near_kernel(*refs):
    ext_ref, up_ref, gain_ref = refs[:3]
    ctx, high, low, high_two, low_two = refs[3:7], refs[7:11], refs[11:13], refs[13:15], refs[15:17]
    give_ref, keep_ref, sc_ref, inv_ref, n2_ref, n2t_ref, upt_ref, gs_ref = refs[17:]
    middle = ext_ref[HALF : HALF + ROWS].astype(F32)
    for k in range(4):
        middle = middle + dot(ctx[k][...], wide(high[k]))
    scaled, inverse = norm_rows(middle)
    sc_ref[...] = scaled
    inv_ref[...] = inverse
    normed = scaled * gain_ref[...]
    n2_ref[...] = normed.astype(BF)
    n2t_ref[...] = normed.T.astype(BF)
    upt_ref[...] = up_ref[...].T
    shared = (n2_ref, n2t_ref, up_ref, upt_ref)
    gs_ref[...] = feed_group(*shared, (low[1], low_two[1]), (high[1], high_two[1]), give_ref)
    gs_ref[...] += feed_group(*shared, (low[0], low_two[0]), (high[0], high_two[0]), keep_ref)


def run_feed_near(ext, up, gain, ctx, high, low, high_two, low_two):
    return pl.pallas_call(
        feed_near_kernel,
        in_specs=[WHOLE] * 17,
        out_specs=[WHOLE] * 8,
        out_shape=[
            jax.ShapeDtypeStruct((2 * D, D), BF),
            jax.ShapeDtypeStruct((2 * D, D), BF),
            jax.ShapeDtypeStruct((ROWS, D), F32),
            jax.ShapeDtypeStruct((ROWS, 1), F32),
            jax.ShapeDtypeStruct((ROWS, D), BF),
            jax.ShapeDtypeStruct((D, ROWS), BF),
            jax.ShapeDtypeStruct((D, ROWS), BF),
            jax.ShapeDtypeStruct((ROWS, D), F32),
        ],
        compiler_params=params(),
        cost_estimate=cost(4e9, 14e6, ROWS * 1024),
        name="feed_near",
    )(ext, up, gain.reshape(1, D), *ctx, *high, *low, *high_two, *low_two)


def feed_far_kernel(*refs):
    up_ref, gain_ref, sc_ref, inv_ref, n2_ref, n2t_ref, upt_ref, gs_in_ref = refs[:8]
    low, high, low_two, high_two = refs[8:10], refs[10:12], refs[12:14], refs[14:16]
    gm_ref, gml_ref, give_ref, keep_ref, gs_ref = refs[16:]
    shared = (n2_ref, n2t_ref, up_ref, upt_ref)
    gs_ref[...] = gs_in_ref[...] + feed_group(*shared, (low[1], low_two[1]), (high[1], high_two[1]), give_ref)
    gs_ref[...] += feed_group(*shared, (low[0], low_two[0]), (high[0], high_two[0]), keep_ref)
    grad_middle = up_ref[...].astype(F32) + norm_back(
        gs_ref[...], sc_ref[...], inv_ref[...], gain_ref[...]
    )
    gm_ref[...] = grad_middle
    gml_ref[...] = grad_middle.astype(BF)


def run_feed_far(up, gain, held, low, high, low_two, high_two):
    return pl.pallas_call(
        feed_far_kernel,
        in_specs=[WHOLE] * 16,
        out_specs=[WHOLE] * 4,
        out_shape=[
            jax.ShapeDtypeStruct((ROWS, D), F32),
            jax.ShapeDtypeStruct((ROWS, D), BF),
            jax.ShapeDtypeStruct((2 * D, D), BF),
            jax.ShapeDtypeStruct((2 * D, D), BF),
        ],
        scratch_shapes=[VMEM((ROWS, D), F32)],
        compiler_params=params(),
        cost_estimate=cost(4e9, 14e6, ROWS * 1024),
        name="feed_far",
    )(up, gain.reshape(1, D), *held, *low, *high, *low_two, *high_two)


def last_kernel(gf_ref, low_ref, high_ref, own_ref, gain_ref, gm_ref, out_ref):
    scaled, inverse = norm_rows(own_ref[HALF : HALF + ROWS].astype(F32))
    grad = gf_ref[...] + jnp.concatenate(
        [low_ref[...].astype(F32), high_ref[...].astype(F32)], axis=0
    )
    out_ref[...] = gm_ref[...] + norm_back(grad, scaled, inverse, gain_ref[...])


def run_last(gf, low, high, own, gain, gm):
    return pl.pallas_call(
        last_kernel,
        in_specs=[WHOLE] * 6,
        out_shape=jax.ShapeDtypeStruct((ROWS, D), F32),
        compiler_params=params(),
        cost_estimate=cost(ROWS * D * 20, 5e6),
        name="frames_grad",
    )(gf, low, high, own, gain.reshape(1, D), gm)


def edge_kernel(i_ref, frames_ref, edge_ref, sem):
    start = pl.multiple_of(jnp.where(i_ref[0] == 3, 3 * ROWS + HALF, 0), HALF)
    copy = pltpu.make_async_copy(frames_ref.at[pl.ds(start, HALF)], edge_ref, sem)
    copy.start()
    copy.wait()


def run_edge(frames, index):
    return pl.pallas_call(
        edge_kernel,
        in_specs=[
            pl.BlockSpec(memory_space=pltpu.SMEM),
            pl.BlockSpec(memory_space=pltpu.HBM),
        ],
        out_specs=WHOLE,
        out_shape=jax.ShapeDtypeStruct((HALF, D), BF),
        scratch_shapes=[pltpu.SemaphoreType.DMA],
        compiler_params=params(58),
        cost_estimate=cost(1e5, 1e6),
        name="edge",
    )(index.reshape(1), frames)


def pack_kernel(i_ref, frames_ref, up_in_ref, q_ref, k_ref, v_ref, o_ref, inner_ref, outer_ref,
                low_ref, high_ref, low_two_ref, high_two_ref, ext_ref, up_ref, sems):
    i = i_ref[0]

    def at(start, size):
        return pl.ds(pl.multiple_of(start, HALF), size)

    moves = [
        (q_ref, low_ref.at[pl.ds(0, D)]),
        (k_ref, low_ref.at[pl.ds(D, D)]),
        (v_ref, high_ref.at[pl.ds(0, D)]),
        (frames_ref.at[at(jnp.maximum(i * ROWS - HALF, 0), HALF)], ext_ref.at[pl.ds(0, HALF)]),
        (frames_ref.at[at(i * ROWS, ROWS)], ext_ref.at[pl.ds(HALF, ROWS)]),
        (
            frames_ref.at[at(jnp.minimum(i * ROWS + ROWS, 3 * ROWS + HALF), HALF)],
            ext_ref.at[pl.ds(HALF + ROWS, HALF)],
        ),
        (up_in_ref.at[at(i * ROWS, ROWS)], up_ref),
    ]
    for j in range(4):
        cols = pl.ds(j * GC, GC)
        moves.append((o_ref.at[:, cols], high_ref.at[pl.ds(D + j * GC, GC)]))
        low, high = (low_ref, high_ref) if j < 2 else (low_two_ref, high_two_ref)
        place = pl.ds(((2 + j) if j < 2 else (j - 2)) * D, D)
        moves.append((inner_ref.at[:, cols], low.at[place]))
        moves.append((outer_ref.at[:, cols], high.at[place]))
    copies = [
        pltpu.make_async_copy(source, target, sems.at[n])
        for n, (source, target) in enumerate(moves)
    ]
    for copy in copies:
        copy.start()
    for copy in copies:
        copy.wait()


def run_pack(frames, upstream, wq, wk, wv, wo, wi, wu, index):
    anywhere = pl.BlockSpec(memory_space=pltpu.HBM)
    shapes = [(4 * D, GC)] * 2 + [(2 * D, GC)] * 2 + [(EXT, D), (ROWS, D)]
    return pl.pallas_call(
        pack_kernel,
        in_specs=[pl.BlockSpec(memory_space=pltpu.SMEM)] + [anywhere] * 8,
        out_specs=[WHOLE] * 6,
        out_shape=[jax.ShapeDtypeStruct(shape, BF) for shape in shapes],
        scratch_shapes=[pltpu.SemaphoreType.DMA((19,))],
        compiler_params=params(58),
        cost_estimate=cost(1e5, 3e6),
        name="pack",
    )(index.reshape(1), frames, upstream, wq, wk, wv, wo, wi, wu)


def add(*terms):
    total = terms[0].astype(F32)
    for term in terms[1:]:
        total = total + term.astype(F32)
    return total.astype(BF)


def feed_split_kernel(near_ref, got_near_ref, far_ref, got_far_ref, out_ref, a_ref, b_ref):
    out_ref[...] = add(near_ref[...], got_near_ref[...])
    a_ref[...] = add(far_ref[:D], got_far_ref[:D])
    b_ref[...] = add(far_ref[D:], got_far_ref[D:])


def proj_split_kernel(keep_ref, got_ref, a_ref, b_ref):
    h = 2 * D
    a_ref[...] = add(keep_ref[:h], got_ref[:h])
    b_ref[...] = add(keep_ref[h:], got_ref[h:])


def join_kernel(near_ref, a_ref, b_ref, keep_ref, got_ref, pa_ref, pb_ref, out_ref):
    for n in range(16):
        feed, proj = (a_ref, pa_ref) if n < 8 else (b_ref, pb_ref)
        rows, part = slice(n * 64, (n + 1) * 64), slice(n % 8 * 64, (n % 8 + 1) * 64)
        out_ref[n, :64] = add(near_ref[rows], feed[part])
        for j in range(4):
            rows = slice(n * GC + j * 32, n * GC + (j + 1) * 32)
            part = slice(n % 8 * GC + j * 32, n % 8 * GC + (j + 1) * 32)
            out_ref[n, 64:, j * GC : (j + 1) * GC] = add(keep_ref[rows], got_ref[rows], proj[part])


def sum_kernel(parts_ref, out_ref):
    out_ref[...] = add(*[parts_ref[n] for n in range(16)])


def spread_kernel(mine_ref, got_ref, out_ref):
    total = add(mine_ref[...], got_ref[...])
    for n in range(16):
        out_ref[n] = total


def end_kernel(scale, total_ref, q_ref, k_ref, v_ref, o_ref, inner_ref, outer_ref):
    for n in range(8):
        inner_ref[n * 64 : (n + 1) * 64] = total_ref[n, :64].astype(F32) * scale
    outer = jnp.concatenate([total_ref[8 + n, :64] for n in range(8)], axis=0)
    outer_ref[...] = outer.astype(F32).T * scale
    for n in range(16):
        for j in range(4):
            block = total_ref[n, 64:, j * GC : (j + 1) * GC].astype(F32) * scale
            if n < 12:
                start = n % 4 * GC + j * 32
                (q_ref, k_ref, v_ref)[n // 4][start : start + 32] = block
            else:
                o_ref[j * 32 : (j + 1) * 32, (n - 12) * GC : (n - 11) * GC] = block


def small(kernel, name, shapes, *arrays, final=False):
    outs = [jax.ShapeDtypeStruct(shape, F32 if final else BF) for shape in shapes]
    extra = {} if final else {"out_specs": [WHOLE] * len(outs)}
    return pl.pallas_call(
        kernel,
        in_specs=[WHOLE] * len(arrays),
        out_shape=outs,
        compiler_params=params(),
        cost_estimate=cost(1e6, 2e6),
        name=name,
        **extra,
    )(*arrays)


def swap(array, bits):
    return lax.ppermute(array, AXES, [(n, n ^ bits) for n in range(128)])


def after(first, *later):
    return lax.optimization_barrier((first,) + later)[0]


PEERS = [[2 * n + half for n in range(16)] for half in range(2)]


def exchange(parts):
    return lax.all_to_all(parts, "tm", 0, 0, axis_index_groups=PEERS, tiled=True)


def local(
    frames,
    upstream,
    recording,
    first_gain,
    query_weight,
    key_weight,
    value_weight,
    out_weight,
    second_gain,
    inner_weight,
    outer_weight,
):
    t = lax.axis_index("tm")
    i = lax.axis_index("ffn")
    slab = frames.shape[0]
    devices = lax.axis_size("tm") * 4
    scale = 1.0 / math.sqrt(recording.shape[0])

    record_pad = jnp.pad(recording, (HALF, HALF), constant_values=-1)
    rec_ext = lax.dynamic_slice_in_dim(record_pad, t * slab + i * ROWS, EXT)
    rec_col = rec_ext.reshape(EXT, 1)
    rec_row = rec_ext[HALF : HALF + ROWS].reshape(BLOCKS, 1, QB)
    rec_col, rec_row, index = lax.optimization_barrier((rec_col, rec_row, i))
    edge = run_edge(frames, index)
    low_own, high_own, low_own2, high_own2, ext, up = run_pack(
        frames, upstream, query_weight, key_weight, value_weight, out_weight,
        inner_weight, outer_weight, after(index, edge),
    )
    pairs = [(4 * n + 3, 4 * n + 4) for n in range(31)] + [(4 * n + 4, 4 * n + 3) for n in range(31)]
    halo = lax.ppermute(edge, AXES, pairs)
    low_far, high_far = swap(after(low_own, halo), 2), swap(after(high_own, halo), 6)
    low_far2, high_far2 = swap(after(low_own2, low_far), 2), swap(after(high_own2, high_far), 6)
    low_near, high_near = swap(low_own, 1), swap(high_own, 1)

    normed, normed_t, bias = run_norm(ext, halo, first_gain, rec_col, rec_row, i)
    qs, ks, vs, ctx, lse = [], [], [], [], []

    def forward(qk, vo):
        q, key, v, c, s = run_context(normed, qk, vo, bias)
        qs.append(q)
        ks.append(key)
        vs.append(v)
        ctx.append(c)
        lse.append(s)

    forward(low_own, high_own)
    forward(low_near, high_near)
    low_far, high_far = after(low_far, *ctx), after(high_far, *ctx)
    low = [low_own, low_near, low_far, swap(low_far, 1)]
    high = [high_own, high_near, high_far, swap(high_far, 1)]
    forward(low[2], high[2])
    forward(low[3], high[3])

    low_near2, high_near2 = swap(after(low_own2, ctx[0]), 1), swap(after(high_own2, ctx[0]), 1)
    give1, keep0, *held = run_feed_near(
        ext, up, second_gain, ctx, high, low[:2], [high_own2, high_near2], [low_own2, low_near2]
    )
    got_near = swap(give1, 1)
    low_far2, high_far2 = after(low_far2, *ctx), after(high_far2, *ctx)
    grad_middle, gml, give3, keep2 = run_feed_far(
        up, second_gain, held, low[2:], high[2:],
        [low_far2, swap(low_far2, 1)], [high_far2, swap(high_far2, 1)],
    )
    got_far = swap(give3, 1)
    near, far_a, far_b = small(
        feed_split_kernel, "feed_split", [(2 * D, D), (D, D), (D, D)],
        keep0, got_near, keep2, got_far,
    )

    dw = [None] * 4

    def back(place, gf, k, grads):
        dw[k], *rest = run_attention_back(
            place, gf, grads, low[k], high[k], ctx[k], qs[k], ks[k], vs[k], lse[k], bias, normed_t
        )
        return rest

    (gf,) = back(0, None, 3, gml)
    got3 = swap(dw[3], 1)
    (gf,) = back(1, gf, 2, after(gml, near, gf))
    proj_a, proj_b = small(proj_split_kernel, "proj_split", [(2 * D, GC)] * 2, dw[2], got3)
    proj_got_a, proj_got_b = swap(proj_a, 2), swap(proj_b, 6)
    (gf,) = back(1, gf, 1, after(gml, proj_a))
    got1 = swap(dw[1], 1)
    feed_got_a, feed_got_b = swap(far_a, 2), swap(far_b, 6)
    gf, before, behind = back(2, gf, 0, after(gml, feed_got_a, feed_got_b))
    from_low = lax.ppermute(behind, AXES, [(n, n + 1) for n in range(devices - 1)])
    from_high = lax.ppermute(before, AXES, [(n + 1, n) for n in range(devices - 1)])

    (parts,) = small(
        join_kernel, "join", [(16, 96, D)],
        near, feed_got_a, feed_got_b, dw[0], got1, proj_got_a, proj_got_b,
    )
    got = exchange(parts)
    grad_frames = run_last(gf, from_low, from_high, ext, first_gain, grad_middle)
    (summed,) = small(sum_kernel, "sum", [(96, D)], got)
    other = swap(summed, 4)
    (spread,) = small(
        spread_kernel, "spread", [(16, 96, D)], after(summed, from_low, from_high), other
    )
    total = exchange(spread)
    grads = small(
        functools.partial(end_kernel, scale), "end", [(D, GC)] * 3 + [(GC, D), (D, D), (D, D)],
        after(total, grad_frames), final=True,
    )
    return (grad_frames, *grads)


def solution(mesh):
    in_specs = (
        P("tm", None),
        P("tm", None),
        P(),
        P(),
        P(None, "ffn"),
        P(None, "ffn"),
        P(None, "ffn"),
        P("ffn", None),
        P(),
        P(None, "ffn"),
        P("ffn", None),
    )
    out_specs = (
        P(("tm", "ffn"), None),
        P(None, "ffn"),
        P(None, "ffn"),
        P(None, "ffn"),
        P("ffn", None),
        P(None, "ffn"),
        P("ffn", None),
    )
    return jax.shard_map(local, mesh=mesh, in_specs=in_specs, out_specs=out_specs, check_vma=False)
```

```python
import functools
import math

import jax
import jax.numpy as jnp
from jax import lax
from jax.experimental import pallas as pl
from jax.experimental.pallas import tpu as pltpu
from jax.sharding import PartitionSpec as P

HEAD_DIM = 64
HALF = 256
ROWS = 512
EXT = ROWS + 2 * HALF
QB = 128
WIN = QB + 2 * HALF
BLOCKS = ROWS // QB
GC = 128
D = 512
epsilon = 1e-05
masked_score = -1e30
BF = jnp.bfloat16
F32 = jnp.float32
AXES = ("tm", "ffn")
VMEM = pltpu.VMEM
WHOLE = pl.BlockSpec(memory_space=pltpu.VMEM)


def dot(a, b):
    return jnp.dot(a, b, preferred_element_type=F32)


def dot_nt(a, b):
    return lax.dot_general(a, b, (((1,), (1,)), ((), ())), preferred_element_type=F32)


def params(mib=16):
    return pltpu.CompilerParams(vmem_limit_bytes=mib * 1024 * 1024)


def cost(flops, nbytes, trans=0):
    return pl.CostEstimate(
        flops=int(flops / 8), bytes_accessed=int(nbytes / 8), transcendentals=int(trans / 8)
    )


def norm_rows(x):
    center = jnp.mean(x, axis=-1, keepdims=True)
    shifted = x - center
    inverse = lax.rsqrt(jnp.mean(shifted * shifted, axis=-1, keepdims=True) + epsilon)
    return shifted * inverse, inverse


def norm_back(grad_normed, scaled, inverse, gain):
    weighted = grad_normed * gain
    first = jnp.mean(weighted, axis=-1, keepdims=True)
    second = jnp.mean(weighted * scaled, axis=-1, keepdims=True)
    return inverse * (weighted - first - scaled * second)


def norm_kernel(i_ref, ext_ref, halo_ref, gain_ref, col_ref, row_ref, n_ref, nt_ref, bias_ref):
    step = pl.program_id(0)
    outside = ((i_ref[0] == 0) & (step == 0)) | ((i_ref[0] == 3) & (step == 3))
    x = jnp.where(outside, halo_ref[...].astype(F32), ext_ref[...].astype(F32))
    scaled, _ = norm_rows(x)
    normed = scaled * gain_ref[...]
    n_ref[...] = normed.astype(BF)
    nt_ref[...] = normed.T.astype(BF)
    keys = col_ref[pl.ds(pl.multiple_of(step * QB, QB), WIN), :]
    offset = lax.broadcasted_iota(jnp.int32, (WIN, QB), 0) - lax.broadcasted_iota(
        jnp.int32, (WIN, QB), 1
    )
    band = (offset >= 0) & (offset < 2 * HALF)
    bias_ref[0] = jnp.where(band & (keys == row_ref[0]), 0.0, masked_score)


def run_norm(ext, halo, gain, rec_col, rec_row, index):
    spec = pltpu.PrefetchScalarGridSpec(
        num_scalar_prefetch=1,
        grid=(4,),
        in_specs=[
            pl.BlockSpec((HALF, D), lambda j, i: (j, 0)),
            pl.BlockSpec((HALF, D), lambda j, i: (0, 0)),
            pl.BlockSpec((1, D), lambda j, i: (0, 0)),
            pl.BlockSpec((EXT, 1), lambda j, i: (0, 0)),
            pl.BlockSpec((1, 1, QB), lambda j, i: (j, 0, 0)),
        ],
        out_specs=[
            pl.BlockSpec((HALF, D), lambda j, i: (j, 0)),
            pl.BlockSpec((D, HALF), lambda j, i: (0, j)),
            pl.BlockSpec((1, WIN, QB), lambda j, i: (j, 0, 0)),
        ],
    )
    return pl.pallas_call(
        norm_kernel,
        grid_spec=spec,
        out_shape=[
            jax.ShapeDtypeStruct((EXT, D), BF),
            jax.ShapeDtypeStruct((D, EXT), BF),
            jax.ShapeDtypeStruct((BLOCKS, WIN, QB), F32),
        ],
        compiler_params=params(),
        cost_estimate=cost(EXT * D * 12, 5e6),
        name="norm_first",
    )(index.reshape(1), ext, halo, gain.reshape(1, D), rec_col, rec_row)


def wide(vo_ref):
    return jnp.concatenate([vo_ref[D + j * GC : D + (j + 1) * GC] for j in range(4)], axis=1)


def square(packed_ref):
    return jnp.concatenate([packed_ref[j * D : (j + 1) * D] for j in range(4)], axis=1)


def stack_heads(block):
    lane = lax.broadcasted_iota(jnp.int32, block.shape, 1)
    zero = jnp.zeros_like(block)
    low = jnp.where(lane < HEAD_DIM, block, zero)
    high = jnp.where(lane < HEAD_DIM, zero, block)
    return jnp.concatenate([low, high], axis=0)


def pick_heads(both):
    return jnp.concatenate([both[:HEAD_DIM, :QB], both[HEAD_DIM:, QB:]], axis=0).T


def context_kernel(n_ref, qk_ref, vo_ref, bias_ref, q_ref, k_ref, v_ref, ctx_ref, lse_ref, vt_ref):
    n = n_ref[...]
    q_ref[...] = dot(n_ref[HALF : HALF + ROWS], qk_ref[:D]).astype(BF) * 0.125
    k_ref[...] = dot(n, qk_ref[D : 2 * D]).astype(BF)
    v = dot(n, vo_ref[:D])
    v_ref[...] = v.astype(BF)
    vt_ref[...] = v.T.astype(BF)
    for b in range(BLOCKS):
        win = slice(b * QB, b * QB + WIN)
        rows = slice(b * QB, b * QB + QB)
        queries = stack_heads(q_ref[rows])
        bias = bias_ref[b]
        scores = dot_nt(k_ref[win], queries) + jnp.concatenate([bias, bias], axis=1)
        peak = jnp.max(scores, axis=0, keepdims=True)
        weights = jnp.exp(scores - peak)
        total = jnp.sum(weights, axis=0, keepdims=True)
        both = dot(vt_ref[:, win], weights.astype(BF)) / total
        ctx_ref[rows] = pick_heads(both).astype(BF)
        lse_ref[b] = peak + jnp.log(total)


def run_context(normed, qk, vo, bias):
    return pl.pallas_call(
        context_kernel,
        in_specs=[WHOLE] * 4,
        out_specs=[WHOLE] * 5,
        out_shape=[
            jax.ShapeDtypeStruct((ROWS, GC), BF),
            jax.ShapeDtypeStruct((EXT, GC), BF),
            jax.ShapeDtypeStruct((EXT, GC), BF),
            jax.ShapeDtypeStruct((ROWS, GC), BF),
            jax.ShapeDtypeStruct((BLOCKS, 1, 2 * QB), F32),
        ],
        scratch_shapes=[VMEM((GC, EXT), BF)],
        compiler_params=params(),
        cost_estimate=cost(2e9, 4e6, BLOCKS * WIN * 2 * QB),
        name="context",
    )(normed, qk, vo, bias)


def attention_back_kernel(place, *refs):
    gml_ref, qk_ref, vo_ref, ctx_ref, q_ref, k_ref, v_ref, lse_ref, bias_ref, nt_ref = refs[:10]
    refs = refs[10:]
    if place > 0:
        gf_in_ref, refs = refs[0], refs[1:]
    dw_ref, gf_ref, refs = refs[0], refs[1], refs[2:]
    if place == 2:
        before_ref, behind_ref, refs = refs[0], refs[1], refs[2:]
    g_ref, kt_ref, dq_ref, dka_ref, dva_ref, dk_ref, dv_ref = refs
    g_ref[...] = dot_nt(gml_ref[...], wide(vo_ref)).astype(BF)
    grad_out = dot(ctx_ref[...].T, gml_ref[...]).astype(BF)
    for j in range(4):
        dw_ref[3 * D + j * GC : 3 * D + (j + 1) * GC] = grad_out[:, j * GC : (j + 1) * GC]
    kt_ref[...] = k_ref[...].T
    dka_ref[...] = jnp.zeros_like(dka_ref)
    dva_ref[...] = jnp.zeros_like(dva_ref)
    for b in range(BLOCKS):
        win = slice(b * QB, b * QB + WIN)
        rows = slice(b * QB, b * QB + QB)
        queries = stack_heads(q_ref[rows])
        grads = stack_heads(g_ref[rows])
        bias = bias_ref[b]
        scores = dot_nt(k_ref[win], queries) + jnp.concatenate([bias, bias], axis=1)
        prob = jnp.exp(scores - lse_ref[b])
        grad_prob = dot_nt(v_ref[win], grads)
        inner = jnp.sum(prob * grad_prob, axis=0, keepdims=True)
        grad_scores = (prob * (grad_prob - inner)).astype(BF)
        dva_ref[win] += dot(prob.astype(BF), grads)
        dka_ref[win] += dot(grad_scores, queries)
        both = dot(kt_ref[:, win], grad_scores)
        dq_ref[rows] = (pick_heads(both) * 0.125).astype(BF)
    dk_ref[...] = dka_ref[...].astype(BF)
    dv_ref[...] = dva_ref[...].astype(BF)
    dw_ref[:D] = dot(nt_ref[:, HALF : HALF + ROWS], dq_ref[...]).astype(BF)
    dw_ref[D : 2 * D] = dot(nt_ref[...], dk_ref[...]).astype(BF)
    dw_ref[2 * D : 3 * D] = dot(nt_ref[...], dv_ref[...]).astype(BF)
    for part in range(4):
        rows = slice(part * HALF, (part + 1) * HALF)
        term = dot_nt(dk_ref[rows], qk_ref[D : 2 * D]) + dot_nt(dv_ref[rows], vo_ref[:D])
        if part in (1, 2):
            own = slice((part - 1) * HALF, part * HALF)
            term = term + dot_nt(dq_ref[own], qk_ref[:D])
        if place > 0:
            term = term + gf_in_ref[rows]
        if place < 2:
            gf_ref[rows] = term
        elif part == 0:
            before_ref[...] = term.astype(BF)
        elif part == 3:
            behind_ref[...] = term.astype(BF)
        else:
            gf_ref[own] = term


def run_attention_back(place, gf, *arrays):
    gf_shape = jax.ShapeDtypeStruct((ROWS if place == 2 else EXT, D), F32)
    edges = [jax.ShapeDtypeStruct((HALF, D), BF)] * 2 if place == 2 else []
    if place > 0:
        arrays = arrays + (gf,)
    return pl.pallas_call(
        functools.partial(attention_back_kernel, place),
        in_specs=[WHOLE] * len(arrays),
        out_specs=[WHOLE] * (2 + len(edges)),
        out_shape=[jax.ShapeDtypeStruct((4 * D, GC), BF), gf_shape] + edges,
        scratch_shapes=[
            VMEM((ROWS, GC), BF),
            VMEM((GC, EXT), BF),
            VMEM((ROWS, GC), BF),
            VMEM((EXT, GC), F32),
            VMEM((EXT, GC), F32),
            VMEM((EXT, GC), BF),
            VMEM((EXT, GC), BF),
        ],
        compiler_params=params(),
        cost_estimate=cost(4e9, 6e6, BLOCKS * WIN * 2 * QB),
        name="attention_back",
    )(*arrays)


def feed_group(n2_ref, n2t_ref, up_ref, upt_ref, low, high, to_ref):
    inner = square(low)
    pre = dot(n2_ref[...], inner)
    grad_act = dot_nt(up_ref[...], square(high)) * 0.5
    gate = jax.nn.sigmoid(pre)
    act = (pre * gate).astype(BF)
    grad_inner = (grad_act * gate * (1.0 + pre * (1.0 - gate))).astype(BF)
    to_ref[:D] = dot(n2t_ref[...], grad_inner).astype(BF)
    to_ref[D:] = (dot(upt_ref[...], act) * 0.5).astype(BF)
    return dot_nt(grad_inner, inner)


def feed_near_kernel(*refs):
    ext_ref, up_ref, gain_ref = refs[:3]
    ctx, vo, high, low = refs[3:7], refs[7:11], refs[11:13], refs[13:15]
    give_ref, keep_ref, sc_ref, inv_ref, n2_ref, n2t_ref, upt_ref, gs_ref = refs[15:]
    middle = ext_ref[HALF : HALF + ROWS].astype(F32)
    for k in range(4):
        middle = middle + dot(ctx[k][...], wide(vo[k]))
    scaled, inverse = norm_rows(middle)
    sc_ref[...] = scaled
    inv_ref[...] = inverse
    normed = scaled * gain_ref[...]
    n2_ref[...] = normed.astype(BF)
    n2t_ref[...] = normed.T.astype(BF)
    upt_ref[...] = up_ref[...].T
    shared = (n2_ref, n2t_ref, up_ref, upt_ref)
    gs_ref[...] = feed_group(*shared, low[1], high[1], give_ref)
    gs_ref[...] += feed_group(*shared, low[0], high[0], keep_ref)


def run_feed_near(ext, up, gain, ctx, vo, high, low):
    return pl.pallas_call(
        feed_near_kernel,
        in_specs=[WHOLE] * 15,
        out_specs=[WHOLE] * 8,
        out_shape=[
            jax.ShapeDtypeStruct((2 * D, D), BF),
            jax.ShapeDtypeStruct((2 * D, D), BF),
            jax.ShapeDtypeStruct((ROWS, D), F32),
            jax.ShapeDtypeStruct((ROWS, 1), F32),
            jax.ShapeDtypeStruct((ROWS, D), BF),
            jax.ShapeDtypeStruct((D, ROWS), BF),
            jax.ShapeDtypeStruct((D, ROWS), BF),
            jax.ShapeDtypeStruct((ROWS, D), F32),
        ],
        compiler_params=params(),
        cost_estimate=cost(4e9, 14e6, ROWS * 1024),
        name="feed_near",
    )(ext, up, gain.reshape(1, D), *ctx, *vo, *high, *low)


def feed_far_kernel(*refs):
    up_ref, gain_ref, sc_ref, inv_ref, n2_ref, n2t_ref, upt_ref, gs_in_ref = refs[:8]
    low, high = refs[8:10], refs[10:12]
    gm_ref, gml_ref, give_ref, keep_ref, gs_ref = refs[12:]
    shared = (n2_ref, n2t_ref, up_ref, upt_ref)
    gs_ref[...] = gs_in_ref[...] + feed_group(*shared, low[1], high[1], give_ref)
    gs_ref[...] += feed_group(*shared, low[0], high[0], keep_ref)
    grad_middle = up_ref[...].astype(F32) + norm_back(
        gs_ref[...], sc_ref[...], inv_ref[...], gain_ref[...]
    )
    gm_ref[...] = grad_middle
    gml_ref[...] = grad_middle.astype(BF)


def run_feed_far(up, gain, held, low, high):
    return pl.pallas_call(
        feed_far_kernel,
        in_specs=[WHOLE] * 12,
        out_specs=[WHOLE] * 4,
        out_shape=[
            jax.ShapeDtypeStruct((ROWS, D), F32),
            jax.ShapeDtypeStruct((ROWS, D), BF),
            jax.ShapeDtypeStruct((2 * D, D), BF),
            jax.ShapeDtypeStruct((2 * D, D), BF),
        ],
        scratch_shapes=[VMEM((ROWS, D), F32)],
        compiler_params=params(),
        cost_estimate=cost(4e9, 14e6, ROWS * 1024),
        name="feed_far",
    )(up, gain.reshape(1, D), *held, *low, *high)


def last_kernel(gf_ref, low_ref, high_ref, own_ref, gain_ref, gm_ref, out_ref):
    scaled, inverse = norm_rows(own_ref[HALF : HALF + ROWS].astype(F32))
    grad = gf_ref[...] + jnp.concatenate(
        [low_ref[...].astype(F32), high_ref[...].astype(F32)], axis=0
    )
    out_ref[...] = gm_ref[...] + norm_back(grad, scaled, inverse, gain_ref[...])


def run_last(gf, low, high, own, gain, gm):
    return pl.pallas_call(
        last_kernel,
        in_specs=[WHOLE] * 6,
        out_shape=jax.ShapeDtypeStruct((ROWS, D), F32),
        compiler_params=params(),
        cost_estimate=cost(ROWS * D * 20, 5e6),
        name="frames_grad",
    )(gf, low, high, own, gain.reshape(1, D), gm)


def edge_kernel(i_ref, frames_ref, edge_ref, sem):
    start = pl.multiple_of(jnp.where(i_ref[0] == 3, 3 * ROWS + HALF, 0), HALF)
    copy = pltpu.make_async_copy(frames_ref.at[pl.ds(start, HALF)], edge_ref, sem)
    copy.start()
    copy.wait()


def run_edge(frames, index):
    return pl.pallas_call(
        edge_kernel,
        in_specs=[
            pl.BlockSpec(memory_space=pltpu.SMEM),
            pl.BlockSpec(memory_space=pltpu.HBM),
        ],
        out_specs=WHOLE,
        out_shape=jax.ShapeDtypeStruct((HALF, D), BF),
        scratch_shapes=[pltpu.SemaphoreType.DMA],
        compiler_params=params(58),
        cost_estimate=cost(1e5, 1e6),
        name="edge",
    )(index.reshape(1), frames)


def pack_kernel(i_ref, frames_ref, up_in_ref, q_ref, k_ref, v_ref, o_ref, inner_ref, outer_ref,
                low_ref, high_ref, low_two_ref, high_two_ref, ext_ref, up_ref, sems):
    i = i_ref[0]

    def at(start, size):
        return pl.ds(pl.multiple_of(start, HALF), size)

    moves = [
        (q_ref, low_ref.at[pl.ds(0, D)]),
        (k_ref, low_ref.at[pl.ds(D, D)]),
        (v_ref, high_ref.at[pl.ds(0, D)]),
        (frames_ref.at[at(jnp.maximum(i * ROWS - HALF, 0), HALF)], ext_ref.at[pl.ds(0, HALF)]),
        (frames_ref.at[at(i * ROWS, ROWS)], ext_ref.at[pl.ds(HALF, ROWS)]),
        (
            frames_ref.at[at(jnp.minimum(i * ROWS + ROWS, 3 * ROWS + HALF), HALF)],
            ext_ref.at[pl.ds(HALF + ROWS, HALF)],
        ),
        (up_in_ref.at[at(i * ROWS, ROWS)], up_ref),
    ]
    for j in range(4):
        cols = pl.ds(j * GC, GC)
        moves.append((o_ref.at[:, cols], high_ref.at[pl.ds(D + j * GC, GC)]))
        place = pl.ds(j * D, D)
        moves.append((inner_ref.at[:, cols], low_two_ref.at[place]))
        moves.append((outer_ref.at[:, cols], high_two_ref.at[place]))
    copies = [
        pltpu.make_async_copy(source, target, sems.at[n])
        for n, (source, target) in enumerate(moves)
    ]
    for copy in copies:
        copy.start()
    for copy in copies:
        copy.wait()


def run_pack(frames, upstream, wq, wk, wv, wo, wi, wu, index):
    anywhere = pl.BlockSpec(memory_space=pltpu.HBM)
    shapes = [(2 * D, GC)] * 2 + [(4 * D, GC)] * 2 + [(EXT, D), (ROWS, D)]
    return pl.pallas_call(
        pack_kernel,
        in_specs=[pl.BlockSpec(memory_space=pltpu.SMEM)] + [anywhere] * 8,
        out_specs=[WHOLE] * 6,
        out_shape=[jax.ShapeDtypeStruct(shape, BF) for shape in shapes],
        scratch_shapes=[pltpu.SemaphoreType.DMA((19,))],
        compiler_params=params(58),
        cost_estimate=cost(1e5, 3e6),
        name="pack",
    )(index.reshape(1), frames, upstream, wq, wk, wv, wo, wi, wu)


def add(*terms):
    total = terms[0].astype(F32)
    for term in terms[1:]:
        total = total + term.astype(F32)
    return total.astype(BF)


def feed_split_kernel(near_ref, got_near_ref, far_ref, got_far_ref, out_ref, a_ref, b_ref):
    out_ref[...] = add(near_ref[...], got_near_ref[...])
    a_ref[...] = add(far_ref[:D], got_far_ref[:D])
    b_ref[...] = add(far_ref[D:], got_far_ref[D:])


def proj_split_kernel(keep_ref, got_ref, a_ref, b_ref):
    h = 2 * D
    a_ref[...] = add(keep_ref[:h], got_ref[:h])
    b_ref[...] = add(keep_ref[h:], got_ref[h:])


def join_kernel(near_ref, a_ref, b_ref, keep_ref, got_ref, pa_ref, pb_ref, out_ref):
    for n in range(16):
        feed, proj = (a_ref, pa_ref) if n < 8 else (b_ref, pb_ref)
        rows, part = slice(n * 64, (n + 1) * 64), slice(n % 8 * 64, (n % 8 + 1) * 64)
        out_ref[n, :64] = add(near_ref[rows], feed[part])
        for j in range(4):
            rows = slice(n * GC + j * 32, n * GC + (j + 1) * 32)
            part = slice(n % 8 * GC + j * 32, n % 8 * GC + (j + 1) * 32)
            out_ref[n, 64:, j * GC : (j + 1) * GC] = add(keep_ref[rows], got_ref[rows], proj[part])


def sum_kernel(parts_ref, out_ref):
    out_ref[...] = add(*[parts_ref[n] for n in range(16)])


def spread_kernel(mine_ref, got_ref, out_ref):
    total = add(mine_ref[...], got_ref[...])
    for n in range(16):
        out_ref[n] = total


def end_kernel(scale, total_ref, q_ref, k_ref, v_ref, o_ref, inner_ref, outer_ref):
    for n in range(8):
        inner_ref[n * 64 : (n + 1) * 64] = total_ref[n, :64].astype(F32) * scale
    outer = jnp.concatenate([total_ref[8 + n, :64] for n in range(8)], axis=0)
    outer_ref[...] = outer.astype(F32).T * scale
    for n in range(16):
        for j in range(4):
            block = total_ref[n, 64:, j * GC : (j + 1) * GC].astype(F32) * scale
            if n < 12:
                start = n % 4 * GC + j * 32
                (q_ref, k_ref, v_ref)[n // 4][start : start + 32] = block
            else:
                o_ref[j * 32 : (j + 1) * 32, (n - 12) * GC : (n - 11) * GC] = block


def small(kernel, name, shapes, *arrays, final=False, loose=False):
    outs = [jax.ShapeDtypeStruct(shape, F32 if final else BF) for shape in shapes]
    extra = {} if final or loose else {"out_specs": [WHOLE] * len(outs)}
    return pl.pallas_call(
        kernel,
        in_specs=[WHOLE] * len(arrays),
        out_shape=outs,
        compiler_params=params(),
        cost_estimate=cost(1e6, 2e6),
        name=name,
        **extra,
    )(*arrays)


def swap(array, bits):
    return lax.ppermute(array, AXES, [(n, n ^ bits) for n in range(128)])


def after(first, *later):
    return lax.optimization_barrier((first,) + later)[0]


PEERS = [[2 * n + half for n in range(16)] for half in range(2)]


def exchange(parts):
    return lax.all_to_all(parts, "tm", 0, 0, axis_index_groups=PEERS, tiled=True)


def local(
    frames,
    upstream,
    recording,
    first_gain,
    query_weight,
    key_weight,
    value_weight,
    out_weight,
    second_gain,
    inner_weight,
    outer_weight,
):
    t = lax.axis_index("tm")
    i = lax.axis_index("ffn")
    slab = frames.shape[0]
    devices = lax.axis_size("tm") * 4
    scale = 1.0 / math.sqrt(recording.shape[0])

    record_pad = jnp.pad(recording, (HALF, HALF), constant_values=-1)
    rec_ext = lax.dynamic_slice_in_dim(record_pad, t * slab + i * ROWS, EXT)
    rec_col = rec_ext.reshape(EXT, 1)
    rec_row = rec_ext[HALF : HALF + ROWS].reshape(BLOCKS, 1, QB)
    rec_col, rec_row, index = lax.optimization_barrier((rec_col, rec_row, i))
    edge = run_edge(frames, index)
    low_own, high_own, low_own2, high_own2, ext, up = run_pack(
        frames, upstream, query_weight, key_weight, value_weight, out_weight,
        inner_weight, outer_weight, after(index, edge),
    )
    pairs = [(4 * n + 3, 4 * n + 4) for n in range(31)] + [(4 * n + 4, 4 * n + 3) for n in range(31)]
    halo = lax.ppermute(edge, AXES, pairs)
    low_far, high_far = swap(after(low_own, halo), 2), swap(after(high_own, halo), 6)
    low_near, high_near = swap(low_own, 1), swap(high_own, 1)

    normed, normed_t, bias = run_norm(ext, halo, first_gain, rec_col, rec_row, i)
    qs, ks, vs, ctx, lse = [], [], [], [], []

    def forward(qk, vo):
        q, key, v, c, s = run_context(normed, qk, vo, bias)
        qs.append(q)
        ks.append(key)
        vs.append(v)
        ctx.append(c)
        lse.append(s)

    forward(low_own, high_own)
    low_far2, high_far2 = swap(after(low_own2, ctx[0]), 2), swap(after(high_own2, ctx[0]), 6)
    forward(low_near, high_near)
    low_far, high_far = after(low_far, *ctx), after(high_far, *ctx)
    low = [low_own, low_near, low_far, swap(low_far, 1)]
    high = [high_own, high_near, high_far, swap(high_far, 1)]
    forward(low[2], high[2])
    forward(low[3], high[3])

    low_near2, high_near2 = swap(after(low_own2, ctx[0]), 1), swap(after(high_own2, ctx[0]), 1)
    give1, keep0, *held = run_feed_near(
        ext, up, second_gain, ctx, high, [high_own2, high_near2], [low_own2, low_near2]
    )
    got_near = swap(give1, 1)
    low_far2, high_far2 = after(low_far2, give1), after(high_far2, give1)
    grad_middle, gml, give3, keep2 = run_feed_far(
        up, second_gain, held, [low_far2, swap(low_far2, 1)], [high_far2, swap(high_far2, 1)],
    )
    got_far = swap(give3, 1)
    near, far_a, far_b = small(
        feed_split_kernel, "feed_split", [(2 * D, D), (D, D), (D, D)],
        keep0, got_near, keep2, got_far,
    )

    dw = [None] * 4

    def back(place, gf, k, grads):
        dw[k], *rest = run_attention_back(
            place, gf, grads, low[k], high[k], ctx[k], qs[k], ks[k], vs[k], lse[k], bias, normed_t
        )
        return rest

    (gf,) = back(0, None, 3, gml)
    got3 = swap(dw[3], 1)
    (gf,) = back(1, gf, 2, after(gml, near, gf))
    proj_a, proj_b = small(proj_split_kernel, "proj_split", [(2 * D, GC)] * 2, dw[2], got3)
    proj_got_a, proj_got_b = swap(proj_a, 2), swap(proj_b, 6)
    (gf,) = back(1, gf, 1, after(gml, proj_a))
    got1 = swap(dw[1], 1)
    feed_got_a, feed_got_b = swap(far_a, 2), swap(far_b, 6)
    gf, before, behind = back(2, gf, 0, after(gml, feed_got_a, feed_got_b))
    from_low = lax.ppermute(behind, AXES, [(n, n + 1) for n in range(devices - 1)])
    from_high = lax.ppermute(before, AXES, [(n + 1, n) for n in range(devices - 1)])

    (parts,) = small(
        join_kernel, "join", [(16, 96, D)],
        near, feed_got_a, feed_got_b, dw[0], got1, proj_got_a, proj_got_b, loose=True,
    )
    got = exchange(parts)
    grad_frames = run_last(gf, from_low, from_high, ext, first_gain, grad_middle)
    (summed,) = small(sum_kernel, "sum", [(96, D)], got)
    other = swap(summed, 4)
    (spread,) = small(
        spread_kernel, "spread", [(16, 96, D)], after(summed, from_low, from_high), other,
        loose=True,
    )
    total = exchange(spread)
    grads = small(
        functools.partial(end_kernel, scale), "end", [(D, GC)] * 3 + [(GC, D), (D, D), (D, D)],
        after(total, grad_frames), final=True,
    )
    return (grad_frames, *grads)


def solution(mesh):
    in_specs = (
        P("tm", None),
        P("tm", None),
        P(),
        P(),
        P(None, "ffn"),
        P(None, "ffn"),
        P(None, "ffn"),
        P("ffn", None),
        P(),
        P(None, "ffn"),
        P("ffn", None),
    )
    out_specs = (
        P(("tm", "ffn"), None),
        P(None, "ffn"),
        P(None, "ffn"),
        P(None, "ffn"),
        P("ffn", None),
        P(None, "ffn"),
        P("ffn", None),
    )
    return jax.shard_map(local, mesh=mesh, in_specs=in_specs, out_specs=out_specs, check_vma=False)
```

```python
import functools
import math

import jax
import jax.numpy as jnp
from jax import lax
from jax.experimental import pallas as pl
from jax.experimental.pallas import tpu as pltpu
from jax.sharding import PartitionSpec as P

HEAD_DIM = 64
HALF = 256
ROWS = 512
EXT = ROWS + 2 * HALF
QB = 128
WIN = QB + 2 * HALF
BLOCKS = ROWS // QB
GC = 128
D = 512
epsilon = 1e-05
masked_score = -1e30
BF = jnp.bfloat16
F32 = jnp.float32
AXES = ("tm", "ffn")
VMEM = pltpu.VMEM
WHOLE = pl.BlockSpec(memory_space=pltpu.VMEM)


def dot(a, b):
    return jnp.dot(a, b, preferred_element_type=F32)


def dot_nt(a, b):
    return lax.dot_general(a, b, (((1,), (1,)), ((), ())), preferred_element_type=F32)


def params(mib=16):
    return pltpu.CompilerParams(vmem_limit_bytes=mib * 1024 * 1024)


def cost(flops, nbytes, trans=0):
    return pl.CostEstimate(
        flops=int(flops / 8), bytes_accessed=int(nbytes / 8), transcendentals=int(trans / 8)
    )


def norm_rows(x):
    center = jnp.mean(x, axis=-1, keepdims=True)
    shifted = x - center
    inverse = lax.rsqrt(jnp.mean(shifted * shifted, axis=-1, keepdims=True) + epsilon)
    return shifted * inverse, inverse


def norm_back(grad_normed, scaled, inverse, gain):
    weighted = grad_normed * gain
    first = jnp.mean(weighted, axis=-1, keepdims=True)
    second = jnp.mean(weighted * scaled, axis=-1, keepdims=True)
    return inverse * (weighted - first - scaled * second)


def norm_kernel(i_ref, ext_ref, halo_ref, gain_ref, col_ref, row_ref, n_ref, nt_ref, bias_ref):
    step = pl.program_id(0)
    outside = ((i_ref[0] == 0) & (step == 0)) | ((i_ref[0] == 3) & (step == 3))
    x = jnp.where(outside, halo_ref[...].astype(F32), ext_ref[...].astype(F32))
    scaled, _ = norm_rows(x)
    normed = scaled * gain_ref[...]
    n_ref[...] = normed.astype(BF)
    nt_ref[...] = normed.T.astype(BF)
    keys = col_ref[pl.ds(pl.multiple_of(step * QB, QB), WIN), :]
    offset = lax.broadcasted_iota(jnp.int32, (WIN, QB), 0) - lax.broadcasted_iota(
        jnp.int32, (WIN, QB), 1
    )
    band = (offset >= 0) & (offset < 2 * HALF)
    bias_ref[0] = jnp.where(band & (keys == row_ref[0]), 0.0, masked_score)


def run_norm(ext, halo, gain, rec_col, rec_row, index):
    spec = pltpu.PrefetchScalarGridSpec(
        num_scalar_prefetch=1,
        grid=(4,),
        in_specs=[
            pl.BlockSpec((HALF, D), lambda j, i: (j, 0)),
            pl.BlockSpec((HALF, D), lambda j, i: (0, 0)),
            pl.BlockSpec((1, D), lambda j, i: (0, 0)),
            pl.BlockSpec((EXT, 1), lambda j, i: (0, 0)),
            pl.BlockSpec((1, 1, QB), lambda j, i: (j, 0, 0)),
        ],
        out_specs=[
            pl.BlockSpec((HALF, D), lambda j, i: (j, 0)),
            pl.BlockSpec((D, HALF), lambda j, i: (0, j)),
            pl.BlockSpec((1, WIN, QB), lambda j, i: (j, 0, 0)),
        ],
    )
    return pl.pallas_call(
        norm_kernel,
        grid_spec=spec,
        out_shape=[
            jax.ShapeDtypeStruct((EXT, D), BF),
            jax.ShapeDtypeStruct((D, EXT), BF),
            jax.ShapeDtypeStruct((BLOCKS, WIN, QB), F32),
        ],
        compiler_params=params(),
        cost_estimate=cost(EXT * D * 12, 5e6),
        name="norm_first",
    )(index.reshape(1), ext, halo, gain.reshape(1, D), rec_col, rec_row)


def wide(vo_ref):
    return jnp.concatenate([vo_ref[D + j * GC : D + (j + 1) * GC] for j in range(4)], axis=1)


def square(packed_ref):
    return jnp.concatenate([packed_ref[j * D : (j + 1) * D] for j in range(4)], axis=1)


def stack_heads(block):
    lane = lax.broadcasted_iota(jnp.int32, block.shape, 1)
    zero = jnp.zeros_like(block)
    low = jnp.where(lane < HEAD_DIM, block, zero)
    high = jnp.where(lane < HEAD_DIM, zero, block)
    return jnp.concatenate([low, high], axis=0)


def pick_heads(both):
    return jnp.concatenate([both[:HEAD_DIM, :QB], both[HEAD_DIM:, QB:]], axis=0).T


def context_kernel(n_ref, qk_ref, vo_ref, bias_ref, q_ref, k_ref, v_ref, ctx_ref, lse_ref, vt_ref):
    n = n_ref[...]
    q_ref[...] = dot(n_ref[HALF : HALF + ROWS], qk_ref[:D]).astype(BF) * 0.125
    k_ref[...] = dot(n, qk_ref[D : 2 * D]).astype(BF)
    v = dot(n, vo_ref[:D])
    v_ref[...] = v.astype(BF)
    vt_ref[...] = v.T.astype(BF)
    for b in range(BLOCKS):
        win = slice(b * QB, b * QB + WIN)
        rows = slice(b * QB, b * QB + QB)
        queries = stack_heads(q_ref[rows])
        bias = bias_ref[b]
        scores = dot_nt(k_ref[win], queries) + jnp.concatenate([bias, bias], axis=1)
        peak = jnp.max(scores, axis=0, keepdims=True)
        weights = jnp.exp(scores - peak)
        total = jnp.sum(weights, axis=0, keepdims=True)
        both = dot(vt_ref[:, win], weights.astype(BF)) / total
        ctx_ref[rows] = pick_heads(both).astype(BF)
        lse_ref[b] = peak + jnp.log(total)


def run_context(normed, qk, vo, bias):
    return pl.pallas_call(
        context_kernel,
        in_specs=[WHOLE] * 4,
        out_specs=[WHOLE] * 5,
        out_shape=[
            jax.ShapeDtypeStruct((ROWS, GC), BF),
            jax.ShapeDtypeStruct((EXT, GC), BF),
            jax.ShapeDtypeStruct((EXT, GC), BF),
            jax.ShapeDtypeStruct((ROWS, GC), BF),
            jax.ShapeDtypeStruct((BLOCKS, 1, 2 * QB), F32),
        ],
        scratch_shapes=[VMEM((GC, EXT), BF)],
        compiler_params=params(),
        cost_estimate=cost(2e9, 4e6, BLOCKS * WIN * 2 * QB),
        name="context",
    )(normed, qk, vo, bias)


def attention_back_kernel(place, *refs):
    gml_ref, qk_ref, vo_ref, ctx_ref, q_ref, k_ref, v_ref, lse_ref, bias_ref, nt_ref = refs[:10]
    refs = refs[10:]
    if place > 0:
        gf_in_ref, refs = refs[0], refs[1:]
    dw_ref, gf_ref, refs = refs[0], refs[1], refs[2:]
    if place == 2:
        before_ref, behind_ref, refs = refs[0], refs[1], refs[2:]
    g_ref, kt_ref, dq_ref, dka_ref, dva_ref, dk_ref, dv_ref = refs
    g_ref[...] = dot_nt(gml_ref[...], wide(vo_ref)).astype(BF)
    grad_out = dot(ctx_ref[...].T, gml_ref[...]).astype(BF)
    for j in range(4):
        dw_ref[3 * D + j * GC : 3 * D + (j + 1) * GC] = grad_out[:, j * GC : (j + 1) * GC]
    kt_ref[...] = k_ref[...].T
    dka_ref[...] = jnp.zeros_like(dka_ref)
    dva_ref[...] = jnp.zeros_like(dva_ref)
    for b in range(BLOCKS):
        win = slice(b * QB, b * QB + WIN)
        rows = slice(b * QB, b * QB + QB)
        queries = stack_heads(q_ref[rows])
        grads = stack_heads(g_ref[rows])
        bias = bias_ref[b]
        scores = dot_nt(k_ref[win], queries) + jnp.concatenate([bias, bias], axis=1)
        prob = jnp.exp(scores - lse_ref[b])
        grad_prob = dot_nt(v_ref[win], grads)
        inner = jnp.sum(prob * grad_prob, axis=0, keepdims=True)
        grad_scores = (prob * (grad_prob - inner)).astype(BF)
        dva_ref[win] += dot(prob.astype(BF), grads)
        dka_ref[win] += dot(grad_scores, queries)
        both = dot(kt_ref[:, win], grad_scores)
        dq_ref[rows] = (pick_heads(both) * 0.125).astype(BF)
    dk_ref[...] = dka_ref[...].astype(BF)
    dv_ref[...] = dva_ref[...].astype(BF)
    dw_ref[:D] = dot(nt_ref[:, HALF : HALF + ROWS], dq_ref[...]).astype(BF)
    dw_ref[D : 2 * D] = dot(nt_ref[...], dk_ref[...]).astype(BF)
    dw_ref[2 * D : 3 * D] = dot(nt_ref[...], dv_ref[...]).astype(BF)
    for part in range(4):
        rows = slice(part * HALF, (part + 1) * HALF)
        term = dot_nt(dk_ref[rows], qk_ref[D : 2 * D]) + dot_nt(dv_ref[rows], vo_ref[:D])
        if part in (1, 2):
            own = slice((part - 1) * HALF, part * HALF)
            term = term + dot_nt(dq_ref[own], qk_ref[:D])
        if place > 0:
            term = term + gf_in_ref[rows]
        if place < 2:
            gf_ref[rows] = term
        elif part == 0:
            before_ref[...] = term.astype(BF)
        elif part == 3:
            behind_ref[...] = term.astype(BF)
        else:
            gf_ref[own] = term


def run_attention_back(place, gf, *arrays):
    gf_shape = jax.ShapeDtypeStruct((ROWS if place == 2 else EXT, D), F32)
    edges = [jax.ShapeDtypeStruct((HALF, D), BF)] * 2 if place == 2 else []
    if place > 0:
        arrays = arrays + (gf,)
    return pl.pallas_call(
        functools.partial(attention_back_kernel, place),
        in_specs=[WHOLE] * len(arrays),
        out_specs=[WHOLE] * (2 + len(edges)),
        out_shape=[jax.ShapeDtypeStruct((4 * D, GC), BF), gf_shape] + edges,
        scratch_shapes=[
            VMEM((ROWS, GC), BF),
            VMEM((GC, EXT), BF),
            VMEM((ROWS, GC), BF),
            VMEM((EXT, GC), F32),
            VMEM((EXT, GC), F32),
            VMEM((EXT, GC), BF),
            VMEM((EXT, GC), BF),
        ],
        compiler_params=params(),
        cost_estimate=cost(4e9, 6e6, BLOCKS * WIN * 2 * QB),
        name="attention_back",
    )(*arrays)


def feed_group(n2_ref, n2t_ref, up_ref, upt_ref, low, high, to_ref):
    inner = square(low)
    pre = dot(n2_ref[...], inner)
    grad_act = dot_nt(up_ref[...], square(high)) * 0.5
    gate = jax.nn.sigmoid(pre)
    act = (pre * gate).astype(BF)
    grad_inner = (grad_act * gate * (1.0 + pre * (1.0 - gate))).astype(BF)
    to_ref[:D] = dot(n2t_ref[...], grad_inner).astype(BF)
    to_ref[D:] = (dot(upt_ref[...], act) * 0.5).astype(BF)
    return dot_nt(grad_inner, inner)


def feed_near_kernel(*refs):
    ext_ref, up_ref, gain_ref = refs[:3]
    ctx, vo, high, low = refs[3:7], refs[7:11], refs[11:13], refs[13:15]
    give_ref, keep_ref, sc_ref, inv_ref, n2_ref, n2t_ref, upt_ref, gs_ref = refs[15:]
    middle = ext_ref[HALF : HALF + ROWS].astype(F32)
    for k in range(4):
        middle = middle + dot(ctx[k][...], wide(vo[k]))
    scaled, inverse = norm_rows(middle)
    sc_ref[...] = scaled
    inv_ref[...] = inverse
    normed = scaled * gain_ref[...]
    n2_ref[...] = normed.astype(BF)
    n2t_ref[...] = normed.T.astype(BF)
    upt_ref[...] = up_ref[...].T
    shared = (n2_ref, n2t_ref, up_ref, upt_ref)
    gs_ref[...] = feed_group(*shared, low[1], high[1], give_ref)
    gs_ref[...] += feed_group(*shared, low[0], high[0], keep_ref)


def run_feed_near(ext, up, gain, ctx, vo, high, low):
    return pl.pallas_call(
        feed_near_kernel,
        in_specs=[WHOLE] * 15,
        out_specs=[WHOLE] * 8,
        out_shape=[
            jax.ShapeDtypeStruct((2 * D, D), BF),
            jax.ShapeDtypeStruct((2 * D, D), BF),
            jax.ShapeDtypeStruct((ROWS, D), F32),
            jax.ShapeDtypeStruct((ROWS, 1), F32),
            jax.ShapeDtypeStruct((ROWS, D), BF),
            jax.ShapeDtypeStruct((D, ROWS), BF),
            jax.ShapeDtypeStruct((D, ROWS), BF),
            jax.ShapeDtypeStruct((ROWS, D), F32),
        ],
        compiler_params=params(),
        cost_estimate=cost(4e9, 14e6, ROWS * 1024),
        name="feed_near",
    )(ext, up, gain.reshape(1, D), *ctx, *vo, *high, *low)


def feed_far_kernel(*refs):
    up_ref, gain_ref, sc_ref, inv_ref, n2_ref, n2t_ref, upt_ref, gs_in_ref = refs[:8]
    low, high = refs[8:10], refs[10:12]
    gm_ref, gml_ref, give_ref, keep_ref, gs_ref = refs[12:]
    shared = (n2_ref, n2t_ref, up_ref, upt_ref)
    gs_ref[...] = gs_in_ref[...] + feed_group(*shared, low[1], high[1], give_ref)
    gs_ref[...] += feed_group(*shared, low[0], high[0], keep_ref)
    grad_middle = up_ref[...].astype(F32) + norm_back(
        gs_ref[...], sc_ref[...], inv_ref[...], gain_ref[...]
    )
    gm_ref[...] = grad_middle
    gml_ref[...] = grad_middle.astype(BF)


def run_feed_far(up, gain, held, low, high):
    return pl.pallas_call(
        feed_far_kernel,
        in_specs=[WHOLE] * 12,
        out_specs=[WHOLE] * 4,
        out_shape=[
            jax.ShapeDtypeStruct((ROWS, D), F32),
            jax.ShapeDtypeStruct((ROWS, D), BF),
            jax.ShapeDtypeStruct((2 * D, D), BF),
            jax.ShapeDtypeStruct((2 * D, D), BF),
        ],
        scratch_shapes=[VMEM((ROWS, D), F32)],
        compiler_params=params(),
        cost_estimate=cost(4e9, 14e6, ROWS * 1024),
        name="feed_far",
    )(up, gain.reshape(1, D), *held, *low, *high)


def last_kernel(gf_ref, low_ref, high_ref, own_ref, gain_ref, gm_ref, out_ref):
    scaled, inverse = norm_rows(own_ref[HALF : HALF + ROWS].astype(F32))
    grad = gf_ref[...] + jnp.concatenate(
        [low_ref[...].astype(F32), high_ref[...].astype(F32)], axis=0
    )
    out_ref[...] = gm_ref[...] + norm_back(grad, scaled, inverse, gain_ref[...])


def run_last(gf, low, high, own, gain, gm):
    return pl.pallas_call(
        last_kernel,
        in_specs=[WHOLE] * 6,
        out_shape=jax.ShapeDtypeStruct((ROWS, D), F32),
        compiler_params=params(),
        cost_estimate=cost(ROWS * D * 20, 5e6),
        name="frames_grad",
    )(gf, low, high, own, gain.reshape(1, D), gm)


def edge_kernel(i_ref, frames_ref, edge_ref, sem):
    start = pl.multiple_of(jnp.where(i_ref[0] == 3, 3 * ROWS + HALF, 0), HALF)
    copy = pltpu.make_async_copy(frames_ref.at[pl.ds(start, HALF)], edge_ref, sem)
    copy.start()
    copy.wait()


def run_edge(frames, index):
    return pl.pallas_call(
        edge_kernel,
        in_specs=[
            pl.BlockSpec(memory_space=pltpu.SMEM),
            pl.BlockSpec(memory_space=pltpu.HBM),
        ],
        out_specs=WHOLE,
        out_shape=jax.ShapeDtypeStruct((HALF, D), BF),
        scratch_shapes=[pltpu.SemaphoreType.DMA],
        compiler_params=params(58),
        cost_estimate=cost(1e5, 1e6),
        name="edge",
    )(index.reshape(1), frames)


def pack_kernel(i_ref, frames_ref, up_in_ref, q_ref, k_ref, v_ref, o_ref, inner_ref, outer_ref,
                low_ref, high_ref, low_two_ref, high_two_ref, ext_ref, up_ref, sems):
    i = i_ref[0]

    def at(start, size):
        return pl.ds(pl.multiple_of(start, HALF), size)

    moves = [
        (q_ref, low_ref.at[pl.ds(0, D)]),
        (k_ref, low_ref.at[pl.ds(D, D)]),
        (v_ref, high_ref.at[pl.ds(0, D)]),
        (frames_ref.at[at(jnp.maximum(i * ROWS - HALF, 0), HALF)], ext_ref.at[pl.ds(0, HALF)]),
        (frames_ref.at[at(i * ROWS, ROWS)], ext_ref.at[pl.ds(HALF, ROWS)]),
        (
            frames_ref.at[at(jnp.minimum(i * ROWS + ROWS, 3 * ROWS + HALF), HALF)],
            ext_ref.at[pl.ds(HALF + ROWS, HALF)],
        ),
        (up_in_ref.at[at(i * ROWS, ROWS)], up_ref),
    ]
    for j in range(4):
        cols = pl.ds(j * GC, GC)
        moves.append((o_ref.at[:, cols], high_ref.at[pl.ds(D + j * GC, GC)]))
        place = pl.ds(j * D, D)
        moves.append((inner_ref.at[:, cols], low_two_ref.at[place]))
        moves.append((outer_ref.at[:, cols], high_two_ref.at[place]))
    copies = [
        pltpu.make_async_copy(source, target, sems.at[n])
        for n, (source, target) in enumerate(moves)
    ]
    for copy in copies:
        copy.start()
    for copy in copies:
        copy.wait()


def run_pack(frames, upstream, wq, wk, wv, wo, wi, wu, index):
    anywhere = pl.BlockSpec(memory_space=pltpu.HBM)
    shapes = [(2 * D, GC)] * 2 + [(4 * D, GC)] * 2 + [(EXT, D), (ROWS, D)]
    return pl.pallas_call(
        pack_kernel,
        in_specs=[pl.BlockSpec(memory_space=pltpu.SMEM)] + [anywhere] * 8,
        out_specs=[WHOLE] * 6,
        out_shape=[jax.ShapeDtypeStruct(shape, BF) for shape in shapes],
        scratch_shapes=[pltpu.SemaphoreType.DMA((19,))],
        compiler_params=params(58),
        cost_estimate=cost(1e5, 3e6),
        name="pack",
    )(index.reshape(1), frames, upstream, wq, wk, wv, wo, wi, wu)


def add(*terms):
    total = terms[0].astype(F32)
    for term in terms[1:]:
        total = total + term.astype(F32)
    return total.astype(BF)


def feed_split_kernel(near_ref, got_near_ref, far_ref, got_far_ref, out_ref, a_ref, b_ref):
    out_ref[...] = add(near_ref[...], got_near_ref[...])
    a_ref[...] = add(far_ref[:D], got_far_ref[:D])
    b_ref[...] = add(far_ref[D:], got_far_ref[D:])


def proj_split_kernel(keep_ref, got_ref, a_ref, b_ref):
    h = 2 * D
    a_ref[...] = add(keep_ref[:h], got_ref[:h])
    b_ref[...] = add(keep_ref[h:], got_ref[h:])


def join_kernel(near_ref, a_ref, b_ref, keep_ref, got_ref, pa_ref, pb_ref, out_ref):
    for n in range(32):
        feed, proj = (a_ref, pa_ref) if n < 16 else (b_ref, pb_ref)
        rows, part = slice(n * 32, (n + 1) * 32), slice(n % 16 * 32, (n % 16 + 1) * 32)
        out_ref[n, :32] = add(near_ref[rows], feed[part])
        for j in range(4):
            rows = slice(n * 64 + j * 16, n * 64 + (j + 1) * 16)
            part = slice(n % 16 * 64 + j * 16, n % 16 * 64 + (j + 1) * 16)
            out_ref[n, 32:, j * GC : (j + 1) * GC] = add(keep_ref[rows], got_ref[rows], proj[part])


def spread_kernel(parts_ref, out_ref):
    total = add(*[parts_ref[n] for n in range(32)])
    for n in range(32):
        out_ref[n] = total


def end_kernel(scale, total_ref, q_ref, k_ref, v_ref, o_ref, inner_ref, outer_ref):
    for n in range(16):
        inner_ref[n * 32 : (n + 1) * 32] = total_ref[n, :32].astype(F32) * scale
    outer = jnp.concatenate([total_ref[16 + n, :32] for n in range(16)], axis=0)
    outer_ref[...] = outer.astype(F32).T * scale
    for n in range(32):
        for j in range(4):
            block = total_ref[n, 32:, j * GC : (j + 1) * GC].astype(F32) * scale
            start = n % 8 * 64 + j * 16
            if n < 24:
                (q_ref, k_ref, v_ref)[n // 8][start : start + 16] = block
            else:
                tile, row = start // GC, start % GC
                o_ref[row : row + 16, tile * GC : (tile + 1) * GC] = block


def small(kernel, name, shapes, *arrays, final=False, loose=False):
    outs = [jax.ShapeDtypeStruct(shape, F32 if final else BF) for shape in shapes]
    extra = {} if final or loose else {"out_specs": [WHOLE] * len(outs)}
    return pl.pallas_call(
        kernel,
        in_specs=[WHOLE] * len(arrays),
        out_shape=outs,
        compiler_params=params(),
        cost_estimate=cost(1e6, 2e6),
        name=name,
        **extra,
    )(*arrays)


def swap(array, bits):
    return lax.ppermute(array, AXES, [(n, n ^ bits) for n in range(128)])


def after(first, *later):
    return lax.optimization_barrier((first,) + later)[0]


def exchange(parts):
    return lax.all_to_all(parts, "tm", 0, 0, tiled=True)


def local(
    frames,
    upstream,
    recording,
    first_gain,
    query_weight,
    key_weight,
    value_weight,
    out_weight,
    second_gain,
    inner_weight,
    outer_weight,
):
    t = lax.axis_index("tm")
    i = lax.axis_index("ffn")
    slab = frames.shape[0]
    devices = lax.axis_size("tm") * 4
    scale = 1.0 / math.sqrt(recording.shape[0])

    record_pad = jnp.pad(recording, (HALF, HALF), constant_values=-1)
    rec_ext = lax.dynamic_slice_in_dim(record_pad, t * slab + i * ROWS, EXT)
    rec_col = rec_ext.reshape(EXT, 1)
    rec_row = rec_ext[HALF : HALF + ROWS].reshape(BLOCKS, 1, QB)
    rec_col, rec_row, index = lax.optimization_barrier((rec_col, rec_row, i))
    edge = run_edge(frames, index)
    low_own, high_own, low_own2, high_own2, ext, up = run_pack(
        frames, upstream, query_weight, key_weight, value_weight, out_weight,
        inner_weight, outer_weight, after(index, edge),
    )
    pairs = [(4 * n + 3, 4 * n + 4) for n in range(31)] + [(4 * n + 4, 4 * n + 3) for n in range(31)]
    halo = lax.ppermute(edge, AXES, pairs)
    low_far, high_far = swap(after(low_own, halo), 2), swap(after(high_own, halo), 6)
    low_near, high_near = swap(low_own, 1), swap(high_own, 1)

    normed, normed_t, bias = run_norm(ext, halo, first_gain, rec_col, rec_row, i)
    qs, ks, vs, ctx, lse = [], [], [], [], []

    def forward(qk, vo):
        q, key, v, c, s = run_context(normed, qk, vo, bias)
        qs.append(q)
        ks.append(key)
        vs.append(v)
        ctx.append(c)
        lse.append(s)

    forward(low_own, high_own)
    low_far2, high_far2 = swap(after(low_own2, ctx[0]), 2), swap(after(high_own2, ctx[0]), 6)
    forward(low_near, high_near)
    low_far, high_far = after(low_far, *ctx), after(high_far, *ctx)
    low = [low_own, low_near, low_far, swap(low_far, 1)]
    high = [high_own, high_near, high_far, swap(high_far, 1)]
    forward(low[2], high[2])
    forward(low[3], high[3])

    low_near2, high_near2 = swap(after(low_own2, ctx[0]), 1), swap(after(high_own2, ctx[0]), 1)
    give1, keep0, *held = run_feed_near(
        ext, up, second_gain, ctx, high, [high_own2, high_near2], [low_own2, low_near2]
    )
    got_near = swap(give1, 1)
    low_far2, high_far2 = after(low_far2, give1), after(high_far2, give1)
    grad_middle, gml, give3, keep2 = run_feed_far(
        up, second_gain, held, [low_far2, swap(low_far2, 1)], [high_far2, swap(high_far2, 1)],
    )
    got_far = swap(give3, 1)
    near, far_a, far_b = small(
        feed_split_kernel, "feed_split", [(2 * D, D), (D, D), (D, D)],
        keep0, got_near, keep2, got_far,
    )

    dw = [None] * 4

    def back(place, gf, k, grads):
        dw[k], *rest = run_attention_back(
            place, gf, grads, low[k], high[k], ctx[k], qs[k], ks[k], vs[k], lse[k], bias, normed_t
        )
        return rest

    (gf,) = back(0, None, 3, gml)
    got3 = swap(dw[3], 1)
    (gf,) = back(1, gf, 2, after(gml, near, gf))
    proj_a, proj_b = small(proj_split_kernel, "proj_split", [(2 * D, GC)] * 2, dw[2], got3)
    proj_got_a, proj_got_b = swap(proj_a, 2), swap(proj_b, 6)
    (gf,) = back(1, gf, 1, after(gml, proj_a))
    got1 = swap(dw[1], 1)
    feed_got_a, feed_got_b = swap(far_a, 2), swap(far_b, 6)
    gf, before, behind = back(2, gf, 0, after(gml, feed_got_a, feed_got_b))
    from_low = lax.ppermute(behind, AXES, [(n, n + 1) for n in range(devices - 1)])
    from_high = lax.ppermute(before, AXES, [(n + 1, n) for n in range(devices - 1)])

    (parts,) = small(
        join_kernel, "join", [(32, 48, D)],
        near, feed_got_a, feed_got_b, dw[0], got1, proj_got_a, proj_got_b, loose=True,
    )
    got = exchange(parts)
    grad_frames = run_last(gf, from_low, from_high, ext, first_gain, grad_middle)
    (spread,) = small(
        spread_kernel, "spread", [(32, 48, D)], after(got, from_low, from_high), loose=True
    )
    total = exchange(spread)
    grads = small(
        functools.partial(end_kernel, scale), "end", [(D, GC)] * 3 + [(GC, D), (D, D), (D, D)],
        after(total, grad_frames), final=True,
    )
    return (grad_frames, *grads)


def solution(mesh):
    in_specs = (
        P("tm", None),
        P("tm", None),
        P(),
        P(),
        P(None, "ffn"),
        P(None, "ffn"),
        P(None, "ffn"),
        P("ffn", None),
        P(),
        P(None, "ffn"),
        P("ffn", None),
    )
    out_specs = (
        P(("tm", "ffn"), None),
        P(None, "ffn"),
        P(None, "ffn"),
        P(None, "ffn"),
        P("ffn", None),
        P(None, "ffn"),
        P("ffn", None),
    )
    return jax.shard_map(local, mesh=mesh, in_specs=in_specs, out_specs=out_specs, check_vma=False)
```

```python
import functools
import math

import jax
import jax.numpy as jnp
from jax import lax
from jax.experimental import pallas as pl
from jax.experimental.pallas import tpu as pltpu
from jax.sharding import PartitionSpec as P

HEAD_DIM = 64
HALF = 256
ROWS = 512
EXT = ROWS + 2 * HALF
QB = 128
WIN = QB + 2 * HALF
BLOCKS = ROWS // QB
GC = 128
D = 512
epsilon = 1e-05
masked_score = -1e30
BF = jnp.bfloat16
F32 = jnp.float32
AXES = ("tm", "ffn")
VMEM = pltpu.VMEM
WHOLE = pl.BlockSpec(memory_space=pltpu.VMEM)


def dot(a, b):
    return jnp.dot(a, b, preferred_element_type=F32)


def dot_nt(a, b):
    return lax.dot_general(a, b, (((1,), (1,)), ((), ())), preferred_element_type=F32)


def params(mib=16):
    return pltpu.CompilerParams(vmem_limit_bytes=mib * 1024 * 1024)


def cost(flops, nbytes, trans=0):
    return pl.CostEstimate(
        flops=int(flops / 8), bytes_accessed=int(nbytes / 8), transcendentals=int(trans / 8)
    )


def norm_rows(x):
    center = jnp.mean(x, axis=-1, keepdims=True)
    shifted = x - center
    inverse = lax.rsqrt(jnp.mean(shifted * shifted, axis=-1, keepdims=True) + epsilon)
    return shifted * inverse, inverse


def norm_back(grad_normed, scaled, inverse, gain):
    weighted = grad_normed * gain
    first = jnp.mean(weighted, axis=-1, keepdims=True)
    second = jnp.mean(weighted * scaled, axis=-1, keepdims=True)
    return inverse * (weighted - first - scaled * second)


def norm_kernel(i_ref, ext_ref, halo_ref, gain_ref, col_ref, row_ref, n_ref, nt_ref, bias_ref):
    step = pl.program_id(0)
    outside = ((i_ref[0] == 0) & (step == 0)) | ((i_ref[0] == 3) & (step == 3))
    x = jnp.where(outside, halo_ref[...].astype(F32), ext_ref[...].astype(F32))
    scaled, _ = norm_rows(x)
    normed = scaled * gain_ref[...]
    n_ref[...] = normed.astype(BF)
    nt_ref[...] = normed.T.astype(BF)
    keys = col_ref[pl.ds(pl.multiple_of(step * QB, QB), WIN), :]
    offset = lax.broadcasted_iota(jnp.int32, (WIN, QB), 0) - lax.broadcasted_iota(
        jnp.int32, (WIN, QB), 1
    )
    band = (offset >= 0) & (offset < 2 * HALF)
    bias_ref[0] = jnp.where(band & (keys == row_ref[0]), 0.0, masked_score)


def run_norm(ext, halo, gain, rec_col, rec_row, index):
    spec = pltpu.PrefetchScalarGridSpec(
        num_scalar_prefetch=1,
        grid=(4,),
        in_specs=[
            pl.BlockSpec((HALF, D), lambda j, i: (j, 0)),
            pl.BlockSpec((HALF, D), lambda j, i: (0, 0)),
            pl.BlockSpec((1, D), lambda j, i: (0, 0)),
            pl.BlockSpec((EXT, 1), lambda j, i: (0, 0)),
            pl.BlockSpec((1, 1, QB), lambda j, i: (j, 0, 0)),
        ],
        out_specs=[
            pl.BlockSpec((HALF, D), lambda j, i: (j, 0)),
            pl.BlockSpec((D, HALF), lambda j, i: (0, j)),
            pl.BlockSpec((1, WIN, QB), lambda j, i: (j, 0, 0)),
        ],
    )
    return pl.pallas_call(
        norm_kernel,
        grid_spec=spec,
        out_shape=[
            jax.ShapeDtypeStruct((EXT, D), BF),
            jax.ShapeDtypeStruct((D, EXT), BF),
            jax.ShapeDtypeStruct((BLOCKS, WIN, QB), F32),
        ],
        compiler_params=params(),
        cost_estimate=cost(EXT * D * 12, 5e6),
        name="norm_first",
    )(index.reshape(1), ext, halo, gain.reshape(1, D), rec_col, rec_row)


def wide(vo_ref):
    return jnp.concatenate([vo_ref[D + j * GC : D + (j + 1) * GC] for j in range(4)], axis=1)


def square(packed_ref):
    return jnp.concatenate([packed_ref[j * D : (j + 1) * D] for j in range(4)], axis=1)


def stack_heads(block):
    lane = lax.broadcasted_iota(jnp.int32, block.shape, 1)
    zero = jnp.zeros_like(block)
    low = jnp.where(lane < HEAD_DIM, block, zero)
    high = jnp.where(lane < HEAD_DIM, zero, block)
    return jnp.concatenate([low, high], axis=0)


def pick_heads(both):
    return jnp.concatenate([both[:HEAD_DIM, :QB], both[HEAD_DIM:, QB:]], axis=0).T


def context_kernel(n_ref, qk_ref, vo_ref, bias_ref, q_ref, k_ref, v_ref, ctx_ref, lse_ref, vt_ref):
    n = n_ref[...]
    q_ref[...] = dot(n_ref[HALF : HALF + ROWS], qk_ref[:D]).astype(BF) * 0.125
    k_ref[...] = dot(n, qk_ref[D : 2 * D]).astype(BF)
    v = dot(n, vo_ref[:D])
    v_ref[...] = v.astype(BF)
    vt_ref[...] = v.T.astype(BF)
    for b in range(BLOCKS):
        win = slice(b * QB, b * QB + WIN)
        rows = slice(b * QB, b * QB + QB)
        queries = stack_heads(q_ref[rows])
        bias = bias_ref[b]
        scores = dot_nt(k_ref[win], queries) + jnp.concatenate([bias, bias], axis=1)
        peak = jnp.max(scores, axis=0, keepdims=True)
        weights = jnp.exp(scores - peak)
        total = jnp.sum(weights, axis=0, keepdims=True)
        both = dot(vt_ref[:, win], weights.astype(BF)) / total
        ctx_ref[rows] = pick_heads(both).astype(BF)
        lse_ref[b] = peak + jnp.log(total)


def run_context(normed, qk, vo, bias):
    return pl.pallas_call(
        context_kernel,
        in_specs=[WHOLE] * 4,
        out_specs=[WHOLE] * 5,
        out_shape=[
            jax.ShapeDtypeStruct((ROWS, GC), BF),
            jax.ShapeDtypeStruct((EXT, GC), BF),
            jax.ShapeDtypeStruct((EXT, GC), BF),
            jax.ShapeDtypeStruct((ROWS, GC), BF),
            jax.ShapeDtypeStruct((BLOCKS, 1, 2 * QB), F32),
        ],
        scratch_shapes=[VMEM((GC, EXT), BF)],
        compiler_params=params(),
        cost_estimate=cost(2e9, 4e6, BLOCKS * WIN * 2 * QB),
        name="context",
    )(normed, qk, vo, bias)


def attention_back_kernel(place, *refs):
    gml_ref, qk_ref, vo_ref, ctx_ref, q_ref, k_ref, v_ref, lse_ref, bias_ref, nt_ref = refs[:10]
    refs = refs[10:]
    if place > 0:
        gf_in_ref, refs = refs[0], refs[1:]
    dw_ref, gf_ref, refs = refs[0], refs[1], refs[2:]
    if place == 2:
        before_ref, behind_ref, refs = refs[0], refs[1], refs[2:]
    g_ref, kt_ref, dq_ref, dka_ref, dva_ref, dk_ref, dv_ref = refs
    g_ref[...] = dot_nt(gml_ref[...], wide(vo_ref)).astype(BF)
    grad_out = dot(ctx_ref[...].T, gml_ref[...]).astype(BF)
    for j in range(4):
        dw_ref[3 * D + j * GC : 3 * D + (j + 1) * GC] = grad_out[:, j * GC : (j + 1) * GC]
    kt_ref[...] = k_ref[...].T
    dka_ref[...] = jnp.zeros_like(dka_ref)
    dva_ref[...] = jnp.zeros_like(dva_ref)
    for b in range(BLOCKS):
        win = slice(b * QB, b * QB + WIN)
        rows = slice(b * QB, b * QB + QB)
        queries = stack_heads(q_ref[rows])
        grads = stack_heads(g_ref[rows])
        bias = bias_ref[b]
        scores = dot_nt(k_ref[win], queries) + jnp.concatenate([bias, bias], axis=1)
        prob = jnp.exp(scores - lse_ref[b])
        grad_prob = dot_nt(v_ref[win], grads)
        inner = jnp.sum(prob * grad_prob, axis=0, keepdims=True)
        grad_scores = (prob * (grad_prob - inner)).astype(BF)
        dva_ref[win] += dot(prob.astype(BF), grads)
        dka_ref[win] += dot(grad_scores, queries)
        both = dot(kt_ref[:, win], grad_scores)
        dq_ref[rows] = (pick_heads(both) * 0.125).astype(BF)
    dk_ref[...] = dka_ref[...].astype(BF)
    dv_ref[...] = dva_ref[...].astype(BF)
    dw_ref[:D] = dot(nt_ref[:, HALF : HALF + ROWS], dq_ref[...]).astype(BF)
    dw_ref[D : 2 * D] = dot(nt_ref[...], dk_ref[...]).astype(BF)
    dw_ref[2 * D : 3 * D] = dot(nt_ref[...], dv_ref[...]).astype(BF)
    for part in range(4):
        rows = slice(part * HALF, (part + 1) * HALF)
        term = dot_nt(dk_ref[rows], qk_ref[D : 2 * D]) + dot_nt(dv_ref[rows], vo_ref[:D])
        if part in (1, 2):
            own = slice((part - 1) * HALF, part * HALF)
            term = term + dot_nt(dq_ref[own], qk_ref[:D])
        if place > 0:
            term = term + gf_in_ref[rows]
        if place < 2:
            gf_ref[rows] = term
        elif part == 0:
            before_ref[...] = term.astype(BF)
        elif part == 3:
            behind_ref[...] = term.astype(BF)
        else:
            gf_ref[own] = term


def run_attention_back(place, gf, *arrays):
    gf_shape = jax.ShapeDtypeStruct((ROWS if place == 2 else EXT, D), F32)
    edges = [jax.ShapeDtypeStruct((HALF, D), BF)] * 2 if place == 2 else []
    if place > 0:
        arrays = arrays + (gf,)
    return pl.pallas_call(
        functools.partial(attention_back_kernel, place),
        in_specs=[WHOLE] * len(arrays),
        out_specs=[WHOLE] * (2 + len(edges)),
        out_shape=[jax.ShapeDtypeStruct((4 * D, GC), BF), gf_shape] + edges,
        scratch_shapes=[
            VMEM((ROWS, GC), BF),
            VMEM((GC, EXT), BF),
            VMEM((ROWS, GC), BF),
            VMEM((EXT, GC), F32),
            VMEM((EXT, GC), F32),
            VMEM((EXT, GC), BF),
            VMEM((EXT, GC), BF),
        ],
        compiler_params=params(),
        cost_estimate=cost(4e9, 6e6, BLOCKS * WIN * 2 * QB),
        name="attention_back",
    )(*arrays)


def feed_group(n2_ref, n2t_ref, up_ref, upt_ref, low, high, to_ref):
    inner = square(low)
    pre = dot(n2_ref[...], inner)
    grad_act = dot_nt(up_ref[...], square(high)) * 0.5
    gate = jax.nn.sigmoid(pre)
    act = (pre * gate).astype(BF)
    grad_inner = (grad_act * gate * (1.0 + pre * (1.0 - gate))).astype(BF)
    to_ref[:D] = dot(n2t_ref[...], grad_inner).astype(BF)
    to_ref[D:] = (dot(upt_ref[...], act) * 0.5).astype(BF)
    return dot_nt(grad_inner, inner)


def feed_near_kernel(*refs):
    ext_ref, up_ref, gain_ref = refs[:3]
    ctx, vo, high, low = refs[3:7], refs[7:11], refs[11:13], refs[13:15]
    give_ref, keep_ref, sc_ref, inv_ref, n2_ref, n2t_ref, upt_ref, gs_ref = refs[15:]
    middle = ext_ref[HALF : HALF + ROWS].astype(F32)
    for k in range(4):
        middle = middle + dot(ctx[k][...], wide(vo[k]))
    scaled, inverse = norm_rows(middle)
    sc_ref[...] = scaled
    inv_ref[...] = inverse
    normed = scaled * gain_ref[...]
    n2_ref[...] = normed.astype(BF)
    n2t_ref[...] = normed.T.astype(BF)
    upt_ref[...] = up_ref[...].T
    shared = (n2_ref, n2t_ref, up_ref, upt_ref)
    gs_ref[...] = feed_group(*shared, low[1], high[1], give_ref)
    gs_ref[...] += feed_group(*shared, low[0], high[0], keep_ref)


def run_feed_near(ext, up, gain, ctx, vo, high, low):
    return pl.pallas_call(
        feed_near_kernel,
        in_specs=[WHOLE] * 15,
        out_specs=[WHOLE] * 8,
        out_shape=[
            jax.ShapeDtypeStruct((2 * D, D), BF),
            jax.ShapeDtypeStruct((2 * D, D), BF),
            jax.ShapeDtypeStruct((ROWS, D), F32),
            jax.ShapeDtypeStruct((ROWS, 1), F32),
            jax.ShapeDtypeStruct((ROWS, D), BF),
            jax.ShapeDtypeStruct((D, ROWS), BF),
            jax.ShapeDtypeStruct((D, ROWS), BF),
            jax.ShapeDtypeStruct((ROWS, D), F32),
        ],
        compiler_params=params(),
        cost_estimate=cost(4e9, 14e6, ROWS * 1024),
        name="feed_near",
    )(ext, up, gain.reshape(1, D), *ctx, *vo, *high, *low)


def feed_mid_kernel(up_ref, n2_ref, n2t_ref, upt_ref, gs_in_ref, low_ref, high_ref, keep_ref, gs_ref):
    shared = (n2_ref, n2t_ref, up_ref, upt_ref)
    gs_ref[...] = gs_in_ref[...] + feed_group(*shared, low_ref, high_ref, keep_ref)


def run_feed_mid(up, held, low, high):
    return pl.pallas_call(
        feed_mid_kernel,
        in_specs=[WHOLE] * 7,
        out_specs=[WHOLE] * 2,
        out_shape=[
            jax.ShapeDtypeStruct((2 * D, D), BF),
            jax.ShapeDtypeStruct((ROWS, D), F32),
        ],
        compiler_params=params(),
        cost_estimate=cost(2e9, 7e6, ROWS * 512),
        name="feed_mid",
    )(up, *held, low, high)


def feed_far_kernel(
    up_ref, gain_ref, sc_ref, inv_ref, n2_ref, n2t_ref, upt_ref, gs_in_ref, low_ref, high_ref,
    gm_ref, gml_ref, give_ref,
):
    shared = (n2_ref, n2t_ref, up_ref, upt_ref)
    grad_second = gs_in_ref[...] + feed_group(*shared, low_ref, high_ref, give_ref)
    grad_middle = up_ref[...].astype(F32) + norm_back(
        grad_second, sc_ref[...], inv_ref[...], gain_ref[...]
    )
    gm_ref[...] = grad_middle
    gml_ref[...] = grad_middle.astype(BF)


def run_feed_far(up, gain, held, low, high):
    return pl.pallas_call(
        feed_far_kernel,
        in_specs=[WHOLE] * 10,
        out_specs=[WHOLE] * 3,
        out_shape=[
            jax.ShapeDtypeStruct((ROWS, D), F32),
            jax.ShapeDtypeStruct((ROWS, D), BF),
            jax.ShapeDtypeStruct((2 * D, D), BF),
        ],
        compiler_params=params(),
        cost_estimate=cost(2e9, 7e6, ROWS * 512),
        name="feed_far",
    )(up, gain.reshape(1, D), *held, low, high)


def last_kernel(gf_ref, low_ref, high_ref, own_ref, gain_ref, gm_ref, out_ref):
    scaled, inverse = norm_rows(own_ref[HALF : HALF + ROWS].astype(F32))
    grad = gf_ref[...] + jnp.concatenate(
        [low_ref[...].astype(F32), high_ref[...].astype(F32)], axis=0
    )
    out_ref[...] = gm_ref[...] + norm_back(grad, scaled, inverse, gain_ref[...])


def run_last(gf, low, high, own, gain, gm):
    return pl.pallas_call(
        last_kernel,
        in_specs=[WHOLE] * 6,
        out_shape=jax.ShapeDtypeStruct((ROWS, D), F32),
        compiler_params=params(),
        cost_estimate=cost(ROWS * D * 20, 5e6),
        name="frames_grad",
    )(gf, low, high, own, gain.reshape(1, D), gm)


def edge_kernel(i_ref, frames_ref, edge_ref, sem):
    start = pl.multiple_of(jnp.where(i_ref[0] == 3, 3 * ROWS + HALF, 0), HALF)
    copy = pltpu.make_async_copy(frames_ref.at[pl.ds(start, HALF)], edge_ref, sem)
    copy.start()
    copy.wait()


def run_edge(frames, index):
    return pl.pallas_call(
        edge_kernel,
        in_specs=[
            pl.BlockSpec(memory_space=pltpu.SMEM),
            pl.BlockSpec(memory_space=pltpu.HBM),
        ],
        out_specs=WHOLE,
        out_shape=jax.ShapeDtypeStruct((HALF, D), BF),
        scratch_shapes=[pltpu.SemaphoreType.DMA],
        compiler_params=params(58),
        cost_estimate=cost(1e5, 1e6),
        name="edge",
    )(index.reshape(1), frames)


def pack_kernel(i_ref, frames_ref, up_in_ref, q_ref, k_ref, v_ref, o_ref, inner_ref, outer_ref,
                low_ref, high_ref, low_two_ref, high_two_ref, ext_ref, up_ref, sems):
    i = i_ref[0]

    def at(start, size):
        return pl.ds(pl.multiple_of(start, HALF), size)

    moves = [
        (q_ref, low_ref.at[pl.ds(0, D)]),
        (k_ref, low_ref.at[pl.ds(D, D)]),
        (v_ref, high_ref.at[pl.ds(0, D)]),
        (frames_ref.at[at(jnp.maximum(i * ROWS - HALF, 0), HALF)], ext_ref.at[pl.ds(0, HALF)]),
        (frames_ref.at[at(i * ROWS, ROWS)], ext_ref.at[pl.ds(HALF, ROWS)]),
        (
            frames_ref.at[at(jnp.minimum(i * ROWS + ROWS, 3 * ROWS + HALF), HALF)],
            ext_ref.at[pl.ds(HALF + ROWS, HALF)],
        ),
        (up_in_ref.at[at(i * ROWS, ROWS)], up_ref),
    ]
    for j in range(4):
        cols = pl.ds(j * GC, GC)
        moves.append((o_ref.at[:, cols], high_ref.at[pl.ds(D + j * GC, GC)]))
        place = pl.ds(j * D, D)
        moves.append((inner_ref.at[:, cols], low_two_ref.at[place]))
        moves.append((outer_ref.at[:, cols], high_two_ref.at[place]))
    copies = [
        pltpu.make_async_copy(source, target, sems.at[n])
        for n, (source, target) in enumerate(moves)
    ]
    for copy in copies:
        copy.start()
    for copy in copies:
        copy.wait()


def run_pack(frames, upstream, wq, wk, wv, wo, wi, wu, index):
    anywhere = pl.BlockSpec(memory_space=pltpu.HBM)
    shapes = [(2 * D, GC)] * 2 + [(4 * D, GC)] * 2 + [(EXT, D), (ROWS, D)]
    return pl.pallas_call(
        pack_kernel,
        in_specs=[pl.BlockSpec(memory_space=pltpu.SMEM)] + [anywhere] * 8,
        out_specs=[WHOLE] * 6,
        out_shape=[jax.ShapeDtypeStruct(shape, BF) for shape in shapes],
        scratch_shapes=[pltpu.SemaphoreType.DMA((19,))],
        compiler_params=params(58),
        cost_estimate=cost(1e5, 3e6),
        name="pack",
    )(index.reshape(1), frames, upstream, wq, wk, wv, wo, wi, wu)


def add(*terms):
    total = terms[0].astype(F32)
    for term in terms[1:]:
        total = total + term.astype(F32)
    return total.astype(BF)


def feed_split_kernel(near_ref, got_near_ref, far_ref, got_far_ref, out_ref, a_ref, b_ref):
    out_ref[...] = add(near_ref[...], got_near_ref[...])
    a_ref[...] = add(far_ref[:D], got_far_ref[:D])
    b_ref[...] = add(far_ref[D:], got_far_ref[D:])


def proj_split_kernel(keep_ref, got_ref, a_ref, b_ref):
    h = 2 * D
    a_ref[...] = add(keep_ref[:h], got_ref[:h])
    b_ref[...] = add(keep_ref[h:], got_ref[h:])


def join_kernel(near_ref, a_ref, b_ref, keep_ref, got_ref, pa_ref, pb_ref, out_ref):
    for n in range(16):
        feed, proj = (a_ref, pa_ref) if n < 8 else (b_ref, pb_ref)
        rows, part = slice(n * 64, (n + 1) * 64), slice(n % 8 * 64, (n % 8 + 1) * 64)
        out_ref[n, :64] = add(near_ref[rows], feed[part])
        for j in range(4):
            rows = slice(n * GC + j * 32, n * GC + (j + 1) * 32)
            part = slice(n % 8 * GC + j * 32, n % 8 * GC + (j + 1) * 32)
            out_ref[n, 64:, j * GC : (j + 1) * GC] = add(keep_ref[rows], got_ref[rows], proj[part])


def sum_kernel(parts_ref, out_ref):
    out_ref[...] = add(*[parts_ref[n] for n in range(16)])


def spread_kernel(mine_ref, got_ref, out_ref):
    total = add(mine_ref[...], got_ref[...])
    for n in range(16):
        out_ref[n] = total


def end_kernel(scale, total_ref, *refs):
    outs, helds, sems = refs[:6], refs[6:12], refs[12]
    copies = [
        pltpu.make_async_copy(held, out, sems.at[n])
        for n, (held, out) in enumerate(zip(helds, outs))
    ]
    q_ref, k_ref, v_ref, o_ref, inner_ref, outer_ref = helds
    outer = jnp.concatenate([total_ref[8 + n, :64] for n in range(8)], axis=0)
    outer_ref[...] = outer.astype(F32).T * scale
    copies[5].start()
    for n in range(8):
        inner_ref[n * 64 : (n + 1) * 64] = total_ref[n, :64].astype(F32) * scale
    copies[4].start()
    for n in range(16):
        for j in range(4):
            block = total_ref[n, 64:, j * GC : (j + 1) * GC].astype(F32) * scale
            if n < 12:
                start = n % 4 * GC + j * 32
                (q_ref, k_ref, v_ref)[n // 4][start : start + 32] = block
            else:
                o_ref[j * 32 : (j + 1) * 32, (n - 12) * GC : (n - 11) * GC] = block
        if n % 4 == 3:
            copies[n // 4].start()
    for copy in copies:
        copy.wait()


def run_end(scale, total):
    shapes = [(D, GC)] * 3 + [(GC, D), (D, D), (D, D)]
    return pl.pallas_call(
        functools.partial(end_kernel, scale),
        in_specs=[WHOLE],
        out_specs=[pl.BlockSpec(memory_space=pltpu.HBM)] * 6,
        out_shape=[jax.ShapeDtypeStruct(shape, F32) for shape in shapes],
        scratch_shapes=[VMEM(shape, F32) for shape in shapes]
        + [pltpu.SemaphoreType.DMA((6,))],
        compiler_params=params(),
        cost_estimate=cost(1e6, 5e6),
        name="end",
    )(total)


def small(kernel, name, shapes, *arrays, final=False, loose=False):
    outs = [jax.ShapeDtypeStruct(shape, F32 if final else BF) for shape in shapes]
    extra = {} if final or loose else {"out_specs": [WHOLE] * len(outs)}
    return pl.pallas_call(
        kernel,
        in_specs=[WHOLE] * len(arrays),
        out_shape=outs,
        compiler_params=params(),
        cost_estimate=cost(1e6, 2e6),
        name=name,
        **extra,
    )(*arrays)


def swap(array, bits):
    return lax.ppermute(array, AXES, [(n, n ^ bits) for n in range(128)])


def after(first, *later):
    return lax.optimization_barrier((first,) + later)[0]


PEERS = [[2 * n + half for n in range(16)] for half in range(2)]


def exchange(parts):
    return lax.all_to_all(parts, "tm", 0, 0, axis_index_groups=PEERS, tiled=True)


def local(
    frames,
    upstream,
    recording,
    first_gain,
    query_weight,
    key_weight,
    value_weight,
    out_weight,
    second_gain,
    inner_weight,
    outer_weight,
):
    t = lax.axis_index("tm")
    i = lax.axis_index("ffn")
    slab = frames.shape[0]
    devices = lax.axis_size("tm") * 4
    scale = 1.0 / math.sqrt(recording.shape[0])

    record_pad = jnp.pad(recording, (HALF, HALF), constant_values=-1)
    rec_ext = lax.dynamic_slice_in_dim(record_pad, t * slab + i * ROWS, EXT)
    rec_col = rec_ext.reshape(EXT, 1)
    rec_row = rec_ext[HALF : HALF + ROWS].reshape(BLOCKS, 1, QB)
    rec_col, rec_row, index = lax.optimization_barrier((rec_col, rec_row, i))
    edge = run_edge(frames, index)
    low_own, high_own, low_own2, high_own2, ext, up = run_pack(
        frames, upstream, query_weight, key_weight, value_weight, out_weight,
        inner_weight, outer_weight, after(index, edge),
    )
    pairs = [(4 * n + 3, 4 * n + 4) for n in range(31)] + [(4 * n + 4, 4 * n + 3) for n in range(31)]
    halo = lax.ppermute(edge, AXES, pairs)
    low_far, high_far = swap(after(low_own, halo), 2), swap(after(high_own, halo), 6)
    low_near, high_near = swap(low_own, 1), swap(high_own, 1)

    normed, normed_t, bias = run_norm(ext, halo, first_gain, rec_col, rec_row, i)
    qs, ks, vs, ctx, lse = [], [], [], [], []

    def forward(qk, vo):
        q, key, v, c, s = run_context(normed, qk, vo, bias)
        qs.append(q)
        ks.append(key)
        vs.append(v)
        ctx.append(c)
        lse.append(s)

    forward(low_own, high_own)
    low_far2, high_far2 = swap(after(low_own2, ctx[0]), 2), swap(after(high_own2, ctx[0]), 6)
    forward(low_near, high_near)
    low_far, high_far = after(low_far, *ctx), after(high_far, *ctx)
    low = [low_own, low_near, low_far, swap(low_far, 1)]
    high = [high_own, high_near, high_far, swap(high_far, 1)]
    forward(low[2], high[2])
    forward(low[3], high[3])

    low_near2, high_near2 = swap(after(low_own2, ctx[0]), 1), swap(after(high_own2, ctx[0]), 1)
    give1, keep0, *held = run_feed_near(
        ext, up, second_gain, ctx, high, [high_own2, high_near2], [low_own2, low_near2]
    )
    got_near = swap(give1, 1)
    low_far2, high_far2 = after(low_far2, give1), after(high_far2, give1)
    scaled, inverse, *shared, partial = held
    low_last, high_last = swap(low_far2, 1), swap(high_far2, 1)
    keep2, partial = run_feed_mid(up, [*shared, partial], low_far2, high_far2)
    grad_middle, gml, give3 = run_feed_far(
        up, second_gain, [scaled, inverse, *shared, partial],
        after(low_last, keep2), after(high_last, keep2),
    )
    got_far = swap(give3, 1)
    near, far_a, far_b = small(
        feed_split_kernel, "feed_split", [(2 * D, D), (D, D), (D, D)],
        keep0, got_near, keep2, got_far,
    )

    dw = [None] * 4

    def back(place, gf, k, grads):
        dw[k], *rest = run_attention_back(
            place, gf, grads, low[k], high[k], ctx[k], qs[k], ks[k], vs[k], lse[k], bias, normed_t
        )
        return rest

    (gf,) = back(0, None, 3, gml)
    got3 = swap(dw[3], 1)
    (gf,) = back(1, gf, 2, after(gml, near, gf))
    proj_a, proj_b = small(proj_split_kernel, "proj_split", [(2 * D, GC)] * 2, dw[2], got3)
    proj_got_a, proj_got_b = swap(proj_a, 2), swap(proj_b, 6)
    (gf,) = back(1, gf, 1, after(gml, proj_a))
    got1 = swap(dw[1], 1)
    feed_got_a, feed_got_b = swap(far_a, 2), swap(far_b, 6)
    gf, before, behind = back(2, gf, 0, after(gml, feed_got_a, feed_got_b))
    from_low = lax.ppermute(behind, AXES, [(n, n + 1) for n in range(devices - 1)])
    from_high = lax.ppermute(before, AXES, [(n + 1, n) for n in range(devices - 1)])

    (parts,) = small(
        join_kernel, "join", [(16, 96, D)],
        near, feed_got_a, feed_got_b, dw[0], got1, proj_got_a, proj_got_b, loose=True,
    )
    got = exchange(parts)
    grad_frames = run_last(gf, from_low, from_high, ext, first_gain, grad_middle)
    (summed,) = small(sum_kernel, "sum", [(96, D)], got)
    other = swap(summed, 4)
    (spread,) = small(
        spread_kernel, "spread", [(16, 96, D)], after(summed, from_low, from_high), other,
        loose=True,
    )
    total = exchange(spread)
    grads = run_end(scale, after(total, grad_frames))
    return (grad_frames, *grads)


def solution(mesh):
    in_specs = (
        P("tm", None),
        P("tm", None),
        P(),
        P(),
        P(None, "ffn"),
        P(None, "ffn"),
        P(None, "ffn"),
        P("ffn", None),
        P(),
        P(None, "ffn"),
        P("ffn", None),
    )
    out_specs = (
        P(("tm", "ffn"), None),
        P(None, "ffn"),
        P(None, "ffn"),
        P(None, "ffn"),
        P("ffn", None),
        P(None, "ffn"),
        P("ffn", None),
    )
    return jax.shard_map(local, mesh=mesh, in_specs=in_specs, out_specs=out_specs, check_vma=False)
```

```python
import functools
import math

import jax
import jax.numpy as jnp
from jax import lax
from jax.experimental import pallas as pl
from jax.experimental.pallas import tpu as pltpu
from jax.sharding import PartitionSpec as P

HEAD_DIM = 64
HALF = 256
ROWS = 512
EXT = ROWS + 2 * HALF
QB = 128
WIN = QB + 2 * HALF
BLOCKS = ROWS // QB
GC = 128
D = 512
epsilon = 1e-05
masked_score = -1e30
BF = jnp.bfloat16
F32 = jnp.float32
AXES = ("tm", "ffn")
VMEM = pltpu.VMEM
WHOLE = pl.BlockSpec(memory_space=pltpu.VMEM)


def dot(a, b):
    return jnp.dot(a, b, preferred_element_type=F32)


def dot_nt(a, b):
    return lax.dot_general(a, b, (((1,), (1,)), ((), ())), preferred_element_type=F32)


def params(mib=16):
    return pltpu.CompilerParams(vmem_limit_bytes=mib * 1024 * 1024)


def cost(flops, nbytes, trans=0):
    return pl.CostEstimate(
        flops=int(flops / 8), bytes_accessed=int(nbytes / 8), transcendentals=int(trans / 8)
    )


def norm_rows(x):
    center = jnp.mean(x, axis=-1, keepdims=True)
    shifted = x - center
    inverse = lax.rsqrt(jnp.mean(shifted * shifted, axis=-1, keepdims=True) + epsilon)
    return shifted * inverse, inverse


def norm_back(grad_normed, scaled, inverse, gain):
    weighted = grad_normed * gain
    first = jnp.mean(weighted, axis=-1, keepdims=True)
    second = jnp.mean(weighted * scaled, axis=-1, keepdims=True)
    return inverse * (weighted - first - scaled * second)


def norm_kernel(i_ref, ext_ref, halo_ref, gain_ref, col_ref, row_ref, n_ref, nt_ref, bias_ref):
    step = pl.program_id(0)
    outside = ((i_ref[0] == 0) & (step == 0)) | ((i_ref[0] == 3) & (step == 3))
    x = jnp.where(outside, halo_ref[...].astype(F32), ext_ref[...].astype(F32))
    scaled, _ = norm_rows(x)
    normed = scaled * gain_ref[...]
    n_ref[...] = normed.astype(BF)
    nt_ref[...] = normed.T.astype(BF)
    keys = col_ref[pl.ds(pl.multiple_of(step * QB, QB), WIN), :]
    offset = lax.broadcasted_iota(jnp.int32, (WIN, QB), 0) - lax.broadcasted_iota(
        jnp.int32, (WIN, QB), 1
    )
    band = (offset >= 0) & (offset < 2 * HALF)
    bias_ref[0] = jnp.where(band & (keys == row_ref[0]), 0.0, masked_score)


def run_norm(ext, halo, gain, rec_col, rec_row, index):
    spec = pltpu.PrefetchScalarGridSpec(
        num_scalar_prefetch=1,
        grid=(4,),
        in_specs=[
            pl.BlockSpec((HALF, D), lambda j, i: (j, 0)),
            pl.BlockSpec((HALF, D), lambda j, i: (0, 0)),
            pl.BlockSpec((1, D), lambda j, i: (0, 0)),
            pl.BlockSpec((EXT, 1), lambda j, i: (0, 0)),
            pl.BlockSpec((1, 1, QB), lambda j, i: (j, 0, 0)),
        ],
        out_specs=[
            pl.BlockSpec((HALF, D), lambda j, i: (j, 0)),
            pl.BlockSpec((D, HALF), lambda j, i: (0, j)),
            pl.BlockSpec((1, WIN, QB), lambda j, i: (j, 0, 0)),
        ],
    )
    return pl.pallas_call(
        norm_kernel,
        grid_spec=spec,
        out_shape=[
            jax.ShapeDtypeStruct((EXT, D), BF),
            jax.ShapeDtypeStruct((D, EXT), BF),
            jax.ShapeDtypeStruct((BLOCKS, WIN, QB), F32),
        ],
        compiler_params=params(),
        cost_estimate=cost(EXT * D * 12, 5e6),
        name="norm_first",
    )(index.reshape(1), ext, halo, gain.reshape(1, D), rec_col, rec_row)


def wide(vo_ref):
    return jnp.concatenate([vo_ref[D + j * GC : D + (j + 1) * GC] for j in range(4)], axis=1)


def square(packed_ref):
    return jnp.concatenate([packed_ref[j * D : (j + 1) * D] for j in range(4)], axis=1)


def stack_heads(block):
    lane = lax.broadcasted_iota(jnp.int32, block.shape, 1)
    zero = jnp.zeros_like(block)
    low = jnp.where(lane < HEAD_DIM, block, zero)
    high = jnp.where(lane < HEAD_DIM, zero, block)
    return jnp.concatenate([low, high], axis=0)


def pick_heads(both):
    return jnp.concatenate([both[:HEAD_DIM, :QB], both[HEAD_DIM:, QB:]], axis=0).T


def context_kernel(n_ref, qk_ref, vo_ref, bias_ref, q_ref, k_ref, v_ref, ctx_ref, lse_ref, vt_ref):
    n = n_ref[...]
    q_ref[...] = dot(n_ref[HALF : HALF + ROWS], qk_ref[:D]).astype(BF) * 0.125
    k_ref[...] = dot(n, qk_ref[D : 2 * D]).astype(BF)
    v = dot(n, vo_ref[:D])
    v_ref[...] = v.astype(BF)
    vt_ref[...] = v.T.astype(BF)
    for b in range(BLOCKS):
        win = slice(b * QB, b * QB + WIN)
        rows = slice(b * QB, b * QB + QB)
        queries = stack_heads(q_ref[rows])
        bias = bias_ref[b]
        scores = dot_nt(k_ref[win], queries) + jnp.concatenate([bias, bias], axis=1)
        peak = jnp.max(scores, axis=0, keepdims=True)
        weights = jnp.exp(scores - peak)
        total = jnp.sum(weights, axis=0, keepdims=True)
        both = dot(vt_ref[:, win], weights.astype(BF)) / total
        ctx_ref[rows] = pick_heads(both).astype(BF)
        lse_ref[b] = peak + jnp.log(total)


def run_context(normed, qk, vo, bias):
    return pl.pallas_call(
        context_kernel,
        in_specs=[WHOLE] * 4,
        out_specs=[WHOLE] * 5,
        out_shape=[
            jax.ShapeDtypeStruct((ROWS, GC), BF),
            jax.ShapeDtypeStruct((EXT, GC), BF),
            jax.ShapeDtypeStruct((EXT, GC), BF),
            jax.ShapeDtypeStruct((ROWS, GC), BF),
            jax.ShapeDtypeStruct((BLOCKS, 1, 2 * QB), F32),
        ],
        scratch_shapes=[VMEM((GC, EXT), BF)],
        compiler_params=params(),
        cost_estimate=cost(2e9, 4e6, BLOCKS * WIN * 2 * QB),
        name="context",
    )(normed, qk, vo, bias)


def attention_back_kernel(place, *refs):
    gml_ref, qk_ref, vo_ref, ctx_ref, q_ref, k_ref, v_ref, lse_ref, bias_ref, nt_ref = refs[:10]
    refs = refs[10:]
    if place > 0:
        gf_in_ref, refs = refs[0], refs[1:]
    dw_ref, gf_ref, refs = refs[0], refs[1], refs[2:]
    if place == 2:
        before_ref, behind_ref, refs = refs[0], refs[1], refs[2:]
    g_ref, kt_ref, dq_ref, dka_ref, dva_ref, dk_ref, dv_ref = refs
    g_ref[...] = dot_nt(gml_ref[...], wide(vo_ref)).astype(BF)
    grad_out = dot(ctx_ref[...].T, gml_ref[...]).astype(BF)
    for j in range(4):
        dw_ref[3 * D + j * GC : 3 * D + (j + 1) * GC] = grad_out[:, j * GC : (j + 1) * GC]
    kt_ref[...] = k_ref[...].T
    dka_ref[...] = jnp.zeros_like(dka_ref)
    dva_ref[...] = jnp.zeros_like(dva_ref)
    for b in range(BLOCKS):
        win = slice(b * QB, b * QB + WIN)
        rows = slice(b * QB, b * QB + QB)
        queries = stack_heads(q_ref[rows])
        grads = stack_heads(g_ref[rows])
        bias = bias_ref[b]
        scores = dot_nt(k_ref[win], queries) + jnp.concatenate([bias, bias], axis=1)
        prob = jnp.exp(scores - lse_ref[b])
        grad_prob = dot_nt(v_ref[win], grads)
        inner = jnp.sum(prob * grad_prob, axis=0, keepdims=True)
        grad_scores = (prob * (grad_prob - inner)).astype(BF)
        dva_ref[win] += dot(prob.astype(BF), grads)
        dka_ref[win] += dot(grad_scores, queries)
        both = dot(kt_ref[:, win], grad_scores)
        dq_ref[rows] = (pick_heads(both) * 0.125).astype(BF)
    dk_ref[...] = dka_ref[...].astype(BF)
    dv_ref[...] = dva_ref[...].astype(BF)
    dw_ref[:D] = dot(nt_ref[:, HALF : HALF + ROWS], dq_ref[...]).astype(BF)
    dw_ref[D : 2 * D] = dot(nt_ref[...], dk_ref[...]).astype(BF)
    dw_ref[2 * D : 3 * D] = dot(nt_ref[...], dv_ref[...]).astype(BF)
    for part in range(4):
        rows = slice(part * HALF, (part + 1) * HALF)
        term = dot_nt(dk_ref[rows], qk_ref[D : 2 * D]) + dot_nt(dv_ref[rows], vo_ref[:D])
        if part in (1, 2):
            own = slice((part - 1) * HALF, part * HALF)
            term = term + dot_nt(dq_ref[own], qk_ref[:D])
        if place > 0:
            term = term + gf_in_ref[rows]
        if place < 2:
            gf_ref[rows] = term
        elif part == 0:
            before_ref[...] = term.astype(BF)
        elif part == 3:
            behind_ref[...] = term.astype(BF)
        else:
            gf_ref[own] = term


def run_attention_back(place, gf, *arrays):
    gf_shape = jax.ShapeDtypeStruct((ROWS if place == 2 else EXT, D), F32)
    edges = [jax.ShapeDtypeStruct((HALF, D), BF)] * 2 if place == 2 else []
    if place > 0:
        arrays = arrays + (gf,)
    return pl.pallas_call(
        functools.partial(attention_back_kernel, place),
        in_specs=[WHOLE] * len(arrays),
        out_specs=[WHOLE] * (2 + len(edges)),
        out_shape=[jax.ShapeDtypeStruct((4 * D, GC), BF), gf_shape] + edges,
        scratch_shapes=[
            VMEM((ROWS, GC), BF),
            VMEM((GC, EXT), BF),
            VMEM((ROWS, GC), BF),
            VMEM((EXT, GC), F32),
            VMEM((EXT, GC), F32),
            VMEM((EXT, GC), BF),
            VMEM((EXT, GC), BF),
        ],
        compiler_params=params(),
        cost_estimate=cost(4e9, 6e6, BLOCKS * WIN * 2 * QB),
        name="attention_back",
    )(*arrays)


def feed_group(n2_ref, n2t_ref, up_ref, upt_ref, low, high, to_ref):
    inner = square(low)
    pre = dot(n2_ref[...], inner)
    grad_act = dot_nt(up_ref[...], square(high)) * 0.5
    gate = jax.nn.sigmoid(pre)
    act = (pre * gate).astype(BF)
    grad_inner = (grad_act * gate * (1.0 + pre * (1.0 - gate))).astype(BF)
    to_ref[:D] = dot(n2t_ref[...], grad_inner).astype(BF)
    to_ref[D:] = (dot(upt_ref[...], act) * 0.5).astype(BF)
    return dot_nt(grad_inner, inner)


def feed_near_kernel(*refs):
    ext_ref, up_ref, gain_ref = refs[:3]
    ctx, vo, high, low = refs[3:7], refs[7:11], refs[11:13], refs[13:15]
    give_ref, keep_ref, sc_ref, inv_ref, n2_ref, n2t_ref, upt_ref, gs_ref = refs[15:]
    middle = ext_ref[HALF : HALF + ROWS].astype(F32)
    for k in range(4):
        middle = middle + dot(ctx[k][...], wide(vo[k]))
    scaled, inverse = norm_rows(middle)
    sc_ref[...] = scaled
    inv_ref[...] = inverse
    normed = scaled * gain_ref[...]
    n2_ref[...] = normed.astype(BF)
    n2t_ref[...] = normed.T.astype(BF)
    upt_ref[...] = up_ref[...].T
    shared = (n2_ref, n2t_ref, up_ref, upt_ref)
    gs_ref[...] = feed_group(*shared, low[1], high[1], give_ref)
    gs_ref[...] += feed_group(*shared, low[0], high[0], keep_ref)


def run_feed_near(ext, up, gain, ctx, vo, high, low):
    return pl.pallas_call(
        feed_near_kernel,
        in_specs=[WHOLE] * 15,
        out_specs=[WHOLE] * 8,
        out_shape=[
            jax.ShapeDtypeStruct((2 * D, D), BF),
            jax.ShapeDtypeStruct((2 * D, D), BF),
            jax.ShapeDtypeStruct((ROWS, D), F32),
            jax.ShapeDtypeStruct((ROWS, 1), F32),
            jax.ShapeDtypeStruct((ROWS, D), BF),
            jax.ShapeDtypeStruct((D, ROWS), BF),
            jax.ShapeDtypeStruct((D, ROWS), BF),
            jax.ShapeDtypeStruct((ROWS, D), F32),
        ],
        compiler_params=params(),
        cost_estimate=cost(4e9, 14e6, ROWS * 1024),
        name="feed_near",
    )(ext, up, gain.reshape(1, D), *ctx, *vo, *high, *low)


def feed_far_kernel(*refs):
    up_ref, gain_ref, sc_ref, inv_ref, n2_ref, n2t_ref, upt_ref, gs_in_ref = refs[:8]
    low, high = refs[8:10], refs[10:12]
    gm_ref, gml_ref, give_ref, keep_ref, gs_ref = refs[12:]
    shared = (n2_ref, n2t_ref, up_ref, upt_ref)
    gs_ref[...] = gs_in_ref[...] + feed_group(*shared, low[1], high[1], give_ref)
    gs_ref[...] += feed_group(*shared, low[0], high[0], keep_ref)
    grad_middle = up_ref[...].astype(F32) + norm_back(
        gs_ref[...], sc_ref[...], inv_ref[...], gain_ref[...]
    )
    gm_ref[...] = grad_middle
    gml_ref[...] = grad_middle.astype(BF)


def run_feed_far(up, gain, held, low, high):
    return pl.pallas_call(
        feed_far_kernel,
        in_specs=[WHOLE] * 12,
        out_specs=[WHOLE] * 4,
        out_shape=[
            jax.ShapeDtypeStruct((ROWS, D), F32),
            jax.ShapeDtypeStruct((ROWS, D), BF),
            jax.ShapeDtypeStruct((2 * D, D), BF),
            jax.ShapeDtypeStruct((2 * D, D), BF),
        ],
        scratch_shapes=[VMEM((ROWS, D), F32)],
        compiler_params=params(),
        cost_estimate=cost(4e9, 14e6, ROWS * 1024),
        name="feed_far",
    )(up, gain.reshape(1, D), *held, *low, *high)


def last_kernel(gf_ref, low_ref, high_ref, own_ref, gain_ref, gm_ref, out_ref):
    scaled, inverse = norm_rows(own_ref[HALF : HALF + ROWS].astype(F32))
    grad = gf_ref[...] + jnp.concatenate(
        [low_ref[...].astype(F32), high_ref[...].astype(F32)], axis=0
    )
    out_ref[...] = gm_ref[...] + norm_back(grad, scaled, inverse, gain_ref[...])


def run_last(gf, low, high, own, gain, gm):
    return pl.pallas_call(
        last_kernel,
        in_specs=[WHOLE] * 6,
        out_shape=jax.ShapeDtypeStruct((ROWS, D), F32),
        compiler_params=params(),
        cost_estimate=cost(ROWS * D * 20, 5e6),
        name="frames_grad",
    )(gf, low, high, own, gain.reshape(1, D), gm)


def edge_kernel(i_ref, frames_ref, edge_ref, sem):
    start = pl.multiple_of(jnp.where(i_ref[0] == 3, 3 * ROWS + HALF, 0), HALF)
    copy = pltpu.make_async_copy(frames_ref.at[pl.ds(start, HALF)], edge_ref, sem)
    copy.start()
    copy.wait()


def run_edge(frames, index):
    return pl.pallas_call(
        edge_kernel,
        in_specs=[
            pl.BlockSpec(memory_space=pltpu.SMEM),
            pl.BlockSpec(memory_space=pltpu.HBM),
        ],
        out_specs=WHOLE,
        out_shape=jax.ShapeDtypeStruct((HALF, D), BF),
        scratch_shapes=[pltpu.SemaphoreType.DMA],
        compiler_params=params(58),
        cost_estimate=cost(1e5, 1e6),
        name="edge",
    )(index.reshape(1), frames)


def pack_kernel(i_ref, frames_ref, up_in_ref, q_ref, k_ref, v_ref, o_ref, inner_ref, outer_ref,
                low_ref, high_ref, low_two_ref, high_two_ref, ext_ref, up_ref, sems):
    i = i_ref[0]

    def at(start, size):
        return pl.ds(pl.multiple_of(start, HALF), size)

    moves = [
        (q_ref, low_ref.at[pl.ds(0, D)]),
        (k_ref, low_ref.at[pl.ds(D, D)]),
        (v_ref, high_ref.at[pl.ds(0, D)]),
        (frames_ref.at[at(jnp.maximum(i * ROWS - HALF, 0), HALF)], ext_ref.at[pl.ds(0, HALF)]),
        (frames_ref.at[at(i * ROWS, ROWS)], ext_ref.at[pl.ds(HALF, ROWS)]),
        (
            frames_ref.at[at(jnp.minimum(i * ROWS + ROWS, 3 * ROWS + HALF), HALF)],
            ext_ref.at[pl.ds(HALF + ROWS, HALF)],
        ),
        (up_in_ref.at[at(i * ROWS, ROWS)], up_ref),
    ]
    for j in range(4):
        cols = pl.ds(j * GC, GC)
        moves.append((o_ref.at[:, cols], high_ref.at[pl.ds(D + j * GC, GC)]))
        place = pl.ds(j * D, D)
        moves.append((inner_ref.at[:, cols], low_two_ref.at[place]))
        moves.append((outer_ref.at[:, cols], high_two_ref.at[place]))
    copies = [
        pltpu.make_async_copy(source, target, sems.at[n])
        for n, (source, target) in enumerate(moves)
    ]
    for copy in copies:
        copy.start()
    for copy in copies:
        copy.wait()


def run_pack(frames, upstream, wq, wk, wv, wo, wi, wu, index):
    anywhere = pl.BlockSpec(memory_space=pltpu.HBM)
    shapes = [(2 * D, GC)] * 2 + [(4 * D, GC)] * 2 + [(EXT, D), (ROWS, D)]
    return pl.pallas_call(
        pack_kernel,
        in_specs=[pl.BlockSpec(memory_space=pltpu.SMEM)] + [anywhere] * 8,
        out_specs=[WHOLE] * 6,
        out_shape=[jax.ShapeDtypeStruct(shape, BF) for shape in shapes],
        scratch_shapes=[pltpu.SemaphoreType.DMA((19,))],
        compiler_params=params(58),
        cost_estimate=cost(1e5, 3e6),
        name="pack",
    )(index.reshape(1), frames, upstream, wq, wk, wv, wo, wi, wu)


def add(*terms):
    total = terms[0].astype(F32)
    for term in terms[1:]:
        total = total + term.astype(F32)
    return total.astype(BF)


def feed_split_kernel(near_ref, got_near_ref, far_ref, got_far_ref, out_ref, a_ref, b_ref):
    out_ref[...] = add(near_ref[...], got_near_ref[...])
    a_ref[...] = add(far_ref[:D], got_far_ref[:D])
    b_ref[...] = add(far_ref[D:], got_far_ref[D:])


def proj_split_kernel(keep_ref, got_ref, a_ref, b_ref):
    h = 2 * D
    a_ref[...] = add(keep_ref[:h], got_ref[:h])
    b_ref[...] = add(keep_ref[h:], got_ref[h:])


def join_kernel(near_ref, a_ref, b_ref, keep_ref, got_ref, pa_ref, pb_ref, out_ref):
    for n in range(16):
        feed, proj = (a_ref, pa_ref) if n < 8 else (b_ref, pb_ref)
        rows, part = slice(n * 64, (n + 1) * 64), slice(n % 8 * 64, (n % 8 + 1) * 64)
        out_ref[n, :64] = add(near_ref[rows], feed[part])
        for j in range(4):
            rows = slice(n * GC + j * 32, n * GC + (j + 1) * 32)
            part = slice(n % 8 * GC + j * 32, n % 8 * GC + (j + 1) * 32)
            out_ref[n, 64:, j * GC : (j + 1) * GC] = add(keep_ref[rows], got_ref[rows], proj[part])


def sum_kernel(parts_ref, out_ref):
    out_ref[...] = add(*[parts_ref[n] for n in range(16)])


def spread_kernel(mine_ref, got_ref, out_ref):
    total = add(mine_ref[...], got_ref[...])
    for n in range(16):
        out_ref[n] = total


def end_kernel(scale, total_ref, *refs):
    outs, helds, sems = refs[:6], refs[6:12], refs[12]
    copies = [
        pltpu.make_async_copy(held, out, sems.at[n])
        for n, (held, out) in enumerate(zip(helds, outs))
    ]
    q_ref, k_ref, v_ref, o_ref, inner_ref, outer_ref = helds
    outer = jnp.concatenate([total_ref[8 + n, :64] for n in range(8)], axis=0)
    outer_ref[...] = outer.astype(F32).T * scale
    copies[5].start()
    for n in range(8):
        inner_ref[n * 64 : (n + 1) * 64] = total_ref[n, :64].astype(F32) * scale
    copies[4].start()
    for n in range(16):
        for j in range(4):
            block = total_ref[n, 64:, j * GC : (j + 1) * GC].astype(F32) * scale
            if n < 12:
                start = n % 4 * GC + j * 32
                (q_ref, k_ref, v_ref)[n // 4][start : start + 32] = block
            else:
                o_ref[j * 32 : (j + 1) * 32, (n - 12) * GC : (n - 11) * GC] = block
        if n % 4 == 3:
            copies[n // 4].start()
    for copy in copies:
        copy.wait()


def run_end(scale, total):
    shapes = [(D, GC)] * 3 + [(GC, D), (D, D), (D, D)]
    return pl.pallas_call(
        functools.partial(end_kernel, scale),
        in_specs=[WHOLE],
        out_specs=[pl.BlockSpec(memory_space=pltpu.HBM)] * 6,
        out_shape=[jax.ShapeDtypeStruct(shape, F32) for shape in shapes],
        scratch_shapes=[VMEM(shape, F32) for shape in shapes]
        + [pltpu.SemaphoreType.DMA((6,))],
        compiler_params=params(),
        cost_estimate=cost(1e6, 5e6),
        name="end",
    )(total)


def small(kernel, name, shapes, *arrays, final=False, loose=False):
    outs = [jax.ShapeDtypeStruct(shape, F32 if final else BF) for shape in shapes]
    extra = {} if final or loose else {"out_specs": [WHOLE] * len(outs)}
    return pl.pallas_call(
        kernel,
        in_specs=[WHOLE] * len(arrays),
        out_shape=outs,
        compiler_params=params(),
        cost_estimate=cost(1e6, 2e6),
        name=name,
        **extra,
    )(*arrays)


def swap(array, bits):
    return lax.ppermute(array, AXES, [(n, n ^ bits) for n in range(128)])


def after(first, *later):
    return lax.optimization_barrier((first,) + later)[0]


PEERS = [[2 * n + half for n in range(16)] for half in range(2)]


def exchange(parts):
    return lax.all_to_all(parts, "tm", 0, 0, axis_index_groups=PEERS, tiled=True)


def local(
    frames,
    upstream,
    recording,
    first_gain,
    query_weight,
    key_weight,
    value_weight,
    out_weight,
    second_gain,
    inner_weight,
    outer_weight,
):
    t = lax.axis_index("tm")
    i = lax.axis_index("ffn")
    slab = frames.shape[0]
    devices = lax.axis_size("tm") * 4
    scale = 1.0 / math.sqrt(recording.shape[0])

    record_pad = jnp.pad(recording, (HALF, HALF), constant_values=-1)
    rec_ext = lax.dynamic_slice_in_dim(record_pad, t * slab + i * ROWS, EXT)
    rec_col = rec_ext.reshape(EXT, 1)
    rec_row = rec_ext[HALF : HALF + ROWS].reshape(BLOCKS, 1, QB)
    rec_col, rec_row, index = lax.optimization_barrier((rec_col, rec_row, i))
    edge = run_edge(frames, index)
    low_own, high_own, low_own2, high_own2, ext, up = run_pack(
        frames, upstream, query_weight, key_weight, value_weight, out_weight,
        inner_weight, outer_weight, after(index, edge),
    )
    pairs = [(4 * n + 3, 4 * n + 4) for n in range(31)] + [(4 * n + 4, 4 * n + 3) for n in range(31)]
    halo = lax.ppermute(edge, AXES, pairs)
    low_far, high_far = swap(after(low_own, halo), 2), swap(after(high_own, halo), 6)
    low_near, high_near = swap(low_own, 1), swap(high_own, 1)

    normed, normed_t, bias = run_norm(ext, halo, first_gain, rec_col, rec_row, i)
    qs, ks, vs, ctx, lse = [], [], [], [], []

    def forward(qk, vo):
        q, key, v, c, s = run_context(normed, qk, vo, bias)
        qs.append(q)
        ks.append(key)
        vs.append(v)
        ctx.append(c)
        lse.append(s)

    forward(low_own, high_own)
    low_far2, high_far2 = swap(after(low_own2, ctx[0]), 2), swap(after(high_own2, ctx[0]), 6)
    forward(low_near, high_near)
    low_far, high_far = after(low_far, *ctx), after(high_far, *ctx)
    low = [low_own, low_near, low_far, swap(low_far, 1)]
    high = [high_own, high_near, high_far, swap(high_far, 1)]
    forward(low[2], high[2])
    forward(low[3], high[3])

    low_near2, high_near2 = swap(after(low_own2, ctx[0]), 1), swap(after(high_own2, ctx[0]), 1)
    give1, keep0, *held = run_feed_near(
        ext, up, second_gain, ctx, high, [high_own2, high_near2], [low_own2, low_near2]
    )
    got_near = swap(give1, 1)
    low_far2, high_far2 = after(low_far2, give1), after(high_far2, give1)
    grad_middle, gml, give3, keep2 = run_feed_far(
        up, second_gain, held, [low_far2, swap(low_far2, 1)], [high_far2, swap(high_far2, 1)],
    )
    got_far = swap(give3, 1)
    near, far_a, far_b = small(
        feed_split_kernel, "feed_split", [(2 * D, D), (D, D), (D, D)],
        keep0, got_near, keep2, got_far,
    )

    dw = [None] * 4

    def back(place, gf, k, grads):
        dw[k], *rest = run_attention_back(
            place, gf, grads, low[k], high[k], ctx[k], qs[k], ks[k], vs[k], lse[k], bias, normed_t
        )
        return rest

    (gf,) = back(0, None, 3, gml)
    got3 = swap(dw[3], 1)
    (gf,) = back(1, gf, 2, after(gml, near, gf))
    proj_a, proj_b = small(proj_split_kernel, "proj_split", [(2 * D, GC)] * 2, dw[2], got3)
    proj_got_a, proj_got_b = swap(proj_a, 2), swap(proj_b, 6)
    (gf,) = back(1, gf, 1, after(gml, proj_a))
    got1 = swap(dw[1], 1)
    feed_got_a, feed_got_b = swap(far_a, 2), swap(far_b, 6)
    gf, before, behind = back(2, gf, 0, after(gml, feed_got_a, feed_got_b))
    from_low = lax.ppermute(behind, AXES, [(n, n + 1) for n in range(devices - 1)])
    from_high = lax.ppermute(before, AXES, [(n + 1, n) for n in range(devices - 1)])

    (parts,) = small(
        join_kernel, "join", [(16, 96, D)],
        near, feed_got_a, feed_got_b, dw[0], got1, proj_got_a, proj_got_b, loose=True,
    )
    got = exchange(parts)
    grad_frames = run_last(gf, from_low, from_high, ext, first_gain, grad_middle)
    (summed,) = small(sum_kernel, "sum", [(96, D)], got)
    other = swap(summed, 4)
    (spread,) = small(
        spread_kernel, "spread", [(16, 96, D)], after(summed, from_low, from_high), other,
        loose=True,
    )
    total = exchange(spread)
    grads = run_end(scale, after(total, grad_frames))
    return (grad_frames, *grads)


def solution(mesh):
    in_specs = (
        P("tm", None),
        P("tm", None),
        P(),
        P(),
        P(None, "ffn"),
        P(None, "ffn"),
        P(None, "ffn"),
        P("ffn", None),
        P(),
        P(None, "ffn"),
        P("ffn", None),
    )
    out_specs = (
        P(("tm", "ffn"), None),
        P(None, "ffn"),
        P(None, "ffn"),
        P(None, "ffn"),
        P("ffn", None),
        P(None, "ffn"),
        P("ffn", None),
    )
    return jax.shard_map(local, mesh=mesh, in_specs=in_specs, out_specs=out_specs, check_vma=False)
```

```python
import functools
import math

import jax
import jax.numpy as jnp
from jax import lax
from jax.experimental import pallas as pl
from jax.experimental.pallas import tpu as pltpu
from jax.sharding import PartitionSpec as P

HEAD_DIM = 64
HALF = 256
ROWS = 512
EXT = ROWS + 2 * HALF
QB = 128
WIN = QB + 2 * HALF
BLOCKS = ROWS // QB
GC = 128
CHUNKS = ((0, 640),)
D = 512
epsilon = 1e-05
masked_score = -1e30
BF = jnp.bfloat16
F32 = jnp.float32
AXES = ("tm", "ffn")
VMEM = pltpu.VMEM
WHOLE = pl.BlockSpec(memory_space=pltpu.VMEM)


def dot(a, b):
    return jnp.dot(a, b, preferred_element_type=F32)


def dot_nt(a, b):
    return lax.dot_general(a, b, (((1,), (1,)), ((), ())), preferred_element_type=F32)


def params(mib=16):
    return pltpu.CompilerParams(vmem_limit_bytes=mib * 1024 * 1024)


def cost(flops, nbytes, trans=0):
    return pl.CostEstimate(
        flops=int(flops / 8), bytes_accessed=int(nbytes / 8), transcendentals=int(trans / 8)
    )


def norm_rows(x):
    center = jnp.mean(x, axis=-1, keepdims=True)
    shifted = x - center
    inverse = lax.rsqrt(jnp.mean(shifted * shifted, axis=-1, keepdims=True) + epsilon)
    return shifted * inverse, inverse


def norm_back(grad_normed, scaled, inverse, gain):
    weighted = grad_normed * gain
    first = jnp.mean(weighted, axis=-1, keepdims=True)
    second = jnp.mean(weighted * scaled, axis=-1, keepdims=True)
    return inverse * (weighted - first - scaled * second)


def norm_kernel(i_ref, ext_ref, halo_ref, gain_ref, col_ref, row_ref, n_ref, nt_ref, bias_ref):
    step = pl.program_id(0)
    outside = ((i_ref[0] == 0) & (step == 0)) | ((i_ref[0] == 3) & (step == 3))
    x = jnp.where(outside, halo_ref[...].astype(F32), ext_ref[...].astype(F32))
    scaled, _ = norm_rows(x)
    normed = scaled * gain_ref[...]
    n_ref[...] = normed.astype(BF)
    nt_ref[...] = normed.T.astype(BF)
    keys = col_ref[pl.ds(pl.multiple_of(step * QB, QB), WIN), :]
    offset = lax.broadcasted_iota(jnp.int32, (WIN, QB), 0) - lax.broadcasted_iota(
        jnp.int32, (WIN, QB), 1
    )
    band = (offset >= 0) & (offset < 2 * HALF)
    bias_ref[0] = jnp.where(band & (keys == row_ref[0]), 0.0, masked_score)


def run_norm(ext, halo, gain, rec_col, rec_row, index):
    spec = pltpu.PrefetchScalarGridSpec(
        num_scalar_prefetch=1,
        grid=(4,),
        in_specs=[
            pl.BlockSpec((HALF, D), lambda j, i: (j, 0)),
            pl.BlockSpec((HALF, D), lambda j, i: (0, 0)),
            pl.BlockSpec((1, D), lambda j, i: (0, 0)),
            pl.BlockSpec((EXT, 1), lambda j, i: (0, 0)),
            pl.BlockSpec((1, 1, QB), lambda j, i: (j, 0, 0)),
        ],
        out_specs=[
            pl.BlockSpec((HALF, D), lambda j, i: (j, 0)),
            pl.BlockSpec((D, HALF), lambda j, i: (0, j)),
            pl.BlockSpec((1, WIN, QB), lambda j, i: (j, 0, 0)),
        ],
    )
    return pl.pallas_call(
        norm_kernel,
        grid_spec=spec,
        out_shape=[
            jax.ShapeDtypeStruct((EXT, D), BF),
            jax.ShapeDtypeStruct((D, EXT), BF),
            jax.ShapeDtypeStruct((BLOCKS, WIN, QB), F32),
        ],
        compiler_params=params(),
        cost_estimate=cost(EXT * D * 12, 5e6),
        name="norm_first",
    )(index.reshape(1), ext, halo, gain.reshape(1, D), rec_col, rec_row)


def wide(vo_ref):
    return jnp.concatenate([vo_ref[D + j * GC : D + (j + 1) * GC] for j in range(4)], axis=1)


def square(packed_ref):
    return jnp.concatenate([packed_ref[j * D : (j + 1) * D] for j in range(4)], axis=1)


def stack_heads(block):
    lane = lax.broadcasted_iota(jnp.int32, block.shape, 1)
    zero = jnp.zeros_like(block)
    low = jnp.where(lane < HEAD_DIM, block, zero)
    high = jnp.where(lane < HEAD_DIM, zero, block)
    return jnp.concatenate([low, high], axis=0)


def pick_heads(both):
    return jnp.concatenate([both[:HEAD_DIM, :QB], both[HEAD_DIM:, QB:]], axis=0).T


def context_kernel(n_ref, qk_ref, vo_ref, bias_ref, q_ref, k_ref, v_ref, ctx_ref, lse_ref, vt_ref):
    n = n_ref[...]
    q_ref[...] = dot(n_ref[HALF : HALF + ROWS], qk_ref[:D]).astype(BF) * 0.125
    k_ref[...] = dot(n, qk_ref[D : 2 * D]).astype(BF)
    v = dot(n, vo_ref[:D])
    v_ref[...] = v.astype(BF)
    vt_ref[...] = v.T.astype(BF)
    for b in range(BLOCKS):
        win = slice(b * QB, b * QB + WIN)
        rows = slice(b * QB, b * QB + QB)
        queries = stack_heads(q_ref[rows])
        bias = bias_ref[b]
        scores = dot_nt(k_ref[win], queries) + jnp.concatenate([bias, bias], axis=1)
        peak = jnp.max(scores, axis=0, keepdims=True)
        weights = jnp.exp(scores - peak)
        total = jnp.sum(weights, axis=0, keepdims=True)
        both = dot(vt_ref[:, win], weights.astype(BF)) / total
        ctx_ref[rows] = pick_heads(both).astype(BF)
        lse_ref[b] = peak + jnp.log(total)


def run_context(normed, qk, vo, bias):
    return pl.pallas_call(
        context_kernel,
        in_specs=[WHOLE] * 4,
        out_specs=[WHOLE] * 5,
        out_shape=[
            jax.ShapeDtypeStruct((ROWS, GC), BF),
            jax.ShapeDtypeStruct((EXT, GC), BF),
            jax.ShapeDtypeStruct((EXT, GC), BF),
            jax.ShapeDtypeStruct((ROWS, GC), BF),
            jax.ShapeDtypeStruct((BLOCKS, 1, 2 * QB), F32),
        ],
        scratch_shapes=[VMEM((GC, EXT), BF)],
        compiler_params=params(),
        cost_estimate=cost(2e9, 4e6, BLOCKS * WIN * 2 * QB),
        name="context",
    )(normed, qk, vo, bias)


def attention_back_kernel(place, *refs):
    gml_ref, qk_ref, vo_ref, ctx_ref, q_ref, k_ref, v_ref, lse_ref, bias_ref, nt_ref = refs[:10]
    refs = refs[10:]
    if place > 0:
        gf_in_ref, refs = refs[0], refs[1:]
    dw_ref, gf_ref, refs = refs[0], refs[1], refs[2:]
    if place == 2:
        before_ref, behind_ref, refs = refs[0], refs[1], refs[2:]
    g_ref, kt_ref, dq_ref, dka_ref, dva_ref, dk_ref, dv_ref = refs
    g_ref[...] = dot_nt(gml_ref[...], wide(vo_ref)).astype(BF)
    grad_out = dot(ctx_ref[...].T, gml_ref[...]).astype(BF)
    for j in range(4):
        dw_ref[3 * D + j * GC : 3 * D + (j + 1) * GC] = grad_out[:, j * GC : (j + 1) * GC]
    kt_ref[...] = k_ref[...].T
    dka_ref[...] = jnp.zeros_like(dka_ref)
    dva_ref[...] = jnp.zeros_like(dva_ref)
    for b in range(BLOCKS):
        rows = slice(b * QB, b * QB + QB)
        queries = stack_heads(q_ref[rows])
        grads = stack_heads(g_ref[rows])
        product = (g_ref[rows].astype(F32) * ctx_ref[rows].astype(F32)).T
        inner = jnp.concatenate(
            [
                jnp.sum(product[:HEAD_DIM], axis=0, keepdims=True),
                jnp.sum(product[HEAD_DIM:], axis=0, keepdims=True),
            ],
            axis=1,
        )
        lse = lse_ref[b]
        both = None
        for start, stop in CHUNKS:
            part = slice(b * QB + start, b * QB + stop)
            bias = bias_ref[b, start:stop]
            scores = dot_nt(k_ref[part], queries) + jnp.concatenate([bias, bias], axis=1)
            prob = jnp.exp(scores - lse)
            grad_scores = (prob * (dot_nt(v_ref[part], grads) - inner)).astype(BF)
            dva_ref[part] += dot(prob.astype(BF), grads)
            dka_ref[part] += dot(grad_scores, queries)
            term = dot(kt_ref[:, part], grad_scores)
            both = term if both is None else both + term
        dq_ref[rows] = (pick_heads(both) * 0.125).astype(BF)
    dk_ref[...] = dka_ref[...].astype(BF)
    dv_ref[...] = dva_ref[...].astype(BF)
    dw_ref[:D] = dot(nt_ref[:, HALF : HALF + ROWS], dq_ref[...]).astype(BF)
    dw_ref[D : 2 * D] = dot(nt_ref[...], dk_ref[...]).astype(BF)
    dw_ref[2 * D : 3 * D] = dot(nt_ref[...], dv_ref[...]).astype(BF)
    for part in range(4):
        rows = slice(part * HALF, (part + 1) * HALF)
        term = dot_nt(dk_ref[rows], qk_ref[D : 2 * D]) + dot_nt(dv_ref[rows], vo_ref[:D])
        if part in (1, 2):
            own = slice((part - 1) * HALF, part * HALF)
            term = term + dot_nt(dq_ref[own], qk_ref[:D])
        if place > 0:
            term = term + gf_in_ref[rows]
        if place < 2:
            gf_ref[rows] = term
        elif part == 0:
            before_ref[...] = term.astype(BF)
        elif part == 3:
            behind_ref[...] = term.astype(BF)
        else:
            gf_ref[own] = term


def run_attention_back(place, gf, *arrays):
    gf_shape = jax.ShapeDtypeStruct((ROWS if place == 2 else EXT, D), F32)
    edges = [jax.ShapeDtypeStruct((HALF, D), BF)] * 2 if place == 2 else []
    if place > 0:
        arrays = arrays + (gf,)
    return pl.pallas_call(
        functools.partial(attention_back_kernel, place),
        in_specs=[WHOLE] * len(arrays),
        out_specs=[WHOLE] * (2 + len(edges)),
        out_shape=[jax.ShapeDtypeStruct((4 * D, GC), BF), gf_shape] + edges,
        scratch_shapes=[
            VMEM((ROWS, GC), BF),
            VMEM((GC, EXT), BF),
            VMEM((ROWS, GC), BF),
            VMEM((EXT, GC), F32),
            VMEM((EXT, GC), F32),
            VMEM((EXT, GC), BF),
            VMEM((EXT, GC), BF),
        ],
        compiler_params=params(),
        cost_estimate=cost(4e9, 6e6, BLOCKS * WIN * 2 * QB),
        name="attention_back",
    )(*arrays)


def feed_group(n2_ref, n2t_ref, up_ref, upt_ref, low, high, to_ref):
    inner = square(low)
    pre = dot(n2_ref[...], inner)
    grad_act = dot_nt(up_ref[...], square(high)) * 0.5
    gate = jax.nn.sigmoid(pre)
    act = (pre * gate).astype(BF)
    grad_inner = (grad_act * gate * (1.0 + pre * (1.0 - gate))).astype(BF)
    to_ref[:D] = dot(n2t_ref[...], grad_inner).astype(BF)
    to_ref[D:] = (dot(upt_ref[...], act) * 0.5).astype(BF)
    return dot_nt(grad_inner, inner)


def feed_near_kernel(*refs):
    ext_ref, up_ref, gain_ref = refs[:3]
    ctx, vo, high, low = refs[3:7], refs[7:11], refs[11:13], refs[13:15]
    give_ref, keep_ref, sc_ref, inv_ref, n2_ref, n2t_ref, upt_ref, gs_ref = refs[15:]
    middle = ext_ref[HALF : HALF + ROWS].astype(F32)
    for k in range(4):
        middle = middle + dot(ctx[k][...], wide(vo[k]))
    scaled, inverse = norm_rows(middle)
    sc_ref[...] = scaled
    inv_ref[...] = inverse
    normed = scaled * gain_ref[...]
    n2_ref[...] = normed.astype(BF)
    n2t_ref[...] = normed.T.astype(BF)
    upt_ref[...] = up_ref[...].T
    shared = (n2_ref, n2t_ref, up_ref, upt_ref)
    gs_ref[...] = feed_group(*shared, low[1], high[1], give_ref)
    gs_ref[...] += feed_group(*shared, low[0], high[0], keep_ref)


def run_feed_near(ext, up, gain, ctx, vo, high, low):
    return pl.pallas_call(
        feed_near_kernel,
        in_specs=[WHOLE] * 15,
        out_specs=[WHOLE] * 8,
        out_shape=[
            jax.ShapeDtypeStruct((2 * D, D), BF),
            jax.ShapeDtypeStruct((2 * D, D), BF),
            jax.ShapeDtypeStruct((ROWS, D), F32),
            jax.ShapeDtypeStruct((ROWS, 1), F32),
            jax.ShapeDtypeStruct((ROWS, D), BF),
            jax.ShapeDtypeStruct((D, ROWS), BF),
            jax.ShapeDtypeStruct((D, ROWS), BF),
            jax.ShapeDtypeStruct((ROWS, D), F32),
        ],
        compiler_params=params(),
        cost_estimate=cost(4e9, 14e6, ROWS * 1024),
        name="feed_near",
    )(ext, up, gain.reshape(1, D), *ctx, *vo, *high, *low)


def feed_far_kernel(*refs):
    up_ref, gain_ref, sc_ref, inv_ref, n2_ref, n2t_ref, upt_ref, gs_in_ref = refs[:8]
    low, high = refs[8:10], refs[10:12]
    gm_ref, gml_ref, give_ref, keep_ref, gs_ref = refs[12:]
    shared = (n2_ref, n2t_ref, up_ref, upt_ref)
    gs_ref[...] = gs_in_ref[...] + feed_group(*shared, low[1], high[1], give_ref)
    gs_ref[...] += feed_group(*shared, low[0], high[0], keep_ref)
    grad_middle = up_ref[...].astype(F32) + norm_back(
        gs_ref[...], sc_ref[...], inv_ref[...], gain_ref[...]
    )
    gm_ref[...] = grad_middle
    gml_ref[...] = grad_middle.astype(BF)


def run_feed_far(up, gain, held, low, high):
    return pl.pallas_call(
        feed_far_kernel,
        in_specs=[WHOLE] * 12,
        out_specs=[WHOLE] * 4,
        out_shape=[
            jax.ShapeDtypeStruct((ROWS, D), F32),
            jax.ShapeDtypeStruct((ROWS, D), BF),
            jax.ShapeDtypeStruct((2 * D, D), BF),
            jax.ShapeDtypeStruct((2 * D, D), BF),
        ],
        scratch_shapes=[VMEM((ROWS, D), F32)],
        compiler_params=params(),
        cost_estimate=cost(4e9, 14e6, ROWS * 1024),
        name="feed_far",
    )(up, gain.reshape(1, D), *held, *low, *high)


def last_kernel(gf_ref, low_ref, high_ref, own_ref, gain_ref, gm_ref, out_ref):
    scaled, inverse = norm_rows(own_ref[HALF : HALF + ROWS].astype(F32))
    grad = gf_ref[...] + jnp.concatenate(
        [low_ref[...].astype(F32), high_ref[...].astype(F32)], axis=0
    )
    out_ref[...] = gm_ref[...] + norm_back(grad, scaled, inverse, gain_ref[...])


def run_last(gf, low, high, own, gain, gm):
    return pl.pallas_call(
        last_kernel,
        in_specs=[WHOLE] * 6,
        out_shape=jax.ShapeDtypeStruct((ROWS, D), F32),
        compiler_params=params(),
        cost_estimate=cost(ROWS * D * 20, 5e6),
        name="frames_grad",
    )(gf, low, high, own, gain.reshape(1, D), gm)


def edge_kernel(i_ref, frames_ref, edge_ref, sem):
    start = pl.multiple_of(jnp.where(i_ref[0] == 3, 3 * ROWS + HALF, 0), HALF)
    copy = pltpu.make_async_copy(frames_ref.at[pl.ds(start, HALF)], edge_ref, sem)
    copy.start()
    copy.wait()


def run_edge(frames, index):
    return pl.pallas_call(
        edge_kernel,
        in_specs=[
            pl.BlockSpec(memory_space=pltpu.SMEM),
            pl.BlockSpec(memory_space=pltpu.HBM),
        ],
        out_specs=WHOLE,
        out_shape=jax.ShapeDtypeStruct((HALF, D), BF),
        scratch_shapes=[pltpu.SemaphoreType.DMA],
        compiler_params=params(58),
        cost_estimate=cost(1e5, 1e6),
        name="edge",
    )(index.reshape(1), frames)


def pack_kernel(i_ref, frames_ref, up_in_ref, q_ref, k_ref, v_ref, o_ref, inner_ref, outer_ref,
                low_ref, high_ref, low_two_ref, high_two_ref, ext_ref, up_ref, sems):
    i = i_ref[0]

    def at(start, size):
        return pl.ds(pl.multiple_of(start, HALF), size)

    moves = [
        (q_ref, low_ref.at[pl.ds(0, D)]),
        (k_ref, low_ref.at[pl.ds(D, D)]),
        (v_ref, high_ref.at[pl.ds(0, D)]),
        (frames_ref.at[at(jnp.maximum(i * ROWS - HALF, 0), HALF)], ext_ref.at[pl.ds(0, HALF)]),
        (frames_ref.at[at(i * ROWS, ROWS)], ext_ref.at[pl.ds(HALF, ROWS)]),
        (
            frames_ref.at[at(jnp.minimum(i * ROWS + ROWS, 3 * ROWS + HALF), HALF)],
            ext_ref.at[pl.ds(HALF + ROWS, HALF)],
        ),
        (up_in_ref.at[at(i * ROWS, ROWS)], up_ref),
    ]
    for j in range(4):
        cols = pl.ds(j * GC, GC)
        moves.append((o_ref.at[:, cols], high_ref.at[pl.ds(D + j * GC, GC)]))
        place = pl.ds(j * D, D)
        moves.append((inner_ref.at[:, cols], low_two_ref.at[place]))
        moves.append((outer_ref.at[:, cols], high_two_ref.at[place]))
    copies = [
        pltpu.make_async_copy(source, target, sems.at[n])
        for n, (source, target) in enumerate(moves)
    ]
    for copy in copies:
        copy.start()
    for copy in copies:
        copy.wait()


def run_pack(frames, upstream, wq, wk, wv, wo, wi, wu, index):
    anywhere = pl.BlockSpec(memory_space=pltpu.HBM)
    shapes = [(2 * D, GC)] * 2 + [(4 * D, GC)] * 2 + [(EXT, D), (ROWS, D)]
    return pl.pallas_call(
        pack_kernel,
        in_specs=[pl.BlockSpec(memory_space=pltpu.SMEM)] + [anywhere] * 8,
        out_specs=[WHOLE] * 6,
        out_shape=[jax.ShapeDtypeStruct(shape, BF) for shape in shapes],
        scratch_shapes=[pltpu.SemaphoreType.DMA((19,))],
        compiler_params=params(58),
        cost_estimate=cost(1e5, 3e6),
        name="pack",
    )(index.reshape(1), frames, upstream, wq, wk, wv, wo, wi, wu)


def add(*terms):
    total = terms[0].astype(F32)
    for term in terms[1:]:
        total = total + term.astype(F32)
    return total.astype(BF)


def feed_split_kernel(near_ref, got_near_ref, far_ref, got_far_ref, out_ref, a_ref, b_ref):
    out_ref[...] = add(near_ref[...], got_near_ref[...])
    a_ref[...] = add(far_ref[:D], got_far_ref[:D])
    b_ref[...] = add(far_ref[D:], got_far_ref[D:])


def proj_split_kernel(keep_ref, got_ref, a_ref, b_ref):
    h = 2 * D
    a_ref[...] = add(keep_ref[:h], got_ref[:h])
    b_ref[...] = add(keep_ref[h:], got_ref[h:])


def join_kernel(near_ref, a_ref, b_ref, keep_ref, got_ref, pa_ref, pb_ref, out_ref):
    for n in range(16):
        feed, proj = (a_ref, pa_ref) if n < 8 else (b_ref, pb_ref)
        rows, part = slice(n * 64, (n + 1) * 64), slice(n % 8 * 64, (n % 8 + 1) * 64)
        out_ref[n, :64] = add(near_ref[rows], feed[part])
        for j in range(4):
            rows = slice(n * GC + j * 32, n * GC + (j + 1) * 32)
            part = slice(n % 8 * GC + j * 32, n % 8 * GC + (j + 1) * 32)
            out_ref[n, 64:, j * GC : (j + 1) * GC] = add(keep_ref[rows], got_ref[rows], proj[part])


def sum_kernel(parts_ref, out_ref):
    out_ref[...] = add(*[parts_ref[n] for n in range(16)])


def spread_kernel(mine_ref, got_ref, out_ref):
    total = add(mine_ref[...], got_ref[...])
    for n in range(16):
        out_ref[n] = total


def end_kernel(scale, total_ref, q_ref, k_ref, v_ref, o_ref, inner_ref, outer_ref):
    for n in range(8):
        inner_ref[n * 64 : (n + 1) * 64] = total_ref[n, :64].astype(F32) * scale
    outer = jnp.concatenate([total_ref[8 + n, :64] for n in range(8)], axis=0)
    outer_ref[...] = outer.astype(F32).T * scale
    for n in range(16):
        for j in range(4):
            block = total_ref[n, 64:, j * GC : (j + 1) * GC].astype(F32) * scale
            if n < 12:
                start = n % 4 * GC + j * 32
                (q_ref, k_ref, v_ref)[n // 4][start : start + 32] = block
            else:
                o_ref[j * 32 : (j + 1) * 32, (n - 12) * GC : (n - 11) * GC] = block


def small(kernel, name, shapes, *arrays, final=False, loose=False):
    outs = [jax.ShapeDtypeStruct(shape, F32 if final else BF) for shape in shapes]
    extra = {} if final or loose else {"out_specs": [WHOLE] * len(outs)}
    return pl.pallas_call(
        kernel,
        in_specs=[WHOLE] * len(arrays),
        out_shape=outs,
        compiler_params=params(),
        cost_estimate=cost(1e6, 2e6),
        name=name,
        **extra,
    )(*arrays)


def swap(array, bits):
    return lax.ppermute(array, AXES, [(n, n ^ bits) for n in range(128)])


def after(first, *later):
    return lax.optimization_barrier((first,) + later)[0]


PEERS = [[2 * n + half for n in range(16)] for half in range(2)]


def exchange(parts):
    return lax.all_to_all(parts, "tm", 0, 0, axis_index_groups=PEERS, tiled=True)


def local(
    frames,
    upstream,
    recording,
    first_gain,
    query_weight,
    key_weight,
    value_weight,
    out_weight,
    second_gain,
    inner_weight,
    outer_weight,
):
    t = lax.axis_index("tm")
    i = lax.axis_index("ffn")
    slab = frames.shape[0]
    devices = lax.axis_size("tm") * 4
    scale = 1.0 / math.sqrt(recording.shape[0])

    record_pad = jnp.pad(recording, (HALF, HALF), constant_values=-1)
    rec_ext = lax.dynamic_slice_in_dim(record_pad, t * slab + i * ROWS, EXT)
    rec_col = rec_ext.reshape(EXT, 1)
    rec_row = rec_ext[HALF : HALF + ROWS].reshape(BLOCKS, 1, QB)
    rec_col, rec_row, index = lax.optimization_barrier((rec_col, rec_row, i))
    edge = run_edge(frames, index)
    low_own, high_own, low_own2, high_own2, ext, up = run_pack(
        frames, upstream, query_weight, key_weight, value_weight, out_weight,
        inner_weight, outer_weight, after(index, edge),
    )
    pairs = [(4 * n + 3, 4 * n + 4) for n in range(31)] + [(4 * n + 4, 4 * n + 3) for n in range(31)]
    halo = lax.ppermute(edge, AXES, pairs)
    low_far, high_far = swap(after(low_own, halo), 2), swap(after(high_own, halo), 6)
    low_near, high_near = swap(low_own, 1), swap(high_own, 1)

    normed, normed_t, bias = run_norm(ext, halo, first_gain, rec_col, rec_row, i)
    qs, ks, vs, ctx, lse = [], [], [], [], []

    def forward(qk, vo):
        q, key, v, c, s = run_context(normed, qk, vo, bias)
        qs.append(q)
        ks.append(key)
        vs.append(v)
        ctx.append(c)
        lse.append(s)

    forward(low_own, high_own)
    low_far2, high_far2 = swap(after(low_own2, ctx[0]), 2), swap(after(high_own2, ctx[0]), 6)
    forward(low_near, high_near)
    low_far, high_far = after(low_far, *ctx), after(high_far, *ctx)
    low = [low_own, low_near, low_far, swap(low_far, 1)]
    high = [high_own, high_near, high_far, swap(high_far, 1)]
    forward(low[2], high[2])
    forward(low[3], high[3])

    low_near2, high_near2 = swap(after(low_own2, ctx[0]), 1), swap(after(high_own2, ctx[0]), 1)
    give1, keep0, *held = run_feed_near(
        ext, up, second_gain, ctx, high, [high_own2, high_near2], [low_own2, low_near2]
    )
    got_near = swap(give1, 1)
    low_far2, high_far2 = after(low_far2, give1), after(high_far2, give1)
    grad_middle, gml, give3, keep2 = run_feed_far(
        up, second_gain, held, [low_far2, swap(low_far2, 1)], [high_far2, swap(high_far2, 1)],
    )
    got_far = swap(give3, 1)
    near, far_a, far_b = small(
        feed_split_kernel, "feed_split", [(2 * D, D), (D, D), (D, D)],
        keep0, got_near, keep2, got_far,
    )

    dw = [None] * 4

    def back(place, gf, k, grads):
        dw[k], *rest = run_attention_back(
            place, gf, grads, low[k], high[k], ctx[k], qs[k], ks[k], vs[k], lse[k], bias, normed_t
        )
        return rest

    (gf,) = back(0, None, 3, gml)
    got3 = swap(dw[3], 1)
    (gf,) = back(1, gf, 2, after(gml, near, gf))
    proj_a, proj_b = small(proj_split_kernel, "proj_split", [(2 * D, GC)] * 2, dw[2], got3)
    proj_got_a, proj_got_b = swap(proj_a, 2), swap(proj_b, 6)
    (gf,) = back(1, gf, 1, after(gml, proj_a))
    got1 = swap(dw[1], 1)
    feed_got_a, feed_got_b = swap(far_a, 2), swap(far_b, 6)
    gf, before, behind = back(2, gf, 0, after(gml, feed_got_a, feed_got_b))
    from_low = lax.ppermute(behind, AXES, [(n, n + 1) for n in range(devices - 1)])
    from_high = lax.ppermute(before, AXES, [(n + 1, n) for n in range(devices - 1)])

    (parts,) = small(
        join_kernel, "join", [(16, 96, D)],
        near, feed_got_a, feed_got_b, dw[0], got1, proj_got_a, proj_got_b, loose=True,
    )
    got = exchange(parts)
    grad_frames = run_last(gf, from_low, from_high, ext, first_gain, grad_middle)
    (summed,) = small(sum_kernel, "sum", [(96, D)], got)
    other = swap(summed, 4)
    (spread,) = small(
        spread_kernel, "spread", [(16, 96, D)], after(summed, from_low, from_high), other,
        loose=True,
    )
    total = exchange(spread)
    grads = small(
        functools.partial(end_kernel, scale), "end", [(D, GC)] * 3 + [(GC, D), (D, D), (D, D)],
        after(total, grad_frames), final=True,
    )
    return (grad_frames, *grads)


def solution(mesh):
    in_specs = (
        P("tm", None),
        P("tm", None),
        P(),
        P(),
        P(None, "ffn"),
        P(None, "ffn"),
        P(None, "ffn"),
        P("ffn", None),
        P(),
        P(None, "ffn"),
        P("ffn", None),
    )
    out_specs = (
        P(("tm", "ffn"), None),
        P(None, "ffn"),
        P(None, "ffn"),
        P(None, "ffn"),
        P("ffn", None),
        P(None, "ffn"),
        P("ffn", None),
    )
    return jax.shard_map(local, mesh=mesh, in_specs=in_specs, out_specs=out_specs, check_vma=False)
```
